256 devices in a mesh: seq: 32 (over x, z), exp: 8 (over y, core).
Axes of the slice: x: 4, y: 4, z: 8, core: 2. Of those that a mesh axis runs over, the one named last changes fastest.
Arguments:
- residual: bfloat16 [8, 8192, 2048], P('exp', 'seq'), may hold values from -36 to 36
- kept_index: int32 [8, 2048], P('exp', 'seq'), may hold values from 0 to 255, as said below
- kept_count: int32 [8, 32], P('exp', 'seq'), may hold values from 16 to 64, as said below
- projected: bfloat16 [8, 2048, 6144], P('exp', 'seq'), may hold values from -6 to 6
- expert_ids: int32 [8, 2048, 6], P('exp', 'seq'), may hold values from 0 to 63, as said below
- gate_values: float32 [8, 2048, 6], P('exp', 'seq'), may hold values from 0.1 to 0.9
- gate_weight: bfloat16 [8, 2048, 1408], P('exp', 'seq'), may hold values from -0.125 to 0.125
- up_weight: bfloat16 [8, 2048, 1408], P('exp', 'seq'), may hold values from -0.125 to 0.125
- down_weight: bfloat16 [8, 1408, 2048], P('exp', None, 'seq'), may hold values from -0.15625 to 0.15625
- cotangent: bfloat16 [8, 8192, 2048], P('exp', 'seq'), may hold values from -6 to 6
Outputs:
- output: bfloat16 [8, 8192, 2048], P('exp', 'seq')
- input_grad: bfloat16 [8, 8192, 2048], P('exp', 'seq')
- projected_grad: bfloat16 [8, 2048, 6144], P('exp', 'seq')
- gate_grads: float32 [8, 2048, 6], P('exp', 'seq')
The draws below stay inside these ranges and needn't reach their ends.
Inputs may be any that keep to these rules, and one draw needn't show every extreme that they name: `kept_index`: within each device's list of 64 entries the local indices are distinct and rise; the first kept_count entries are the kept tokens, the rest are padding. `kept_count`: every sequence has a device whose list is entirely live. `expert_ids`: each entry names 6 different experts; every expert is named. In one device's list each expert below 8 is named at most 12 times, only by live entries, and for every index of seq one such expert is named exactly 12 times in the list of every device of that index.
All inputs are finite; a program needn't handle non-finite values.
Results may differ from the reference program's by a relative error of at most 0.014.
Values may be sent and summed in bfloat16 or wider, within the bound.
A program may use at most 128 MiB of HBM per device.

```python
import math
from functools import partial
import jax
import jax.numpy as jnp
from jax import lax

D = 2048
HEADS = 16
HS = 128
FF = 1408
EXPERTS = 64
TOPK = 6
TOK_DEV = 256
KEEP_CAP = 64
CAP = 12
SEQS = 8
FLIGHT = 8
TOKENS = 8192
KS = 2048
N_SEQ = 32


def draw_residual(key, part):
    key = jax.random.fold_in(key, 3)
    first, second, third = jax.random.split(key, 3)
    shape = (SEQS, TOKENS, D)
    row_scale = jnp.exp(jax.random.uniform(first, (SEQS, TOKENS, 1), jnp.float32, math.log(0.3), math.log(3.0)))
    column_scale = jnp.exp(jax.random.uniform(second, (1, 1, D), jnp.float32, math.log(0.3), math.log(3.0)))
    base = jnp.clip(jax.random.normal(third, shape, jnp.float32), -4.0, 4.0)
    return (base * row_scale * column_scale).astype(jnp.bfloat16)


def draw_kept_index(key, part):
    key = jax.random.fold_in(key, 5)
    block_keys = jax.random.split(key, SEQS * N_SEQ)

    def one_list(block_key):
        picked = jax.random.permutation(block_key, TOK_DEV)[:KEEP_CAP]
        return jnp.sort(picked).astype(jnp.int32)
    return jax.vmap(one_list)(block_keys).reshape(SEQS, KS)


def draw_kept_count(key, part):
    key = jax.random.fold_in(key, 6)
    first, second = jax.random.split(key)
    counts = jax.random.randint(first, (SEQS, N_SEQ), KEEP_CAP // 4, KEEP_CAP + 1)
    full_at = jax.random.randint(second, (SEQS, 1), 0, N_SEQ)
    return jnp.where(jnp.arange(N_SEQ)[None, :] == full_at, KEEP_CAP, counts).astype(jnp.int32)


def draw_expert_ids(key, part):
    key = jax.random.fold_in(key, 7)
    full_key, block_key = jax.random.split(key)
    full_expert = jax.random.randint(full_key, (N_SEQ,), 0, FLIGHT)
    quarter = KEEP_CAP // 4
    remain_rows = KEEP_CAP - quarter
    others = EXPERTS - FLIGHT
    lowest = CAP // 2
    highest = CAP - 1

    def one_list(list_key, favored):
        key_one, key_two, key_three, key_four, key_five = jax.random.split(list_key, 5)
        loads_in = jax.random.randint(key_one, (FLIGHT,), lowest, highest + 1)
        loads_in = jnp.where(jnp.arange(FLIGHT) == favored, CAP, loads_in)
        remaining = KEEP_CAP * TOPK - jnp.sum(loads_in)
        loads_out = remaining // others + (jnp.arange(others) < remaining % others).astype(jnp.int32)
        order_in = jax.random.permutation(key_two, FLIGHT)
        order_out = FLIGHT + jax.random.permutation(key_three, others)
        names = jnp.concatenate([order_in, order_out]).astype(jnp.int32)
        loads = jnp.concatenate([loads_in[order_in], loads_out])
        ends = jnp.cumsum(loads)
        spots = jnp.arange(KEEP_CAP * TOPK, dtype=jnp.int32)
        which = jnp.searchsorted(ends, spots, side='right')
        chosen = names[which]
        early = spots < quarter * TOPK
        later = spots - quarter * TOPK
        row_at = jnp.where(early, spots % quarter, quarter + later % remain_rows)
        column_at = jnp.where(early, spots // quarter, later // remain_rows)
        table = jnp.zeros((KEEP_CAP, TOPK), jnp.int32).at[row_at, column_at].set(chosen)
        shuffle = jnp.concatenate([jax.random.permutation(key_four, quarter), quarter + jax.random.permutation(key_five, remain_rows)])
        return table[shuffle]
    list_keys = jax.random.split(block_key, SEQS * N_SEQ)
    favored_all = jnp.tile(full_expert, SEQS)
    return jax.vmap(one_list)(list_keys, favored_all).reshape(SEQS, KS, TOPK)


def draw_projected(key, part):
    key = jax.random.fold_in(key, 9)
    shape = (SEQS, KS, 3 * D)
    values = jnp.clip(jax.random.normal(key, shape, jnp.float32), -6.0, 6.0)
    return values.astype(jnp.bfloat16)


def steps_of(own_key, dims, cuts, smallest, high):
    factor_of = 1.0
    for dim, parts in cuts:
        heights = jax.random.uniform(jax.random.fold_in(jax.random.fold_in(own_key, 6), dim), (parts,), jnp.float32, smallest / len(cuts), high / len(cuts))
        factor_of = factor_of * jnp.repeat(jnp.exp(heights), dims[dim] // parts).reshape((-1,) + (1,) * (len(dims) - 1 - dim))
    return factor_of


def scatter_about(stream_key, dims, scale, bound, pieces=(), kind=jnp.bfloat16):
    values = jax.random.normal(stream_key, dims, jnp.float32) * scale
    if len(pieces) > 0:
        values = steps_of(stream_key, dims, pieces, -0.22, 0.18) * values
    return jnp.clip(values, min=-bound, max=bound).astype(kind)


def setup_inputs(seed: int = 0) -> dict:
    splits = jax.random.split(jax.random.key(seed), 11)
    return {
        "residual": draw_residual(jax.random.fold_in(splits[10], 71), 0),
        "kept_index": draw_kept_index(jax.random.fold_in(splits[10], 71), 0),
        "kept_count": draw_kept_count(jax.random.fold_in(splits[10], 71), 0),
        "projected": draw_projected(jax.random.fold_in(splits[10], 71), 0),
        "expert_ids": draw_expert_ids(jax.random.fold_in(splits[10], 71), 0),
        "gate_values": jnp.clip(0.1 + 0.79999997 * jax.random.uniform(splits[5], (SEQS, KS, TOPK), jnp.float32) ** steps_of(splits[5], (SEQS, KS, TOPK), ((0, 8), (1, 32)), -0.2, 0.2), 0.1, 0.9),
        "gate_weight": scatter_about(splits[6], (FLIGHT, D, FF), D ** -0.5, 0.125, ((0, 8), (1, 32))),
        "up_weight": scatter_about(splits[7], (FLIGHT, D, FF), D ** -0.5, 0.125, ((0, 8), (1, 32))),
        "down_weight": scatter_about(splits[8], (FLIGHT, FF, D), FF ** -0.5, 0.15625, ((0, 8), (2, 32))),
        "cotangent": scatter_about(splits[9], (SEQS, TOKENS, D), 1.0, 6.0, ((0, 8), (1, 32))),
    }


EPSILON = 1e-06

def dispatch_tables(expert_list, live_rows, weight_list, flight, capacity):
    experts = jnp.arange(flight, dtype=jnp.int32)
    matches = (expert_list[:, :, None] == experts[None, None, :]) & live_rows[:, None, None]
    assigned = jnp.any(matches, axis=1).astype(jnp.int32)
    slot_rank = jnp.cumsum(assigned, axis=0) - assigned
    slot_ids = jnp.arange(capacity, dtype=jnp.int32)
    chosen = (assigned[None, :, :] == 1) & (slot_rank[None, :, :] == slot_ids[:, None, None])
    slot_table = jnp.transpose(chosen, (2, 0, 1)).astype(jnp.float32)
    weight_at = lax.optimization_barrier(jnp.sum(jnp.where(matches, weight_list[:, :, None], 0.0), axis=1))
    slot_gate = lax.optimization_barrier(jnp.sum(slot_table * jnp.transpose(weight_at)[:, None, :], axis=2))
    return (slot_table, matches.astype(jnp.float32), weight_at, slot_gate)

def allowed_mask(position, live_rows):
    causal = live_rows[None, :] & (position[None, :] <= position[:, None])
    first_key = (jnp.arange(position.shape[0]) == 0)[None, :]
    return jnp.where(live_rows[:, None], causal, first_key)

def probabilities(query, key_rows, allowed):
    scores = jnp.dot(query, key_rows.T, preferred_element_type=jnp.float32) * HS ** (-0.5)
    scores = jnp.where(allowed, scores, -jnp.inf)
    row_max = lax.optimization_barrier(jnp.max(scores, axis=-1, keepdims=True))
    exponent = jnp.exp(scores - row_max)
    return exponent / lax.optimization_barrier(jnp.sum(exponent, axis=-1, keepdims=True))

def head_forward(inputs):
    query, key_rows, value_rows, position, live_rows = inputs
    attention = probabilities(query, key_rows, allowed_mask(position, live_rows))
    return jnp.dot(attention.astype(jnp.bfloat16), value_rows, preferred_element_type=jnp.float32)

def head_backward(inputs):
    query, key_rows, value_rows, position, live_rows, grad_out, attended_f = inputs
    attention = probabilities(query, key_rows, allowed_mask(position, live_rows))
    rounded = attention.astype(jnp.bfloat16)
    row_delta = lax.optimization_barrier(jnp.sum(grad_out.astype(jnp.float32) * attended_f, axis=-1, keepdims=True))
    grad_prob = jnp.dot(grad_out, value_rows.T, preferred_element_type=jnp.float32)
    score_grad = (attention * (grad_prob - row_delta) * HS ** (-0.5)).astype(jnp.bfloat16)
    query_grad = jnp.dot(score_grad, key_rows, preferred_element_type=jnp.float32).astype(jnp.bfloat16)
    key_grad = jnp.dot(score_grad.T, query, preferred_element_type=jnp.float32).astype(jnp.bfloat16)
    value_grad = jnp.dot(rounded.T, grad_out, preferred_element_type=jnp.float32).astype(jnp.bfloat16)
    return (query_grad, key_grad, value_grad)

def expert_forward(inputs):
    row_data, gate_w, up_w, down_w = inputs
    gate_pre = jnp.dot(row_data, gate_w, preferred_element_type=jnp.float32)
    up_pre = jnp.dot(row_data, up_w, preferred_element_type=jnp.float32)
    middle = (gate_pre * jax.nn.sigmoid(gate_pre) * up_pre).astype(jnp.bfloat16)
    return (gate_pre, up_pre, jnp.dot(middle, down_w, preferred_element_type=jnp.float32).astype(jnp.bfloat16))

def expert_backward(inputs):
    grads, gate_pre, up_pre, gate_w, up_w, down_w = inputs
    mid_grad = jnp.dot(grads, down_w.T, preferred_element_type=jnp.float32)
    sigma = jax.nn.sigmoid(gate_pre)
    gate_grad = (mid_grad * up_pre * sigma * (1.0 + gate_pre * (1.0 - sigma))).astype(jnp.bfloat16)
    up_grad = (mid_grad * gate_pre * sigma).astype(jnp.bfloat16)
    summed = jnp.dot(gate_grad, gate_w.T, preferred_element_type=jnp.float32) + jnp.dot(up_grad, up_w.T, preferred_element_type=jnp.float32)
    return summed.astype(jnp.bfloat16)

def split_heads(values):
    return jnp.transpose(values.reshape(SEQS, KS, HEADS, HS), (0, 2, 1, 3)).reshape(SEQS * HEADS, KS, HS)

def join_heads(values):
    return jnp.transpose(values.reshape(SEQS, HEADS, KS, HS), (0, 2, 1, 3)).reshape(SEQS, KS, D)

def place_rows(target, position, row_data):
    return target.at[position].set(row_data)

def reference(residual, kept_index, kept_count, projected, expert_ids, gate_values, gate_weight, up_weight, down_weight, cotangent):
    entries = jnp.arange(KS, dtype=jnp.int32)
    shard_of = entries // KEEP_CAP
    live_rows = (entries % KEEP_CAP)[None, :] < kept_count[:, shard_of]
    position = shard_of[None, :] * TOK_DEV + kept_index
    kept_rows = jnp.take_along_axis(residual, position[:, :, None], axis=1)
    query = split_heads(projected[:, :, :D])
    key_rows = split_heads(projected[:, :, D:2 * D])
    value_rows = split_heads(projected[:, :, 2 * D:])
    position_heads = jnp.repeat(position, HEADS, axis=0)
    live_heads = jnp.repeat(live_rows, HEADS, axis=0)
    attended_f = lax.map(head_forward, (query, key_rows, value_rows, position_heads, live_heads))
    attended = join_heads(attended_f).astype(jnp.bfloat16)
    hidden_one = jnp.where(live_rows[:, :, None], kept_rows.astype(jnp.float32) + attended.astype(jnp.float32), 0.0)
    inv_rms = lax.rsqrt(lax.optimization_barrier(jnp.mean(hidden_one * hidden_one, axis=-1, keepdims=True)) + EPSILON)
    normed = (hidden_one * inv_rms).astype(jnp.bfloat16)
    blocks = SEQS * N_SEQ
    live_blocks = live_rows.reshape(blocks, KEEP_CAP)
    slot_table, matches, weight_at, slot_gate = jax.vmap(partial(dispatch_tables, flight=FLIGHT, capacity=CAP))(expert_ids.reshape(blocks, KEEP_CAP, TOPK), live_blocks, gate_values.reshape(blocks, KEEP_CAP, TOPK))
    normed_blocks = normed.reshape(blocks, KEEP_CAP, D).astype(jnp.float32)
    row_data = jnp.einsum('beci,bid->becd', slot_table, normed_blocks).astype(jnp.bfloat16)
    per_expert = jnp.transpose(row_data, (1, 0, 2, 3)).reshape(FLIGHT, blocks * CAP, D)
    gate_pre, up_pre, expert_out = lax.map(expert_forward, (per_expert, gate_weight, up_weight, down_weight))
    out_blocks = jnp.transpose(expert_out.reshape(FLIGHT, blocks, CAP, D), (1, 0, 2, 3)).astype(jnp.float32)
    weighted = slot_table * jnp.transpose(weight_at, (0, 2, 1))[:, :, None, :]
    mixture = jnp.einsum('beci,becd->bid', weighted, out_blocks)
    hidden_blocks = hidden_one.reshape(blocks, KEEP_CAP, D)
    kept_blocks = kept_rows.reshape(blocks, KEEP_CAP, D)
    new_rows = jnp.where(live_blocks[:, :, None], (hidden_blocks + mixture).astype(jnp.bfloat16), kept_blocks)
    output = jax.vmap(place_rows)(residual, position, new_rows.reshape(SEQS, KS, D))
    grad_rows = jnp.take_along_axis(cotangent, position[:, :, None], axis=1).reshape(blocks, KEEP_CAP, D)
    grad_f = grad_rows.astype(jnp.float32)
    products = jnp.einsum('becd,bid->beci', out_blocks, grad_f)
    per_entry = lax.optimization_barrier(jnp.sum(slot_table * products, axis=2))
    gate_grads = jnp.einsum('bike,bei->bik', matches, per_entry).reshape(SEQS, KS, TOPK)
    expert_grad = (slot_gate[:, :, :, None] * jnp.einsum('beci,bid->becd', slot_table, grad_f)).astype(jnp.bfloat16)
    per_expert_grad = jnp.transpose(expert_grad, (1, 0, 2, 3)).reshape(FLIGHT, blocks * CAP, D)
    rows_grad = lax.map(expert_backward, (per_expert_grad, gate_pre, up_pre, gate_weight, up_weight, down_weight))
    back_blocks = jnp.transpose(rows_grad.reshape(FLIGHT, blocks, CAP, D), (1, 0, 2, 3)).astype(jnp.float32)
    normed_grad = jnp.einsum('beci,becd->bid', slot_table, back_blocks)
    inv_blocks = inv_rms.reshape(blocks, KEEP_CAP, 1)
    cubed = inv_blocks * inv_blocks * inv_blocks
    hidden_grad = grad_f + inv_blocks * normed_grad - hidden_blocks * cubed * lax.optimization_barrier(jnp.mean(normed_grad * hidden_blocks, axis=-1, keepdims=True))
    hidden_grad = jnp.where(live_blocks[:, :, None], hidden_grad, 0.0).astype(jnp.bfloat16)
    grad_rows_new = jnp.where(live_blocks[:, :, None], hidden_grad, grad_rows)
    input_grad = jax.vmap(place_rows)(cotangent, position, grad_rows_new.reshape(SEQS, KS, D))
    grad_out = split_heads(hidden_grad.reshape(SEQS, KS, D))
    query_grad, key_grad, value_grad = lax.map(head_backward, (query, key_rows, value_rows, position_heads, live_heads, grad_out, attended_f))
    projected_grad = jnp.concatenate([join_heads(query_grad), join_heads(key_grad), join_heads(value_grad)], axis=-1)
    return (output, input_grad, projected_grad, gate_grads)
```

```python
import functools

import jax
import jax.numpy as jnp
from jax import lax
from jax.experimental import pallas as pl
from jax.experimental.pallas import tpu as pltpu
from jax.sharding import PartitionSpec as P

HS = 128
SLOT = 16
EPSILON = 1e-06
X = 4
QSRC = 8
F32 = jnp.float32
BF16 = jnp.bfloat16
MESH = pl.DeviceIdType.MESH
NEG = -1e30


def nn(a, b):
    return lax.dot_general(a, b, (((1,), (0,)), ((), ())), preferred_element_type=F32)


def nt(a, b):
    return lax.dot_general(a, b, (((1,), (1,)), ((), ())), preferred_element_type=F32)


def kernel(
    S,
    E,
    residual,
    kept_index,
    kept_count,
    projected,
    expert_ids,
    gate_values,
    gate_w,
    up_w,
    down_w,
    cotangent,
    output,
    input_grad,
    projected_grad,
    gate_grads,
    q_send,
    q_recv,
    a_send,
    a_recv,
    g_send,
    g_recv,
    b_send,
    b_recv,
    x_send,
    x_recv,
    gu,
    dn,
    bias,
    k_t,
    v_t,
    prob,
    att_t,
    dk_acc,
    dv_acc,
    q_ss,
    q_rs,
    a_ss,
    a_rs,
    g_ss,
    g_rs,
    b_ss,
    b_rs,
    x_ss,
    x_rs,
    gu_rs,
    dn_rs,
    gu_zs,
    gu_xs,
    dn_xs,
    dn_zs,
):
    Z = S // X
    KEEP = kept_index.shape[1]
    TOK, D = residual.shape
    FF = gate_w.shape[1]
    HEADS = D // HS
    SPLIT = S // HEADS
    PR = KEEP // SPLIT
    NB = S // QSRC
    KB = QSRC * KEEP
    QB = QSRC * PR
    NS = E * SLOT
    XD = X
    scale = HS**-0.5
    me = lax.axis_index("seq")
    ex = lax.axis_index("exp")
    mx = me // Z
    mz = lax.rem(me, Z)
    part = lax.rem(me, SPLIT)

    barrier = pltpu.get_barrier_semaphore()

    def greet_seq(k, c):
        pl.semaphore_signal(
            barrier, inc=1, device_id={"seq": lax.rem(me + k, S)}, device_id_type=MESH
        )
        return c

    def greet_exp(k, c):
        pl.semaphore_signal(
            barrier, inc=1, device_id={"exp": lax.rem(ex + k, E)}, device_id_type=MESH
        )
        return c

    lax.fori_loop(1, S, greet_seq, 0)
    lax.fori_loop(1, E, greet_exp, 0)

    count = kept_count[...]
    meta = jnp.broadcast_to(count.astype(F32), (16, HS)).astype(BF16)
    for d in range(S):
        h, p = d // SPLIT, d % SPLIT
        c0 = h * HS
        q_send[d, 0:KEEP] = projected[:, D + c0 : D + c0 + HS]
        q_send[d, KEEP : 2 * KEEP] = projected[:, 2 * D + c0 : 2 * D + c0 + HS]
        q_send[d, 2 * KEEP : 2 * KEEP + PR] = projected[p * PR : (p + 1) * PR, c0 : c0 + HS]
        q_send[d, 2 * KEEP + PR :] = meta
    gu[mx, mz, 0] = gate_w[...]
    gu[mx, mz, 1] = up_w[...]
    dn[mx, mz] = down_w[...]
    q_recv[me] = q_send[me]

    pl.semaphore_wait(barrier, S - 1 + E - 1)

    def to_seq(send, recv, ss, rs, d):
        return pltpu.make_async_remote_copy(
            src_ref=send.at[d],
            dst_ref=recv.at[me],
            send_sem=ss.at[d],
            recv_sem=rs.at[me],
            device_id={"seq": d},
            device_id_type=MESH,
        )

    def from_seq(send, recv, ss, rs, d):
        return pltpu.make_async_remote_copy(
            src_ref=send.at[d],
            dst_ref=recv.at[d],
            send_sem=ss.at[d],
            recv_sem=rs.at[d],
            device_id={"seq": d},
            device_id_type=MESH,
        )

    def start_all(*arrays):
        def step(k, c):
            to_seq(*arrays, lax.rem(me + k, S)).start()
            return c

        lax.fori_loop(1, S, step, 0)

    def start_block(block, *arrays):
        def step(k, c):
            d = block * QSRC + lax.rem(me + k, QSRC)

            @pl.when(d != me)
            def _():
                to_seq(*arrays, d).start()

            return c

        lax.fori_loop(0, QSRC, step, 0)

    def recv_all(*arrays):
        def step(k, c):
            from_seq(*arrays, lax.rem(me + k, S)).wait_recv()
            return c

        lax.fori_loop(1, S, step, 0)

    def sent_all(*arrays):
        def step(k, c):
            to_seq(*arrays, lax.rem(me + k, S)).wait_send()
            return c

        lax.fori_loop(1, S, step, 0)

    def exp_copy(n, d, slot):
        return pltpu.make_async_remote_copy(
            src_ref=x_send.at[n, d],
            dst_ref=x_recv.at[n, slot],
            send_sem=x_ss.at[n, d],
            recv_sem=x_rs.at[n, slot],
            device_id={"exp": d},
            device_id_type=MESH,
        )

    def exp_start(n):
        x_recv[n, ex] = x_send[n, ex]

        def step(k, c):
            exp_copy(n, lax.rem(ex + k, E), ex).start()
            return c

        lax.fori_loop(1, E, step, 0)

    def exp_recv(n):
        def step(k, c):
            d = lax.rem(ex + k, E)
            exp_copy(n, d, d).wait_recv()
            return c

        lax.fori_loop(1, E, step, 0)

    def exp_sent(n):
        def step(k, c):
            exp_copy(n, lax.rem(ex + k, E), ex).wait_send()
            return c

        lax.fori_loop(1, E, step, 0)

    sent = []

    def at_x(o):
        return lax.rem(mx + o + X, X)

    def at_z(o):
        return lax.rem(mz + o + Z, Z)

    def piece(ref, sems, ox, oz, half, dev, ss):
        ax, az = at_x(ox), at_z(oz)
        view = ref.at[ax, az]
        if half is not None:
            view = ref.at[ax, az, half]
        return pltpu.make_async_remote_copy(
            src_ref=view,
            dst_ref=view,
            send_sem=ss,
            recv_sem=sems.at[ax, az, half or 0],
            device_id={"seq": dev},
            device_id_type=MESH,
        )

    def send(ref, sems, ox, oz, half, dev, ss):
        copy = piece(ref, sems, ox, oz, half, dev, ss)
        copy.start()
        sent.append(copy)

    def wait(ref, sems, ox, oz, halves):
        for half in (0, 1) if halves else (None,):
            piece(ref, sems, ox, oz, half, me, gu_zs.at[0, 0]).wait_recv()

    def side(axis, sgn):
        if axis == "x":
            return at_x(sgn) * Z + mz
        return mx * Z + at_z(sgn)

    def hop(ref, sems, axis, sgn, k, other, ss):
        n = X if axis == "x" else Z
        if k >= n // 2:
            return
        half = None if k < n // 2 - 1 else (0 if sgn > 0 else 1)
        ox, oz = (-sgn * k, other) if axis == "x" else (other, -sgn * k)
        send(ref, sems, ox, oz, half, side(axis, sgn), ss.at[0 if sgn > 0 else 1, other % 8, k])

    def gu_z(sgn, k):
        hop(gu, gu_rs, "z", sgn, k, 0, gu_zs)

    def gu_x(sgn, k, oz):
        hop(gu, gu_rs, "x", sgn, k, oz, gu_xs)

    def dn_x(sgn, k):
        hop(dn, dn_rs, "x", sgn, k, 0, dn_xs)

    def dn_z(sgn, k, ox):
        hop(dn, dn_rs, "z", sgn, k, ox, dn_zs)

    both = (1, -1)

    def gu_along_z(k):
        if k == Z // 2:
            wait(gu, gu_rs, 0, k, True)
            for s in both:
                gu_x(s, 0, k)
            return
        for s in both:
            wait(gu, gu_rs, 0, -s * k, False)
            gu_z(s, k)
            for t in both:
                gu_x(t, 0, -s * k)

    def gu_along_x(oz):
        for s in both:
            wait(gu, gu_rs, -s, oz, False)
            gu_x(s, 1, oz)

    def dn_along_x(k):
        if k == X // 2:
            wait(dn, dn_rs, k, 0, True)
            for s in both:
                dn_z(s, 0, k)
            return
        for s in both:
            wait(dn, dn_rs, -s * k, 0, False)
            dn_x(s, k)
            for t in both:
                dn_z(t, 0, -s * k)

    def dn_along_z(k, ox):
        for s in both:
            wait(dn, dn_rs, ox, -s * k, False)
            dn_z(s, k, ox)

    def ring_start():
        for s in both:
            gu_z(s, 0)
        for s in both:
            dn_x(s, 0)
        for s in both:
            gu_x(s, 0, 0)
        for s in both:
            dn_z(s, 0, 0)

    def ring_first():
        dn_along_x(1)
        gu_along_z(1)
        dn_along_x(2)
        gu_along_x(0)
        dn_along_z(1, 0)

    def ring_round(k):
        gu_along_z(k)
        for oz in (k - 1, 1 - k):
            gu_along_x(oz)
        if k < Z // 2:
            for ox in (1, -1, 2):
                dn_along_z(k - 1, ox)
            dn_along_z(k, 0)
        else:
            for ox in (1, -1, 2):
                dn_along_z(k - 1, ox)

    def ring_last():
        gu_along_x(Z // 2)
        for oz in range(Z):
            wait(gu, gu_rs, X // 2, oz, True)
        for ox in (0, 1, -1, 2):
            wait(dn, dn_rs, ox, Z // 2, True)

    start_all(q_send, q_recv, q_ss, q_rs)
    ring_start()

    slot_row = lax.broadcasted_iota(jnp.int32, (NS, KEEP), 0)
    slot_exp = slot_row // SLOT
    slot_pos = slot_row - slot_exp * SLOT
    entry = lax.broadcasted_iota(jnp.int32, (NS, KEEP), 1)
    live = entry < count
    assigned = jnp.zeros((NS, KEEP), F32)
    weight = jnp.zeros((NS, KEEP), F32)
    for k in range(expert_ids.shape[0]):
        match = (expert_ids[k : k + 1, :] == slot_exp) & live
        assigned = assigned + jnp.where(match, 1.0, 0.0)
        weight = weight + jnp.where(match, gate_values[k : k + 1, :], 0.0)
    ei = lax.broadcasted_iota(jnp.int32, (KEEP, KEEP), 0)
    ej = lax.broadcasted_iota(jnp.int32, (KEEP, KEEP), 1)
    earlier = jnp.where(ei < ej, 1.0, 0.0).astype(BF16)
    rank = nn(assigned.astype(BF16), earlier)
    table = jnp.where((assigned > 0.5) & (rank == slot_pos.astype(F32)), 1.0, 0.0)
    table_half = table.astype(BF16)
    weighted = table * weight
    slot_gate = jnp.sum(weighted, axis=1, keepdims=True)

    def turned(a):
        if a.shape[1] < 128:
            a = jnp.concatenate([a, jnp.zeros((a.shape[0], 128 - a.shape[1]), F32)], 1)
        return a.T

    table_t = turned(table)[:KEEP].astype(BF16)
    weighted_t = turned(weighted)[:KEEP]
    w_high = weighted_t.astype(BF16)
    w_low = (weighted_t - w_high.astype(F32)).astype(BF16)

    index_row = kept_index[...]
    index_col = jnp.sum(jnp.where(ei == ej, index_row, 0), axis=1, keepdims=True)
    pick = jnp.where(
        lax.broadcasted_iota(jnp.int32, (KEEP, TOK), 1) == index_col, 1.0, 0.0
    ).astype(BF16)
    live_col = lax.broadcasted_iota(jnp.int32, (KEEP, 1), 0) < count
    grad_f = nn(pick, cotangent[...])
    kept_f = nn(pick, residual[...])
    grad_sel = nn(table_half, grad_f.astype(BF16))
    x_send[0] = (slot_gate * grad_sel).astype(BF16).reshape(E, SLOT, D)
    grad_sel = grad_sel.astype(BF16)
    exp_start(0)

    ring_first()
    recv_all(q_send, q_recv, q_ss, q_rs)

    row_in = lax.broadcasted_iota(jnp.int32, (S, KEEP, HS), 1).astype(F32)
    counts = q_recv[:, 2 * KEEP + PR : 2 * KEEP + PR + 16, :].astype(F32)[:, 0:1, :]
    bias[...] = jnp.where(row_in < counts, 0.0, NEG).reshape(S * KEEP, HS)
    for b in range(NB):
        k_blk = q_recv[b * QSRC : (b + 1) * QSRC, 0:KEEP].reshape(KB, HS)
        v_blk = q_recv[b * QSRC : (b + 1) * QSRC, KEEP : 2 * KEEP].reshape(KB, HS)
        k_t[:, b * KB : (b + 1) * KB] = k_blk.astype(F32).T.astype(BF16)
        v_t[:, b * KB : (b + 1) * KB] = v_blk.astype(F32).T.astype(BF16)

    qcol = lax.broadcasted_iota(jnp.int32, (KB, QB), 1)
    qent = (qcol // PR) * KEEP + part * PR + lax.rem(qcol, PR)
    causal = lax.broadcasted_iota(jnp.int32, (KB, QB), 0) <= qent

    def key_block(c):
        return q_recv[c * QSRC : (c + 1) * QSRC, 0:KEEP].reshape(KB, HS)

    def value_block(c):
        return q_recv[c * QSRC : (c + 1) * QSRC, KEEP : 2 * KEEP].reshape(KB, HS)

    def query_block(b):
        return q_recv[b * QSRC : (b + 1) * QSRC, 2 * KEEP : 2 * KEEP + PR].reshape(QB, HS)

    def forward_block(b):
        cols = slice(b * QB, (b + 1) * QB)
        q_blk = query_block(b)
        top = None
        for c in range(b + 1):
            rows = slice(c * KB, (c + 1) * KB)
            half = bias[rows, :]
            sc = nt(key_block(c), q_blk) * scale + jnp.concatenate([half] * (QB // HS), 1)
            if c == b:
                sc = jnp.where(causal, sc, NEG)
            prob[rows, cols] = sc
            m = jnp.max(sc, axis=0, keepdims=True)
            top = m if top is None else jnp.maximum(top, m)
        total = jnp.zeros((1, QB), F32)
        for c in range(b + 1):
            rows = slice(c * KB, (c + 1) * KB)
            e = jnp.exp(prob[rows, cols] - top)
            prob[rows, cols] = e
            total = total + jnp.sum(e, axis=0, keepdims=True)
        inv = 1.0 / total
        acc = jnp.zeros((HS, QB), F32)
        for c in range(b + 1):
            rows = slice(c * KB, (c + 1) * KB)
            pr = prob[rows, cols] * inv
            prob[rows, cols] = pr
            acc = acc + nn(v_t[:, rows], pr.astype(BF16))
        att_t[:, cols] = acc
        a_send[b * QSRC : (b + 1) * QSRC] = acc.T.astype(BF16).reshape(QSRC, PR, HS)
        start_block(b, a_send, a_recv, a_ss, a_rs)

    for b in range(NB):
        forward_block(b)
        if b == 1:
            ring_round(2)
    a_recv[me] = a_send[me]
    recv_all(a_send, a_recv, a_ss, a_rs)

    def rows_of(recv):
        parts = []
        for p in range(SPLIT):
            parts.append(jnp.concatenate([recv[h * SPLIT + p] for h in range(HEADS)], 1))
        return jnp.concatenate(parts, 0)

    h1 = jnp.where(live_col, kept_f + rows_of(a_recv).astype(F32), 0.0)
    inv_rms = lax.rsqrt(jnp.mean(h1 * h1, axis=1, keepdims=True) + EPSILON)
    normed = (h1 * inv_rms).astype(BF16)
    x_send[1] = nn(table_half, normed).astype(BF16).reshape(E, SLOT, D)
    exp_start(1)
    for k in range(3, Z // 2 + 1):
        ring_round(k)
    exp_recv(0)
    exp_recv(1)
    ring_last()

    rows_in = x_recv[1].reshape(NS, D)
    grads_in = x_recv[0].reshape(NS, D)
    KC = Z * KEEP
    gate_pre = jnp.zeros((NS, FF), F32)
    up_pre = jnp.zeros((NS, FF), F32)
    mid_grad = jnp.zeros((NS, FF), F32)
    for c in range(XD):
        r = rows_in[:, c * KC : (c + 1) * KC]
        gate_pre = gate_pre + nn(r, gu[c, :, 0].reshape(KC, FF))
        up_pre = up_pre + nn(r, gu[c, :, 1].reshape(KC, FF))
        mid_grad = mid_grad + nn(
            grads_in[:, c * KC : (c + 1) * KC], dn[c].reshape(KC, FF)
        )
    sig = 1.0 / (1.0 + jnp.exp(-gate_pre))
    act = gate_pre * sig
    gate_grad = (mid_grad * up_pre * sig * (1.0 + gate_pre * (1.0 - sig))).astype(BF16)
    up_grad = (mid_grad * act).astype(BF16)
    mid = (act * up_pre).astype(BF16)
    for c in range(XD):
        back = nt(gate_grad, gu[c, :, 0].reshape(KC, FF)) + nt(
            up_grad, gu[c, :, 1].reshape(KC, FF)
        )
        x_send[2, :, :, c * KC : (c + 1) * KC] = back.astype(BF16).reshape(E, SLOT, KC)
    exp_start(2)
    for c in range(XD):
        made = nt(mid, dn[c].reshape(KC, FF))
        x_send[3, :, :, c * KC : (c + 1) * KC] = made.astype(BF16).reshape(E, SLOT, KC)
    exp_start(3)
    exp_recv(2)
    normed_grad = nn(table_t, x_recv[2].reshape(NS, D))
    cubed = inv_rms * inv_rms * inv_rms
    h1_grad = (
        grad_f
        + inv_rms * normed_grad
        - h1 * cubed * jnp.mean(normed_grad * h1, axis=1, keepdims=True)
    )
    h1_grad = jnp.where(live_col, h1_grad, 0.0).astype(BF16)
    for d in range(S):
        h, p = d // SPLIT, d % SPLIT
        g_send[d] = h1_grad[p * PR : (p + 1) * PR, h * HS : (h + 1) * HS]
    g_recv[me] = g_send[me]
    start_all(g_send, g_recv, g_ss, g_rs)

    token = lax.broadcasted_iota(jnp.int32, (TOK, KEEP), 0)
    put = jnp.where(
        (token == index_row)
        & (lax.broadcasted_iota(jnp.int32, (TOK, KEEP), 1) < count),
        1.0,
        0.0,
    )
    replaced = jnp.sum(put, axis=1, keepdims=True) > 0.5
    put = put.astype(BF16)
    input_grad[...] = jnp.where(replaced, nn(put, h1_grad), cotangent[...].astype(F32)).astype(
        BF16
    )
    exp_recv(3)
    results = x_recv[3].reshape(NS, D)
    mixture = nn(w_high, results) + nn(w_low, results)
    new_rows = (h1 + mixture).astype(BF16)
    output[...] = jnp.where(replaced, nn(put, new_rows), residual[...].astype(F32)).astype(BF16)
    per_slot = jnp.sum(results.astype(F32) * grad_sel.astype(F32), axis=1, keepdims=True)
    spread = table * per_slot
    for k in range(expert_ids.shape[0]):
        hit = expert_ids[k : k + 1, :] == slot_exp
        gate_grads[k : k + 1, :] = jnp.sum(jnp.where(hit, spread, 0.0), axis=0, keepdims=True)

    recv_all(g_send, g_recv, g_ss, g_rs)
    dk_acc[...] = jnp.zeros_like(dk_acc)
    dv_acc[...] = jnp.zeros_like(dv_acc)
    for b in reversed(range(NB)):
        cols = slice(b * QB, (b + 1) * QB)
        q_blk = query_block(b)
        dout = g_recv[b * QSRC : (b + 1) * QSRC].reshape(QB, HS)
        delta = jnp.sum(dout.astype(F32).T * att_t[:, cols], axis=0, keepdims=True)
        dq_t = jnp.zeros((HS, QB), F32)
        for c in range(b + 1):
            rows = slice(c * KB, (c + 1) * KB)
            pr = prob[rows, cols]
            ds = (pr * (nt(value_block(c), dout) - delta) * scale).astype(BF16)
            dq_t = dq_t + nn(k_t[:, rows], ds)
            dk_acc[rows] += nn(ds, q_blk)
            dv_acc[rows] += nn(pr.astype(BF16), dout)
        rows = slice(b * KB, (b + 1) * KB)
        src = slice(b * QSRC, (b + 1) * QSRC)
        b_send[src, 0:KEEP] = dk_acc[rows].astype(BF16).reshape(QSRC, KEEP, HS)
        b_send[src, KEEP : 2 * KEEP] = dv_acc[rows].astype(BF16).reshape(QSRC, KEEP, HS)
        b_send[src, 2 * KEEP :] = dq_t.T.astype(BF16).reshape(QSRC, PR, HS)
        start_block(b, b_send, b_recv, b_ss, b_rs)
    b_recv[me] = b_send[me]
    recv_all(b_send, b_recv, b_ss, b_rs)
    for h in range(HEADS):
        c0 = h * HS
        dk = b_recv[h * SPLIT, 0:KEEP].astype(F32)
        dv = b_recv[h * SPLIT, KEEP : 2 * KEEP].astype(F32)
        for p in range(SPLIT):
            projected_grad[p * PR : (p + 1) * PR, c0 : c0 + HS] = b_recv[
                h * SPLIT + p, 2 * KEEP :
            ]
            if p:
                dk = dk + b_recv[h * SPLIT + p, 0:KEEP].astype(F32)
                dv = dv + b_recv[h * SPLIT + p, KEEP : 2 * KEEP].astype(F32)
        projected_grad[:, D + c0 : D + c0 + HS] = dk.astype(BF16)
        projected_grad[:, 2 * D + c0 : 2 * D + c0 + HS] = dv.astype(BF16)

    sent_all(q_send, q_recv, q_ss, q_rs)
    sent_all(a_send, a_recv, a_ss, a_rs)
    sent_all(g_send, g_recv, g_ss, g_rs)
    sent_all(b_send, b_recv, b_ss, b_rs)
    for n in range(4):
        exp_sent(n)
    for copy in sent:
        copy.wait_send()


def body(
    residual,
    kept_index,
    kept_count,
    projected,
    expert_ids,
    gate_values,
    gate_weight,
    up_weight,
    down_weight,
    cotangent,
):
    S = lax.axis_size("seq")
    E = lax.axis_size("exp")
    _, TOK, D = residual.shape
    KEEP = kept_index.shape[1]
    FF = gate_weight.shape[2]
    TOPK = expert_ids.shape[2]
    Z = S // X
    HEADS = D // HS
    PR = KEEP * HEADS // S
    vm = pl.BlockSpec(memory_space=pltpu.VMEM)
    dma = pltpu.SemaphoreType.DMA
    pay = 2 * KEEP + PR + 16
    back = 2 * KEEP + PR
    out = pl.pallas_call(
        functools.partial(kernel, S, E),
        out_shape=[
            jax.ShapeDtypeStruct((TOK, D), BF16),
            jax.ShapeDtypeStruct((TOK, D), BF16),
            jax.ShapeDtypeStruct((KEEP, 3 * D), BF16),
            jax.ShapeDtypeStruct((TOPK, KEEP), F32),
        ],
        in_specs=[vm] * 10,
        out_specs=[vm] * 4,
        scratch_shapes=[
            pltpu.VMEM((S, pay, HS), BF16),
            pltpu.VMEM((S, pay, HS), BF16),
            pltpu.VMEM((S, PR, HS), BF16),
            pltpu.VMEM((S, PR, HS), BF16),
            pltpu.VMEM((S, PR, HS), BF16),
            pltpu.VMEM((S, PR, HS), BF16),
            pltpu.VMEM((S, back, HS), BF16),
            pltpu.VMEM((S, back, HS), BF16),
            pltpu.VMEM((4, E, SLOT, D), BF16),
            pltpu.VMEM((4, E, SLOT, D), BF16),
            pltpu.VMEM((X, Z, 2, KEEP, FF), BF16),
            pltpu.VMEM((X, Z, 2, KEEP // 2, FF), BF16),
            pltpu.VMEM((S * KEEP, HS), F32),
            pltpu.VMEM((HS, S * KEEP), BF16),
            pltpu.VMEM((HS, S * KEEP), BF16),
            pltpu.VMEM((S * KEEP, S * PR), F32),
            pltpu.VMEM((HS, S * PR), F32),
            pltpu.VMEM((S * KEEP, HS), F32),
            pltpu.VMEM((S * KEEP, HS), F32),
        ]
        + [dma((S,))] * 8
        + [dma((4, E))] * 2
        + [
            dma((X, Z, 2)),
            dma((X, Z, 2)),
            dma((2, 8, Z // 2)),
            dma((2, 8, X // 2)),
            dma((2, 8, X // 2)),
            dma((2, 8, Z // 2)),
        ],
        compiler_params=pltpu.CompilerParams(
            collective_id=0, has_side_effects=True, vmem_limit_bytes=60 * 1024 * 1024
        ),
    )(
        residual[0],
        kept_index,
        kept_count,
        projected[0],
        expert_ids[0].T,
        gate_values[0].T,
        gate_weight[0],
        up_weight[0],
        down_weight[0].T.reshape(2, KEEP // 2, FF),
        cotangent[0],
    )
    return (out[0][None], out[1][None], out[2][None], out[3].T[None])


def solution(mesh):
    row = P("exp", "seq", None)
    in_specs = (row, P("exp", "seq"), P("exp", "seq")) + (row,) * 5 + (P("exp", None, "seq"), row)
    return jax.shard_map(
        body, mesh=mesh, in_specs=in_specs, out_specs=(row,) * 4, check_vma=False
    )
```

```python
import functools

import jax
import jax.numpy as jnp
from jax import lax
from jax.experimental import pallas as pl
from jax.experimental.pallas import tpu as pltpu
from jax.sharding import PartitionSpec as P

HS = 128
SLOT = 16
EPSILON = 1e-06
X = 4
QSRC = 8
F32 = jnp.float32
BF16 = jnp.bfloat16
MESH = pl.DeviceIdType.MESH
NEG = -1e30
MARK = 1024.0


def nn(a, b):
    return lax.dot_general(a, b, (((1,), (0,)), ((), ())), preferred_element_type=F32)


def nt(a, b):
    return lax.dot_general(a, b, (((1,), (1,)), ((), ())), preferred_element_type=F32)


def kernel(
    S,
    E,
    residual,
    kept_index,
    kept_count,
    projected,
    expert_ids,
    gate_values,
    gate_w,
    up_w,
    down_w,
    cotangent,
    output,
    input_grad,
    projected_grad,
    gate_grads,
    kv_send,
    kv,
    q_send,
    q_recv,
    a_send,
    a_recv,
    g_send,
    g_recv,
    b_send,
    b_recv,
    x_send,
    x_recv,
    gu,
    dn,
    bias,
    k_t,
    v_t,
    prob,
    att_t,
    acc,
    other,
    kv_ss,
    q_ss,
    g_ss,
    a_rs,
    b_rs,
    kv_rs,
    q_rs,
    g_rs,
    a_ss,
    b_ss,
    x_ss,
    x_rs,
    swap_ss,
    swap_rs,
    gu_rs,
    dn_rs,
    ring_ss,
    pair_ss,
    core_ss,
    init_ss,
):
    Z = S // X
    KEEP = kept_index.shape[1]
    TOK, D = residual.shape
    FF = gate_w.shape[1]
    HEADS = D // HS
    PR = KEEP // 2
    NB = S // QSRC
    KB = QSRC * KEEP
    QB = QSRC * PR
    NS = E * SLOT
    scale = HS**-0.5
    me = lax.axis_index("seq")
    ex = lax.axis_index("exp")
    mx = me // Z
    mz = lax.rem(me, Z)
    yy = ex // 2
    core = lax.rem(ex, 2)
    sib = 1 - core
    grp = mx // 2
    mirror = X - 1 - mx
    partner = 4 * grp + 1 - mx
    head = me // 2
    par = lax.rem(me, 2)
    expert = 2 * yy + grp

    barrier = pltpu.get_barrier_semaphore()

    def greet(seq, exp):
        pl.semaphore_signal(
            barrier, inc=1, device_id={"seq": seq, "exp": exp}, device_id_type=MESH
        )

    def greet_plane(k, t):
        i = lax.rem(2 * me + core + k, 2 * S)
        greet(i // 2, 2 * yy + lax.rem(i, 2))
        return t

    def greet_others(k, t):
        e = lax.rem(2 * yy + 2 + k, E)
        greet(me, e)
        greet(mirror * Z + mz, e)
        return t

    lax.fori_loop(1, 2 * S, greet_plane, 0)
    lax.fori_loop(0, E - 2, greet_others, 0)

    count = kept_count[...]
    live_col = lax.broadcasted_iota(jnp.int32, (KEEP, 1), 0) < count
    for h in range(HEADS):
        c0 = h * HS
        keys = projected[:, D + c0 : D + c0 + HS].astype(F32)
        kv_send[0, h] = jnp.where(live_col, keys, MARK).astype(BF16)
        kv_send[1, h] = projected[:, 2 * D + c0 : 2 * D + c0 + HS]
        for p in range(2):
            q_send[p, h] = projected[p * PR : (p + 1) * PR, c0 : c0 + HS]

    @pl.when(par == core)
    def _():
        kv[core, me] = kv_send[core, head]
        q_recv[me] = q_send[core, head]

    origin = mx + core * (X - 1 - 2 * mx)
    origin_p = partner + core * (X - 1 - 2 * partner)
    other_o = mx + sib * (X - 1 - 2 * mx)
    other_p = partner + sib * (X - 1 - 2 * partner)

    @pl.when((core == 0) & (grp == 0))
    def _():
        gu[mx, mz, 0] = gate_w[...]
        gu[mx, mz, 1] = up_w[...]
        dn[mx, mz] = down_w[...]

    pl.semaphore_wait(barrier, 2 * S - 1 + 2 * (E - 2))

    def remote(src, dst, ss, rs, seq, exp):
        return pltpu.make_async_remote_copy(
            src_ref=src,
            dst_ref=dst,
            send_sem=ss,
            recv_sem=rs,
            device_id={"seq": seq, "exp": exp},
            device_id_type=MESH,
        )

    def kv_copy(h, p):
        return remote(
            kv_send.at[p, h], kv.at[p, me], kv_ss.at[p, h], kv_rs.at[me], 2 * h + core, 2 * yy + p
        )

    def head_copy(send, recv, ss, rs, h, p):
        return remote(
            send.at[p, h], recv.at[me], ss.at[p, h], rs.at[me], 2 * h + core, 2 * yy + p
        )

    def each_head(do):
        def step(k, t):
            i = lax.rem(k + 2 * head, 2 * HEADS)
            h, p = i // 2, lax.rem(i, 2)

            @pl.when((2 * h + core != me) | (p != core))
            def _():
                do(h, p)

            return t

        lax.fori_loop(0, 2 * HEADS, step, 0)

    def each_source(do, first=0, n=S):
        def step(k, t):
            d = first + lax.rem(me + k, n)

            @pl.when((d != me) | (par != core))
            def _():
                do(d)

            return t

        lax.fori_loop(0, n, step, 0)

    def source_copy(send, recv, ss, rs, d):
        return remote(
            send.at[d], recv.at[core, head], ss.at[d], rs.at[core, head], d, 2 * yy + par
        )

    def wait_kv(d):
        view = kv.at[core, d]
        remote(view, view, kv_ss.at[0, 0], kv_rs.at[d], d, 2 * yy + par).wait_recv()

    def wait_source(recv, ss, rs, d):
        view = recv.at[d]
        remote(view, view, ss.at[0, 0], rs.at[d], d, 2 * yy + par).wait_recv()

    def wait_head(recv, ss, rs, h, p):
        view = recv.at[p, h]
        remote(view, view, ss.at[0], rs.at[p, h], 2 * h + core, 2 * yy + p).wait_recv()

    def expert_at(e):
        cross = (lax.rem(e, 2) - grp) * (lax.rem(e, 2) - grp)
        seq = (mx + cross * (X - 1 - 2 * mx)) * Z + mz
        return seq, 2 * (e // 2) + cross

    def to_expert(n, e):
        seq, exp = expert_at(e)
        return remote(
            x_send.at[n, e], x_recv.at[n, ex], x_ss.at[n, e], x_rs.at[n, ex], seq, exp
        )

    def to_list(n, b):
        return remote(
            x_send.at[n, b],
            x_recv.at[n, expert],
            x_ss.at[n, b],
            x_rs.at[n, expert],
            origin * Z + mz,
            b,
        )

    def wait_x(n, i, seq, exp):
        view = x_recv.at[n, i]
        remote(view, view, x_ss.at[n, i], x_rs.at[n, i], seq, exp).wait_recv()

    def each_expert(do):
        def step(k, t):
            e = lax.rem(ex + k, E)

            @pl.when((e != expert) | (core != 0))
            def _():
                do(e)

            return t

        lax.fori_loop(0, E, step, 0)

    def each_list(do):
        def step(k, t):
            b = lax.rem(ex + k, E)

            @pl.when((b != ex) | (core != 0))
            def _():
                do(b)

            return t

        lax.fori_loop(0, E, step, 0)

    def out_start(n):
        @pl.when(core == 0)
        def _():
            x_recv[n, ex] = x_send[n, expert]

        each_expert(lambda e: to_expert(n, e).start())

    def back_start(n):
        @pl.when(core == 0)
        def _():
            x_recv[n, expert] = x_send[n, ex]

        each_list(lambda b: to_list(n, b).start())

    def out_recv(n):
        each_list(lambda b: wait_x(n, b, origin * Z + mz, b))

    def back_recv(n):
        each_expert(lambda e: wait_x(n, e, *expert_at(e)))

    sent = []

    def at_z(o):
        return lax.rem(mz + o + Z, Z)

    def piece(ref, sems, w, oz, half, seq, exp, ss):
        ax, az = (origin_p if w else origin), at_z(oz)
        view = ref.at[ax, az] if half is None else ref.at[ax, az, half]
        return remote(view, view, ss, sems.at[ax, az, half or 0], seq, exp)

    def send(*args):
        copy = piece(*args)
        copy.start()
        sent.append(copy)

    def wait(ref, sems, w, oz, halves):
        for half in (0, 1) if halves else (None,):
            piece(ref, sems, w, oz, half, me, 2 * yy + sib, init_ss.at[0]).wait_recv()

    kinds = ((gu, gu_rs), (dn, dn_rs))
    both = (1, -1)

    def hop(i, w, sgn, k):
        if k < Z // 2:
            half = None if k < Z // 2 - 1 else (0 if sgn > 0 else 1)
            ss = ring_ss.at[i, w, 0 if sgn > 0 else 1, k]
            send(*kinds[i], w, -sgn * k, half, mx * Z + at_z(sgn), ex, ss)

    def to_pair(i, oz):
        send(*kinds[i], 0, oz, None, partner * Z + mz, ex, pair_ss.at[i, oz % Z])

    def to_core(i, w, oz):
        send(*kinds[i], w, oz, None, me, 2 * yy + sib, core_ss.at[i, w, oz % Z])

    def along_z(i, w, k):
        if k == Z // 2:
            wait(*kinds[i], w, k, True)
            if i == 0:
                to_pair(i, k)
            to_core(i, w, k)
            return
        for s in both:
            wait(*kinds[i], w, -s * k, False)
            hop(i, w, s, k)
            if i == 0:
                to_pair(i, -s * k)
            to_core(i, w, -s * k)

    def from_pair(i, oz):
        wait(*kinds[i], 1, oz, False)
        to_core(i, 1, oz)

    def init_copies(seq, exp):
        return (
            remote(gate_w, gu.at[mx, mz, 0], init_ss.at[0], gu_rs.at[mx, mz, 0], seq, exp),
            remote(up_w, gu.at[mx, mz, 1], init_ss.at[1], gu_rs.at[mx, mz, 1], seq, exp),
            remote(down_w, dn.at[mx, mz], init_ss.at[2], dn_rs.at[mx, mz, 0], seq, exp),
        )

    @pl.when(core != grp)
    def _():
        for copy in init_copies(mirror * Z + mz, 2 * yy + 1):
            copy.start()

    @pl.when((core == 1) & (grp == 1))
    def _():
        for copy in init_copies(me, 2 * yy):
            copy.start()

    each_head(lambda h, p: kv_copy(h, p).start())
    each_head(lambda h, p: head_copy(q_send, q_recv, q_ss, q_rs, h, p).start())

    @pl.when((core == 1) | (grp == 1))
    def _():
        wait(gu, gu_rs, 0, 0, True)
        wait(dn, dn_rs, 0, 0, False)

    for s in both:
        hop(0, 0, s, 0)
    to_pair(1, 0)
    to_pair(0, 0)
    for i in (0, 1):
        to_core(i, 0, 0)

    slot_row = lax.broadcasted_iota(jnp.int32, (NS, KEEP), 0)
    slot_exp = slot_row // SLOT
    slot_pos = slot_row - slot_exp * SLOT
    entry = lax.broadcasted_iota(jnp.int32, (NS, KEEP), 1)
    live = entry < count
    assigned = jnp.zeros((NS, KEEP), F32)
    weight = jnp.zeros((NS, KEEP), F32)
    for k in range(expert_ids.shape[0]):
        match = (expert_ids[k : k + 1, :] == slot_exp) & live
        assigned = assigned + jnp.where(match, 1.0, 0.0)
        weight = weight + jnp.where(match, gate_values[k : k + 1, :], 0.0)
    ei = lax.broadcasted_iota(jnp.int32, (KEEP, KEEP), 0)
    ej = lax.broadcasted_iota(jnp.int32, (KEEP, KEEP), 1)
    earlier = jnp.where(ei < ej, 1.0, 0.0).astype(BF16)
    rank = nn(assigned.astype(BF16), earlier)
    table = jnp.where((assigned > 0.5) & (rank == slot_pos.astype(F32)), 1.0, 0.0)
    table_half = table.astype(BF16)
    weighted = table * weight
    slot_gate = jnp.sum(weighted, axis=1, keepdims=True)

    def turned(a):
        if a.shape[1] < 128:
            a = jnp.concatenate([a, jnp.zeros((a.shape[0], 128 - a.shape[1]), F32)], 1)
        return a.T

    table_t = turned(table)[:KEEP].astype(BF16)
    weighted_t = turned(weighted)[:KEEP]
    w_high = weighted_t.astype(BF16)
    w_low = (weighted_t - w_high.astype(F32)).astype(BF16)

    index_row = kept_index[...]
    index_col = jnp.sum(jnp.where(ei == ej, index_row, 0), axis=1, keepdims=True)
    pick = jnp.where(
        lax.broadcasted_iota(jnp.int32, (KEEP, TOK), 1) == index_col, 1.0, 0.0
    ).astype(BF16)
    grad_f = nn(pick, cotangent[...])
    kept_f = nn(pick, residual[...])
    grad_sel = nn(table_half, grad_f.astype(BF16))
    x_send[0] = (slot_gate * grad_sel).astype(BF16).reshape(E, SLOT, D)
    grad_sel = grad_sel.astype(BF16)
    out_start(0)

    along_z(0, 0, 1)
    from_pair(1, 0)
    for w in (0, 1):
        for s in both:
            hop(1, w, s, 0)
    along_z(0, 0, 2)

    def swap_copy(b):
        view = kv.at[core, pl.ds(b * QSRC, QSRC)]
        return remote(view, view, swap_ss.at[0, b], swap_rs.at[0, b], me, 2 * yy + sib)

    def swap_wait(b):
        view = kv.at[sib, pl.ds(b * QSRC, QSRC)]
        remote(view, view, swap_ss.at[0, b], swap_rs.at[0, b], me, 2 * yy + sib).wait_recv()

    for b in range(NB):
        each_source(wait_kv, b * QSRC, QSRC)
        swap_copy(b).start()
    each_source(lambda d: wait_source(q_recv, q_ss, q_rs, d))
    for b in range(NB):
        swap_wait(b)

    def key_block(c):
        return kv[0, c * QSRC : (c + 1) * QSRC].reshape(KB, HS)

    def value_block(c):
        return kv[1, c * QSRC : (c + 1) * QSRC].reshape(KB, HS)

    def query_block(b):
        return q_recv[b * QSRC : (b + 1) * QSRC].reshape(QB, HS)

    for b in range(NB):
        k_f = key_block(b).astype(F32)
        bias[b * KB : (b + 1) * KB] = jnp.where(k_f > MARK / 2, NEG, 0.0)
        k_t[:, b * KB : (b + 1) * KB] = k_f.T.astype(BF16)
        v_t[:, b * KB : (b + 1) * KB] = value_block(b).astype(F32).T.astype(BF16)

    qcol = lax.broadcasted_iota(jnp.int32, (KB, QB), 1)
    qent = (qcol // PR) * KEEP + core * PR + lax.rem(qcol, PR)
    causal = lax.broadcasted_iota(jnp.int32, (KB, QB), 0) <= qent

    def forward_block(b):
        cols = slice(b * QB, (b + 1) * QB)
        q_blk = query_block(b)
        top = None
        for c in range(b + 1):
            rows = slice(c * KB, (c + 1) * KB)
            half = bias[rows, :]
            sc = nt(key_block(c), q_blk) * scale + jnp.concatenate([half] * (QB // HS), 1)
            if c == b:
                sc = jnp.where(causal, sc, NEG)
            prob[rows, cols] = sc
            m = jnp.max(sc, axis=0, keepdims=True)
            top = m if top is None else jnp.maximum(top, m)
        total = jnp.zeros((1, QB), F32)
        for c in range(b + 1):
            rows = slice(c * KB, (c + 1) * KB)
            e = jnp.exp(prob[rows, cols] - top)
            prob[rows, cols] = e
            total = total + jnp.sum(e, axis=0, keepdims=True)
        inv = 1.0 / total
        out = jnp.zeros((HS, QB), F32)
        for c in range(b + 1):
            rows = slice(c * KB, (c + 1) * KB)
            pr = prob[rows, cols] * inv
            prob[rows, cols] = pr
            out = out + nn(v_t[:, rows], pr.astype(BF16))
        att_t[:, cols] = out
        a_send[b * QSRC : (b + 1) * QSRC] = out.T.astype(BF16).reshape(QSRC, PR, HS)
        each_source(
            lambda d: source_copy(a_send, a_recv, a_ss, a_rs, d).start(), b * QSRC, QSRC
        )

    for b in range(NB):
        forward_block(b)

    @pl.when(par == core)
    def _():
        a_recv[core, head] = a_send[me]

    along_z(0, 0, 3)
    from_pair(0, 0)
    along_z(1, 0, 1)
    along_z(1, 1, 1)
    each_head(lambda h, p: wait_head(a_recv, a_ss, a_rs, h, p))

    attended = jnp.concatenate(
        [jnp.concatenate([a_recv[p, h] for h in range(HEADS)], 1) for p in range(2)], 0
    )
    h1 = jnp.where(live_col, kept_f + attended.astype(F32), 0.0)
    inv_rms = lax.rsqrt(jnp.mean(h1 * h1, axis=1, keepdims=True) + EPSILON)
    normed = (h1 * inv_rms).astype(BF16)
    x_send[1] = nn(table_half, normed).astype(BF16).reshape(E, SLOT, D)
    out_start(1)
    along_z(0, 0, Z // 2)
    for k in range(2, Z // 2 + 1):
        for s in both:
            from_pair(0, s * (k - 1))
        for w in (0, 1):
            along_z(1, w, k)
    from_pair(0, Z // 2)
    out_recv(0)
    out_recv(1)
    for ax in (other_o, other_p):
        for az in range(Z):
            for ref, sems in kinds:
                view = ref.at[ax, az]
                remote(
                    view, view, init_ss.at[0], sems.at[ax, az, 0], me, 2 * yy + sib
                ).wait_recv()

    rows_in = x_recv[1].reshape(NS, D)
    grads_in = x_recv[0].reshape(NS, D)
    KC = Z * KEEP
    gate_pre = jnp.zeros((NS, FF), F32)
    up_pre = jnp.zeros((NS, FF), F32)
    mid_grad = jnp.zeros((NS, FF), F32)
    for c in range(X):
        r = rows_in[:, c * KC : (c + 1) * KC]
        gate_pre = gate_pre + nn(r, gu[c, :, 0].reshape(KC, FF))
        up_pre = up_pre + nn(r, gu[c, :, 1].reshape(KC, FF))
        mid_grad = mid_grad + nn(grads_in[:, c * KC : (c + 1) * KC], dn[c].reshape(KC, FF))
    sig = 1.0 / (1.0 + jnp.exp(-gate_pre))
    act = gate_pre * sig
    gate_grad = (mid_grad * up_pre * sig * (1.0 + gate_pre * (1.0 - sig))).astype(BF16)
    up_grad = (mid_grad * act).astype(BF16)
    mid = (act * up_pre).astype(BF16)
    for c in range(X):
        back = nt(gate_grad, gu[c, :, 0].reshape(KC, FF)) + nt(
            up_grad, gu[c, :, 1].reshape(KC, FF)
        )
        x_send[2, :, :, c * KC : (c + 1) * KC] = back.astype(BF16).reshape(E, SLOT, KC)
    back_start(2)
    for c in range(X):
        made = nt(mid, dn[c].reshape(KC, FF))
        x_send[3, :, :, c * KC : (c + 1) * KC] = made.astype(BF16).reshape(E, SLOT, KC)
    back_start(3)
    back_recv(2)
    normed_grad = nn(table_t, x_recv[2].reshape(NS, D))
    cubed = inv_rms * inv_rms * inv_rms
    h1_grad = (
        grad_f
        + inv_rms * normed_grad
        - h1 * cubed * jnp.mean(normed_grad * h1, axis=1, keepdims=True)
    )
    h1_grad = jnp.where(live_col, h1_grad, 0.0).astype(BF16)
    for h in range(HEADS):
        for p in range(2):
            g_send[p, h] = h1_grad[p * PR : (p + 1) * PR, h * HS : (h + 1) * HS]

    @pl.when(par == core)
    def _():
        g_recv[me] = g_send[core, head]

    each_head(lambda h, p: head_copy(g_send, g_recv, g_ss, g_rs, h, p).start())

    token = lax.broadcasted_iota(jnp.int32, (TOK, KEEP), 0)
    put = jnp.where(
        (token == index_row) & (lax.broadcasted_iota(jnp.int32, (TOK, KEEP), 1) < count),
        1.0,
        0.0,
    )
    replaced = jnp.sum(put, axis=1, keepdims=True) > 0.5
    put = put.astype(BF16)
    input_grad[...] = jnp.where(replaced, nn(put, h1_grad), cotangent[...].astype(F32)).astype(
        BF16
    )
    back_recv(3)
    results = x_recv[3].reshape(NS, D)
    mixture = nn(w_high, results) + nn(w_low, results)
    new_rows = (h1 + mixture).astype(BF16)
    output[...] = jnp.where(replaced, nn(put, new_rows), residual[...].astype(F32)).astype(BF16)
    per_slot = jnp.sum(results.astype(F32) * grad_sel.astype(F32), axis=1, keepdims=True)
    spread = table * per_slot
    for k in range(expert_ids.shape[0]):
        hit = expert_ids[k : k + 1, :] == slot_exp
        gate_grads[k : k + 1, :] = jnp.sum(jnp.where(hit, spread, 0.0), axis=0, keepdims=True)

    each_source(lambda d: wait_source(g_recv, g_ss, g_rs, d))
    acc[...] = jnp.zeros_like(acc)

    def give_copy(b):
        rows = pl.ds(b * KB, KB)
        return remote(
            acc.at[sib, rows],
            other.at[rows],
            swap_ss.at[1, b],
            swap_rs.at[1, b],
            me,
            2 * yy + sib,
        )

    def finish_block(b):
        give_copy(b).wait_recv()
        rows = slice(b * KB, (b + 1) * KB)
        src = slice(b * QSRC, (b + 1) * QSRC)
        whole = acc[core, rows] + other[rows]
        b_send[src, 0:KEEP] = whole.astype(BF16).reshape(QSRC, KEEP, HS)
        each_source(
            lambda d: source_copy(b_send, b_recv, b_ss, b_rs, d).start(), b * QSRC, QSRC
        )

    for b in reversed(range(NB)):
        cols = slice(b * QB, (b + 1) * QB)
        q_blk = query_block(b)
        dout = g_recv[b * QSRC : (b + 1) * QSRC].reshape(QB, HS)
        delta = jnp.sum(dout.astype(F32).T * att_t[:, cols], axis=0, keepdims=True)
        dq_t = jnp.zeros((HS, QB), F32)
        for c in range(b + 1):
            rows = slice(c * KB, (c + 1) * KB)
            pr = prob[rows, cols]
            ds = (pr * (nt(value_block(c), dout) - delta) * scale).astype(BF16)
            dq_t = dq_t + nn(k_t[:, rows], ds)
            acc[0, rows] += nn(ds, q_blk)
            acc[1, rows] += nn(pr.astype(BF16), dout)
        b_send[b * QSRC : (b + 1) * QSRC, KEEP:] = dq_t.T.astype(BF16).reshape(QSRC, PR, HS)
        give_copy(b).start()
        if b < NB - 1:
            finish_block(b + 1)
    finish_block(0)

    @pl.when(par == core)
    def _():
        b_recv[core, head] = b_send[me]

    each_head(lambda h, p: wait_head(b_recv, b_ss, b_rs, h, p))
    for h in range(HEADS):
        c0 = h * HS
        for p in range(2):
            projected_grad[p * PR : (p + 1) * PR, c0 : c0 + HS] = b_recv[p, h, KEEP:]
            o = (1 + p) * D + c0
            projected_grad[:, o : o + HS] = b_recv[p, h, 0:KEEP]

    each_head(lambda h, p: kv_copy(h, p).wait_send())
    each_head(lambda h, p: head_copy(q_send, q_recv, q_ss, q_rs, h, p).wait_send())
    each_head(lambda h, p: head_copy(g_send, g_recv, g_ss, g_rs, h, p).wait_send())
    each_source(lambda d: source_copy(a_send, a_recv, a_ss, a_rs, d).wait_send())
    each_source(lambda d: source_copy(b_send, b_recv, b_ss, b_rs, d).wait_send())
    for n in (0, 1):
        each_expert(lambda e, n=n: to_expert(n, e).wait_send())
    for n in (2, 3):
        each_list(lambda b, n=n: to_list(n, b).wait_send())
    for b in range(NB):
        swap_copy(b).wait_send()
        give_copy(b).wait_send()

    @pl.when(core != grp)
    def _():
        for copy in init_copies(mirror * Z + mz, 2 * yy + 1):
            copy.wait_send()

    @pl.when((core == 1) & (grp == 1))
    def _():
        for copy in init_copies(me, 2 * yy):
            copy.wait_send()

    for copy in sent:
        copy.wait_send()


def body(
    residual,
    kept_index,
    kept_count,
    projected,
    expert_ids,
    gate_values,
    gate_weight,
    up_weight,
    down_weight,
    cotangent,
):
    S = lax.axis_size("seq")
    E = lax.axis_size("exp")
    _, TOK, D = residual.shape
    KEEP = kept_index.shape[1]
    FF = gate_weight.shape[2]
    TOPK = expert_ids.shape[2]
    Z = S // X
    HEADS = D // HS
    PR = KEEP // 2
    NB = S // QSRC
    vm = pl.BlockSpec(memory_space=pltpu.VMEM)
    dma = pltpu.SemaphoreType.DMA
    out = pl.pallas_call(
        functools.partial(kernel, S, E),
        out_shape=[
            jax.ShapeDtypeStruct((TOK, D), BF16),
            jax.ShapeDtypeStruct((TOK, D), BF16),
            jax.ShapeDtypeStruct((KEEP, 3 * D), BF16),
            jax.ShapeDtypeStruct((TOPK, KEEP), F32),
        ],
        in_specs=[vm] * 10,
        out_specs=[vm] * 4,
        scratch_shapes=[
            pltpu.VMEM((2, HEADS, KEEP, HS), BF16),
            pltpu.VMEM((2, S, KEEP, HS), BF16),
            pltpu.VMEM((2, HEADS, PR, HS), BF16),
            pltpu.VMEM((S, PR, HS), BF16),
            pltpu.VMEM((S, PR, HS), BF16),
            pltpu.VMEM((2, HEADS, PR, HS), BF16),
            pltpu.VMEM((2, HEADS, PR, HS), BF16),
            pltpu.VMEM((S, PR, HS), BF16),
            pltpu.VMEM((S, KEEP + PR, HS), BF16),
            pltpu.VMEM((2, HEADS, KEEP + PR, HS), BF16),
            pltpu.VMEM((4, E, SLOT, D), BF16),
            pltpu.VMEM((4, E, SLOT, D), BF16),
            pltpu.VMEM((X, Z, 2, KEEP, FF), BF16),
            pltpu.VMEM((X, Z, 2, KEEP // 2, FF), BF16),
            pltpu.VMEM((S * KEEP, HS), F32),
            pltpu.VMEM((HS, S * KEEP), BF16),
            pltpu.VMEM((HS, S * KEEP), BF16),
            pltpu.VMEM((S * KEEP, S * PR), F32),
            pltpu.VMEM((HS, S * PR), F32),
            pltpu.VMEM((2, S * KEEP, HS), F32),
            pltpu.VMEM((S * KEEP, HS), F32),
        ]
        + [dma((2, HEADS))] * 5
        + [dma((S,))] * 5
        + [dma((4, E))] * 2
        + [dma((2, NB))] * 2
        + [
            dma((X, Z, 2)),
            dma((X, Z, 2)),
            dma((2, 2, 2, Z // 2)),
            dma((2, Z)),
            dma((2, 2, Z)),
            dma((3,)),
        ],
        compiler_params=pltpu.CompilerParams(
            collective_id=0, has_side_effects=True, vmem_limit_bytes=60 * 1024 * 1024
        ),
    )(
        residual[0],
        kept_index,
        kept_count,
        projected[0],
        expert_ids[0].T,
        gate_values[0].T,
        gate_weight[0],
        up_weight[0],
        down_weight[0].T.reshape(2, KEEP // 2, FF),
        cotangent[0],
    )
    return (out[0][None], out[1][None], out[2][None], out[3].T[None])


def solution(mesh):
    row = P("exp", "seq", None)
    in_specs = (row, P("exp", "seq"), P("exp", "seq")) + (row,) * 5 + (P("exp", None, "seq"), row)
    return jax.shard_map(
        body, mesh=mesh, in_specs=in_specs, out_specs=(row,) * 4, check_vma=False
    )
```

```python
import functools

import jax
import jax.numpy as jnp
from jax import lax
from jax.experimental import pallas as pl
from jax.experimental.pallas import tpu as pltpu
from jax.sharding import PartitionSpec as P

HS = 128
SLOT = 16
EPSILON = 1e-06
X = 4
QSRC = 8
F32 = jnp.float32
BF16 = jnp.bfloat16
MESH = pl.DeviceIdType.MESH
NEG = -1e30
MARK = 1024.0


def nn(a, b):
    return lax.dot_general(a, b, (((1,), (0,)), ((), ())), preferred_element_type=F32)


def nt(a, b):
    return lax.dot_general(a, b, (((1,), (1,)), ((), ())), preferred_element_type=F32)


def kernel(
    S,
    E,
    residual_h,
    kept_index,
    kept_count,
    projected_h,
    expert_ids,
    gate_values,
    gate_w,
    up_w,
    down_w,
    cotangent_h,
    output_h,
    input_grad_h,
    projected_grad_h,
    gate_grads,
    residual,
    cotangent,
    projected,
    output,
    input_grad,
    projected_grad,
    io_sem,
    kv_send,
    kv,
    q_send,
    q_recv,
    a_send,
    a_recv,
    g_send,
    g_recv,
    b_send,
    b_recv,
    dq_send,
    dq_recv,
    x_send,
    x_recv,
    gu,
    dn,
    bias,
    k_t,
    v_t,
    prob,
    att_t,
    acc,
    other,
    send_ss,
    kv_rs,
    q_rs,
    a_rs,
    g_rs,
    b_rs,
    x_rs,
    rows_rs,
    swap_rs,
    gu_rs,
    dn_rs,
    core_rs,
    init_ss,
):
    Z = S // X
    KEEP = kept_index.shape[1]
    TOK, D = residual.shape
    FF = gate_w.shape[1]
    HEADS = D // HS
    PR = KEEP // 2
    NB = S // QSRC
    KB = QSRC * KEEP
    QB = QSRC * PR
    NS = E * SLOT
    scale = HS**-0.5
    me = lax.axis_index("seq")
    ex = lax.axis_index("exp")
    mx = me // Z
    mz = lax.rem(me, Z)
    yy = ex // 2
    core = lax.rem(ex, 2)
    sib = 1 - core
    grp = mx // 2
    mirror = X - 1 - mx
    partner = 4 * grp + 1 - mx
    head = me // 2
    par = lax.rem(me, 2)
    expert = 2 * yy + grp

    def load(i, src, dst):
        return pltpu.make_async_copy(src, dst, io_sem.at[i])

    projected_in = load(0, projected_h, projected)
    cotangent_in = load(1, cotangent_h, cotangent)
    residual_in = load(2, residual_h, residual)
    for copy in (projected_in, cotangent_in, residual_in):
        copy.start()

    def home_copies():
        return (
            load(3, gate_w, gu.at[mx, mz, 0]),
            load(4, up_w, gu.at[mx, mz, 1]),
            load(5, down_w, dn.at[mx, mz]),
        )

    @pl.when((core == 0) & (grp == 0))
    def _():
        for copy in home_copies():
            copy.start()

    barrier = pltpu.get_barrier_semaphore()

    def greet(seq, exp):
        pl.semaphore_signal(
            barrier, inc=1, device_id={"seq": seq, "exp": exp}, device_id_type=MESH
        )

    def greet_plane(k, t):
        i = lax.rem(2 * me + core + k, 2 * S)
        greet(i // 2, 2 * yy + lax.rem(i, 2))
        return t

    def greet_others(k, t):
        e = lax.rem(2 * yy + 2 + k, E)
        greet(me, e)
        greet(mirror * Z + mz, e)
        return t

    lax.fori_loop(1, 2 * S, greet_plane, 0)
    lax.fori_loop(0, E - 2, greet_others, 0)

    projected_in.wait()
    count = kept_count[...]
    live_col = lax.broadcasted_iota(jnp.int32, (KEEP, 1), 0) < count
    for h in range(HEADS):
        c0 = h * HS
        keys = projected[:, D + c0 : D + c0 + HS].astype(F32)
        kv_send[2 * h] = jnp.where(live_col, keys, MARK).astype(BF16)
        kv_send[2 * h + 1] = projected[:, 2 * D + c0 : 2 * D + c0 + HS]
        for p in range(2):
            q_send[2 * h + p] = projected[p * PR : (p + 1) * PR, c0 : c0 + HS]

    origin = mx + core * (X - 1 - 2 * mx)
    origin_p = partner + core * (X - 1 - 2 * partner)
    other_o = mx + sib * (X - 1 - 2 * mx)
    other_p = partner + sib * (X - 1 - 2 * partner)

    @pl.when((core == 0) & (grp == 0))
    def _():
        for copy in home_copies():
            copy.wait()

    slot_row = lax.broadcasted_iota(jnp.int32, (NS, KEEP), 0)
    slot_exp = slot_row // SLOT
    slot_pos = slot_row - slot_exp * SLOT
    entry = lax.broadcasted_iota(jnp.int32, (NS, KEEP), 1)
    live = entry < count
    assigned = jnp.zeros((NS, KEEP), F32)
    weight = jnp.zeros((NS, KEEP), F32)
    for k in range(expert_ids.shape[0]):
        match = (expert_ids[k] == slot_exp) & live
        assigned = assigned + jnp.where(match, 1.0, 0.0)
        weight = weight + jnp.where(match, gate_values[k], 0.0)
    ei = lax.broadcasted_iota(jnp.int32, (KEEP, KEEP), 0)
    ej = lax.broadcasted_iota(jnp.int32, (KEEP, KEEP), 1)
    earlier = jnp.where(ei < ej, 1.0, 0.0).astype(BF16)
    rank = nn(assigned.astype(BF16), earlier)
    table = jnp.where((assigned > 0.5) & (rank == slot_pos.astype(F32)), 1.0, 0.0)
    table_half = table.astype(BF16)
    weighted = table * weight
    slot_gate = jnp.sum(weighted, axis=1, keepdims=True)

    def turned(a):
        if a.shape[1] < 128:
            a = jnp.concatenate([a, jnp.zeros((a.shape[0], 128 - a.shape[1]), F32)], 1)
        return a.T

    table_t = turned(table)[:KEEP].astype(BF16)
    weighted_t = turned(weighted)[:KEEP]
    w_high = weighted_t.astype(BF16)
    w_low = (weighted_t - w_high.astype(F32)).astype(BF16)

    cotangent_in.wait()
    residual_in.wait()
    index_row = kept_index[...]
    index_col = jnp.sum(jnp.where(ei == ej, index_row, 0), axis=1, keepdims=True)
    pick = jnp.where(
        lax.broadcasted_iota(jnp.int32, (KEEP, TOK), 1) == index_col, 1.0, 0.0
    ).astype(BF16)
    grad_f = nn(pick, cotangent[...])
    kept_f = nn(pick, residual[...])
    grad_sel = nn(table_half, grad_f.astype(BF16))
    x_send[0] = (slot_gate * grad_sel).astype(BF16).reshape(E, SLOT, D)
    grad_sel = grad_sel.astype(BF16)
    pl.semaphore_wait(barrier, 2 * S - 1 + 2 * (E - 2))

    def remote(src, dst, ss, rs, seq, exp):
        return pltpu.make_async_remote_copy(
            src_ref=src,
            dst_ref=dst,
            send_sem=ss,
            recv_sem=rs,
            device_id={"seq": seq, "exp": exp},
            device_id_type=MESH,
        )

    def landed(view, sem):
        remote(view, view, init_ss.at[0], sem, me, 2 * yy + sib).wait_recv()

    def left(n, view):
        remote(view, view, send_ss.at[n], init_ss.at[0], me, 2 * yy + sib).wait_send()

    def left_all(n, ref):
        @pl.when(par == core)
        def _():
            left(n, ref.at[pl.ds(0, S - 1)])

        @pl.when(par != core)
        def _():
            left(n, ref)

    here = 2 * head + core

    def each_head(do):
        def step(k, t):
            i = lax.rem(k + 2 * head, S)

            @pl.when((2 * (i // 2) + core != me) | (lax.rem(i, 2) != core))
            def _():
                do(i)

            return t

        lax.fori_loop(0, S, step, 0)

    def each_source(do, first=0, n=S):
        def step(k, t):
            d = first + lax.rem(me + k, n)

            @pl.when((d != me) | (par != core))
            def _():
                do(d)

            return t

        lax.fori_loop(0, n, step, 0)

    def kv_copy(i):
        p = lax.rem(i, 2)
        return remote(
            kv_send.at[i],
            kv.at[p, me],
            send_ss.at[0],
            kv_rs.at[me // QSRC],
            2 * (i // 2) + core,
            2 * yy + p,
        )

    def head_copy(n, send, recv, rs, i):
        return remote(
            send.at[i],
            recv.at[me],
            send_ss.at[n],
            rs,
            2 * (i // 2) + core,
            2 * yy + lax.rem(i, 2),
        )

    def source_copy(n, send, recv, rs, d):
        return remote(send.at[d], recv.at[here], send_ss.at[n], rs, d, 2 * yy + par)

    def own_copy(src, dst, sem):
        @pl.when(par == core)
        def _():
            pltpu.make_async_copy(src, dst, sem).start()

    def expert_at(e):
        cross = (lax.rem(e, 2) - grp) * (lax.rem(e, 2) - grp)
        seq = (mx + cross * (X - 1 - 2 * mx)) * Z + mz
        return seq, 2 * (e // 2) + cross

    def to_expert(n, e):
        seq, exp = expert_at(e)
        return remote(
            x_send.at[n, e], x_recv.at[n, ex], send_ss.at[6 + n], x_rs.at[n], seq, exp
        )

    def to_list(n, b):
        return remote(
            x_send.at[n, b],
            x_recv.at[n, expert],
            send_ss.at[6 + n],
            x_rs.at[n],
            origin * Z + mz,
            b,
        )

    def each_expert(do):
        def step(k, t):
            e = lax.rem(ex + k, E)

            @pl.when((e != expert) | (core != 0))
            def _():
                do(e)

            return t

        lax.fori_loop(0, E, step, 0)

    def each_list(do):
        def step(k, t):
            b = lax.rem(ex + k, E)

            @pl.when((b != ex) | (core != 0))
            def _():
                do(b)

            return t

        lax.fori_loop(0, E, step, 0)

    def out_start(n):
        @pl.when(core == 0)
        def _():
            pltpu.make_async_copy(x_send.at[n, expert], x_recv.at[n, ex], x_rs.at[n]).start()

        each_expert(lambda e: to_expert(n, e).start())

    def back_start(n):
        @pl.when(core == 0)
        def _():
            pltpu.make_async_copy(x_send.at[n, ex], x_recv.at[n, expert], x_rs.at[n]).start()

        each_list(lambda b: to_list(n, b).start())

    def x_landed(n):
        landed(x_recv.at[n], x_rs.at[n])

    def x_left(n, i, cols):
        @pl.when(core == 0)
        def _():
            left(i, x_send.at[n, pl.ds(0, E - 1), :, cols])

        @pl.when(core != 0)
        def _():
            left(i, x_send.at[n, :, :, cols])

    def part_cols(c):
        return pl.ds(c * Z * KEEP, Z * KEEP)

    def rows_copy(c, b):
        cols = part_cols(c)
        return remote(
            x_send.at[2, b, :, cols],
            x_recv.at[2, expert, :, cols],
            send_ss.at[10 + c],
            rows_rs.at[c],
            origin * Z + mz,
            b,
        )

    def rows_start(c):
        cols = part_cols(c)

        @pl.when(core == 0)
        def _():
            pltpu.make_async_copy(
                x_send.at[2, ex, :, cols], x_recv.at[2, expert, :, cols], rows_rs.at[c]
            ).start()

        each_list(lambda b: rows_copy(c, b).start())

    def at_z(o):
        return lax.rem(mz + o + Z, Z)

    RING, PAIR, CORE = 14, 16, 18

    def piece(i, w, oz, half, group, seq, exp, sem):
        ref = kinds[i][0]
        ax, az = (origin_p if w else origin), at_z(oz)
        view = ref.at[ax, az] if half is None else ref.at[ax, az, half]
        return remote(view, view, send_ss.at[group + i], sem, seq, exp)

    def arrival(i, w, oz, half):
        return kinds[i][1].at[w, oz % Z if half != 1 else Z]

    def wait(i, w, oz, halves):
        for half in (0, 1) if halves else (None,):
            piece(i, w, oz, half, RING, me, 2 * yy + sib, arrival(i, w, oz, half)).wait_recv()

    kinds = ((gu, gu_rs), (dn, dn_rs))
    both = (1, -1)

    def hop(i, w, sgn, k):
        if k < Z // 2:
            half = None if k < Z // 2 - 1 else (0 if sgn > 0 else 1)
            sem = arrival(i, w, -sgn * (k + 1), half)
            piece(i, w, -sgn * k, half, RING, mx * Z + at_z(sgn), ex, sem).start()

    def to_pair(i, oz):
        piece(i, 0, oz, None, PAIR, partner * Z + mz, ex, arrival(i, 1, oz, None)).start()

    def to_core(i, w, oz):
        piece(i, w, oz, None, CORE, me, 2 * yy + sib, core_rs.at[i, w]).start()

    def along_z(i, w, k):
        if k == Z // 2:
            wait(i, w, k, True)
            if i == 0:
                to_pair(i, k)
            to_core(i, w, k)
            return
        for s in both:
            wait(i, w, -s * k, False)
            hop(i, w, s, k)
            if i == 0:
                to_pair(i, -s * k)
            to_core(i, w, -s * k)

    def from_pair(i, oz):
        wait(i, 1, oz, False)
        to_core(i, 1, oz)

    def init_copies(seq, exp):
        return (
            remote(gate_w, gu.at[mx, mz, 0], init_ss.at[0], gu_rs.at[0, 0], seq, exp),
            remote(up_w, gu.at[mx, mz, 1], init_ss.at[1], gu_rs.at[0, Z + 1], seq, exp),
            remote(down_w, dn.at[mx, mz], init_ss.at[2], dn_rs.at[0, 0], seq, exp),
        )

    @pl.when(core != grp)
    def _():
        for copy in init_copies(mirror * Z + mz, 2 * yy + 1):
            copy.start()

    @pl.when((core == 1) & (grp == 1))
    def _():
        for copy in init_copies(me, 2 * yy):
            copy.start()

    own_copy(kv_send.at[here], kv.at[core, me], kv_rs.at[me // QSRC])
    own_copy(q_send.at[here], q_recv.at[me], q_rs.at[0])
    each_head(lambda i: kv_copy(i).start())
    each_head(lambda i: head_copy(1, q_send, q_recv, q_rs.at[0], i).start())

    @pl.when((core == 1) | (grp == 1))
    def _():
        landed(gu.at[origin, mz, 0], gu_rs.at[0, 0])
        landed(gu.at[origin, mz, 1], gu_rs.at[0, Z + 1])
        landed(dn.at[origin, mz], dn_rs.at[0, 0])

    for s in both:
        hop(0, 0, s, 0)
    to_pair(1, 0)
    to_pair(0, 0)
    for i in (0, 1):
        to_core(i, 0, 0)

    out_start(0)

    along_z(0, 0, 1)
    along_z(0, 0, 2)

    def swap_copy(b):
        view = kv.at[core, pl.ds(b * QSRC, QSRC)]
        return remote(view, view, send_ss.at[20], swap_rs.at[0, b], me, 2 * yy + sib)

    for b in range(NB):
        landed(kv.at[core, pl.ds(b * QSRC, QSRC)], kv_rs.at[b])
        swap_copy(b).start()
    landed(q_recv, q_rs.at[0])
    for b in range(NB):
        landed(kv.at[sib, pl.ds(b * QSRC, QSRC)], swap_rs.at[0, b])

    def key_block(c):
        return kv[0, c * QSRC : (c + 1) * QSRC].reshape(KB, HS)

    def value_block(c):
        return kv[1, c * QSRC : (c + 1) * QSRC].reshape(KB, HS)

    def query_block(b):
        return q_recv[b * QSRC : (b + 1) * QSRC].reshape(QB, HS)

    for b in range(NB):
        k_f = key_block(b).astype(F32)
        bias[b * KB : (b + 1) * KB] = jnp.where(k_f > MARK / 2, NEG, 0.0)
        k_t[:, b * KB : (b + 1) * KB] = k_f.T.astype(BF16)
        v_t[:, b * KB : (b + 1) * KB] = value_block(b).astype(F32).T.astype(BF16)

    qcol = lax.broadcasted_iota(jnp.int32, (KB, QB), 1)
    qent = (qcol // PR) * KEEP + core * PR + lax.rem(qcol, PR)
    causal = lax.broadcasted_iota(jnp.int32, (KB, QB), 0) <= qent

    def forward_block(b):
        cols = slice(b * QB, (b + 1) * QB)
        q_blk = query_block(b)
        top = None
        for c in range(b + 1):
            rows = slice(c * KB, (c + 1) * KB)
            half = bias[rows, :]
            sc = nt(key_block(c), q_blk) * scale + jnp.concatenate([half] * (QB // HS), 1)
            if c == b:
                sc = jnp.where(causal, sc, NEG)
            prob[rows, cols] = sc
            m = jnp.max(sc, axis=0, keepdims=True)
            top = m if top is None else jnp.maximum(top, m)
        total = jnp.zeros((1, QB), F32)
        for c in range(b + 1):
            rows = slice(c * KB, (c + 1) * KB)
            e = jnp.exp(prob[rows, cols] - top)
            prob[rows, cols] = e
            total = total + jnp.sum(e, axis=0, keepdims=True)
        inv = 1.0 / total
        out = jnp.zeros((HS, QB), F32)
        for c in range(b + 1):
            rows = slice(c * KB, (c + 1) * KB)
            pr = prob[rows, cols] * inv
            prob[rows, cols] = pr
            out = out + nn(v_t[:, rows], pr.astype(BF16))
        att_t[:, cols] = out
        a_send[b * QSRC : (b + 1) * QSRC] = out.T.astype(BF16).reshape(QSRC, PR, HS)
        each_source(
            lambda d: source_copy(2, a_send, a_recv, a_rs.at[0], d).start(), b * QSRC, QSRC
        )

    for b in range(NB):
        forward_block(b)
        if b == 1:
            along_z(0, 0, 3)
            from_pair(1, 0)
            for w in (0, 1):
                for s in both:
                    hop(1, w, s, 0)

    own_copy(a_send.at[me], a_recv.at[here], a_rs.at[0])
    along_z(0, 0, Z // 2)
    for w in (0, 1):
        along_z(1, w, 1)
    from_pair(0, 0)
    for w in (0, 1):
        along_z(1, w, 2)
    landed(a_recv, a_rs.at[0])

    attended = jnp.concatenate(
        [jnp.concatenate([a_recv[2 * h + p] for h in range(HEADS)], 1) for p in range(2)], 0
    )
    h1 = jnp.where(live_col, kept_f + attended.astype(F32), 0.0)
    inv_rms = lax.rsqrt(jnp.mean(h1 * h1, axis=1, keepdims=True) + EPSILON)
    normed = (h1 * inv_rms).astype(BF16)
    x_send[1] = nn(table_half, normed).astype(BF16).reshape(E, SLOT, D)
    out_start(1)
    for o in (1, -1):
        from_pair(0, o)
    for w in (0, 1):
        along_z(1, w, 3)
    for o in (2, -2):
        from_pair(0, o)
    for w in (0, 1):
        along_z(1, w, Z // 2)
    x_landed(0)
    x_landed(1)

    KC = Z * KEEP
    pre = [jnp.zeros((NS, FF), F32)] * 3

    def expert_chunk(ax):
        cols = pl.ds(pl.multiple_of(ax * KC, KC), KC)
        r = x_recv[1, :, :, cols].reshape(NS, KC)
        g = x_recv[0, :, :, cols].reshape(NS, KC)
        pre[0] = pre[0] + nn(r, gu[ax, :, 0].reshape(KC, FF))
        pre[1] = pre[1] + nn(r, gu[ax, :, 1].reshape(KC, FF))
        pre[2] = pre[2] + nn(g, dn[ax].reshape(KC, FF))

    def core_landed(w, ax):
        for i, (ref, _) in enumerate(kinds):
            landed(ref.at[ax], core_rs.at[i, w])

    expert_chunk(origin)
    for o in (3, -3, Z // 2):
        from_pair(0, o)
    core_landed(0, other_o)
    expert_chunk(other_o)
    expert_chunk(origin_p)
    core_landed(1, other_p)
    expert_chunk(other_p)
    gate_pre, up_pre, mid_grad = pre
    sig = 1.0 / (1.0 + jnp.exp(-gate_pre))
    act = gate_pre * sig
    gate_grad = (mid_grad * up_pre * sig * (1.0 + gate_pre * (1.0 - sig))).astype(BF16)
    up_grad = (mid_grad * act).astype(BF16)
    mid = (act * up_pre).astype(BF16)
    for c in range(X):
        back = nt(gate_grad, gu[c, :, 0].reshape(KC, FF)) + nt(
            up_grad, gu[c, :, 1].reshape(KC, FF)
        )
        x_send[2, :, :, c * KC : (c + 1) * KC] = back.astype(BF16).reshape(E, SLOT, KC)
        rows_start(c)
    for c in range(X):
        made = nt(mid, dn[c].reshape(KC, FF))
        x_send[3, :, :, c * KC : (c + 1) * KC] = made.astype(BF16).reshape(E, SLOT, KC)
    parts = []
    for c in range(X):
        landed(x_recv.at[2, :, :, part_cols(c)], rows_rs.at[c])
        parts.append(nn(table_t, x_recv[2, :, :, c * KC : (c + 1) * KC].reshape(NS, KC)))
    normed_grad = jnp.concatenate(parts, 1)
    cubed = inv_rms * inv_rms * inv_rms
    h1_grad = (
        grad_f
        + inv_rms * normed_grad
        - h1 * cubed * jnp.mean(normed_grad * h1, axis=1, keepdims=True)
    )
    h1_grad = jnp.where(live_col, h1_grad, 0.0).astype(BF16)
    for h in range(HEADS):
        for p in range(2):
            g_send[2 * h + p] = h1_grad[p * PR : (p + 1) * PR, h * HS : (h + 1) * HS]
    own_copy(g_send.at[here], g_recv.at[me], g_rs.at[me // QSRC])
    each_head(lambda i: head_copy(3, g_send, g_recv, g_rs.at[me // QSRC], i).start())

    token = lax.broadcasted_iota(jnp.int32, (TOK, KEEP), 0)
    put = jnp.where(
        (token == index_row) & (lax.broadcasted_iota(jnp.int32, (TOK, KEEP), 1) < count),
        1.0,
        0.0,
    )
    replaced = jnp.sum(put, axis=1, keepdims=True) > 0.5
    put = put.astype(BF16)
    input_grad[...] = jnp.where(replaced, nn(put, h1_grad), cotangent[...].astype(F32)).astype(
        BF16
    )
    input_grad_out = load(0, input_grad, input_grad_h)
    input_grad_out.start()
    back_start(3)

    def give_copy(c):
        rows = pl.ds(c * KB, KB)
        return remote(
            acc.at[sib, rows],
            other.at[rows],
            send_ss.at[21],
            swap_rs.at[1, c],
            me,
            2 * yy + sib,
        )

    def finish_block(c):
        rows = slice(c * KB, (c + 1) * KB)
        landed(other.at[pl.ds(c * KB, KB)], swap_rs.at[1, c])
        whole = acc[core, rows] + other[rows]
        b_send[c * QSRC : (c + 1) * QSRC] = whole.astype(BF16).reshape(QSRC, KEEP, HS)
        each_source(
            lambda d: source_copy(4, b_send, b_recv, b_rs.at[0], d).start(), c * QSRC, QSRC
        )

    dout = [None] * NB
    delta = [None] * NB
    dq_t = [jnp.zeros((HS, QB), F32)] * NB
    for c in reversed(range(NB)):
        rows = slice(c * KB, (c + 1) * KB)
        block = pl.ds(c * QSRC, QSRC)
        landed(g_recv.at[block], g_rs.at[c])
        dout[c] = g_recv[c * QSRC : (c + 1) * QSRC].reshape(QB, HS)
        turn = dout[c].astype(F32).T * att_t[:, c * QB : (c + 1) * QB]
        delta[c] = jnp.sum(turn, axis=0, keepdims=True)
        dk = jnp.zeros((KB, HS), F32)
        dv = jnp.zeros((KB, HS), F32)
        for b in range(c, NB):
            pr = prob[rows, b * QB : (b + 1) * QB]
            ds = (pr * (nt(value_block(c), dout[b]) - delta[b]) * scale).astype(BF16)
            dq_t[b] = dq_t[b] + nn(k_t[:, rows], ds)
            dk = dk + nn(ds, query_block(b))
            dv = dv + nn(pr.astype(BF16), dout[b])
        acc[0, rows] = dk
        acc[1, rows] = dv
        give_copy(c).start()
        if c < NB - 1:
            finish_block(c + 1)
    for b in range(NB):
        dq_send[b * QSRC : (b + 1) * QSRC] = dq_t[b].T.astype(BF16).reshape(QSRC, PR, HS)
    each_source(lambda d: source_copy(5, dq_send, dq_recv, b_rs.at[1], d).start())
    finish_block(0)
    own_copy(dq_send.at[me], dq_recv.at[here], b_rs.at[1])
    own_copy(b_send.at[me], b_recv.at[here], b_rs.at[0])

    x_landed(3)
    results = x_recv[3].reshape(NS, D)
    mixture = nn(w_high, results) + nn(w_low, results)
    new_rows = (h1 + mixture).astype(BF16)
    output[...] = jnp.where(replaced, nn(put, new_rows), residual[...].astype(F32)).astype(BF16)
    per_slot = jnp.sum(results.astype(F32) * grad_sel.astype(F32), axis=1, keepdims=True)
    spread = table * per_slot
    for k in range(expert_ids.shape[0]):
        hit = expert_ids[k] == slot_exp
        gate_grads[k] = jnp.sum(jnp.where(hit, spread, 0.0), axis=0, keepdims=True)
    output_out = load(1, output, output_h)
    output_out.start()
    left_all(0, kv_send)
    left_all(1, q_send)
    left_all(2, a_send)
    left_all(3, g_send)
    for n in (0, 1, 3):
        x_left(n, 6 + n, pl.ds(0, D))
    for c in range(X):
        x_left(2, 10 + c, part_cols(c))
    for i, (ref, _) in enumerate(kinds):
        if i == 0:
            left(RING + i, ref.at[0, pl.ds(0, Z - 1)])
            left(PAIR + i, ref.at[0])
        else:
            left(RING + i, ref.at[pl.ds(0, 2), pl.ds(0, Z - 1)])
            left(PAIR + i, ref.at[0, 0])
        left(CORE + i, ref.at[pl.ds(0, 2)])
    left(20, kv.at[core])
    left(21, acc.at[sib])

    @pl.when(core != grp)
    def _():
        for copy in init_copies(mirror * Z + mz, 2 * yy + 1):
            copy.wait_send()

    @pl.when((core == 1) & (grp == 1))
    def _():
        for copy in init_copies(me, 2 * yy):
            copy.wait_send()

    landed(b_recv, b_rs.at[0])
    landed(dq_recv, b_rs.at[1])
    for h in range(HEADS):
        c0 = h * HS
        for p in range(2):
            projected_grad[p * PR : (p + 1) * PR, c0 : c0 + HS] = dq_recv[2 * h + p]
            o = (1 + p) * D + c0
            projected_grad[:, o : o + HS] = b_recv[2 * h + p]
    projected_grad_out = load(2, projected_grad, projected_grad_h)
    projected_grad_out.start()
    left_all(4, b_send)
    left_all(5, dq_send)
    for copy in (input_grad_out, output_out, projected_grad_out):
        copy.wait()


def body(
    residual,
    kept_index,
    kept_count,
    projected,
    expert_ids,
    gate_values,
    gate_weight,
    up_weight,
    down_weight,
    cotangent,
):
    S = lax.axis_size("seq")
    E = lax.axis_size("exp")
    _, TOK, D = residual.shape
    KEEP = kept_index.shape[1]
    FF = gate_weight.shape[2]
    TOPK = expert_ids.shape[2]
    Z = S // X
    HEADS = D // HS
    PR = KEEP // 2
    NB = S // QSRC
    vm = pl.BlockSpec(memory_space=pltpu.VMEM)
    hbm = pl.BlockSpec(memory_space=pl.ANY)
    dma = pltpu.SemaphoreType.DMA
    out = pl.pallas_call(
        functools.partial(kernel, S, E),
        out_shape=[
            jax.ShapeDtypeStruct((TOK, D), BF16),
            jax.ShapeDtypeStruct((TOK, D), BF16),
            jax.ShapeDtypeStruct((KEEP, 3 * D), BF16),
            jax.ShapeDtypeStruct((TOPK, 1, KEEP), F32),
        ],
        in_specs=[hbm, vm, vm, hbm, vm, vm, hbm, hbm, hbm, hbm],
        out_specs=[hbm, hbm, hbm, vm],
        scratch_shapes=[
            pltpu.VMEM((TOK, D), BF16),
            pltpu.VMEM((TOK, D), BF16),
            pltpu.VMEM((KEEP, 3 * D), BF16),
            pltpu.VMEM((TOK, D), BF16),
            pltpu.VMEM((TOK, D), BF16),
            pltpu.VMEM((KEEP, 3 * D), BF16),
            dma((6,)),
            pltpu.VMEM((S, KEEP, HS), BF16),
            pltpu.VMEM((2, S, KEEP, HS), BF16),
            pltpu.VMEM((S, PR, HS), BF16),
            pltpu.VMEM((S, PR, HS), BF16),
            pltpu.VMEM((S, PR, HS), BF16),
            pltpu.VMEM((S, PR, HS), BF16),
            pltpu.VMEM((S, PR, HS), BF16),
            pltpu.VMEM((S, PR, HS), BF16),
            pltpu.VMEM((S, KEEP, HS), BF16),
            pltpu.VMEM((S, KEEP, HS), BF16),
            pltpu.VMEM((S, PR, HS), BF16),
            pltpu.VMEM((S, PR, HS), BF16),
            pltpu.VMEM((4, E, SLOT, D), BF16),
            pltpu.VMEM((4, E, SLOT, D), BF16),
            pltpu.VMEM((X, Z, 2, KEEP, FF), BF16),
            pltpu.VMEM((X, Z, 2, KEEP // 2, FF), BF16),
            pltpu.VMEM((S * KEEP, HS), F32),
            pltpu.VMEM((HS, S * KEEP), BF16),
            pltpu.VMEM((HS, S * KEEP), BF16),
            pltpu.VMEM((S * KEEP, S * PR), F32),
            pltpu.VMEM((HS, S * PR), F32),
            pltpu.VMEM((2, S * KEEP, HS), F32),
            pltpu.VMEM((S * KEEP, HS), F32),
        ]
        + [
            dma((22,)),
            dma((NB,)),
            dma((1,)),
            dma((1,)),
            dma((NB,)),
            dma((2,)),
            dma((4,)),
            dma((X,)),
            dma((2, NB)),
            dma((2, Z + 2)),
            dma((2, Z + 2)),
            dma((2, 2)),
            dma((3,)),
        ],
        compiler_params=pltpu.CompilerParams(
            collective_id=0, has_side_effects=True, vmem_limit_bytes=60 * 1024 * 1024
        ),
    )(
        residual[0],
        kept_index,
        kept_count,
        projected[0],
        jnp.transpose(expert_ids, (2, 0, 1)),
        jnp.transpose(gate_values, (2, 0, 1)),
        gate_weight[0],
        up_weight[0],
        down_weight[0].T.reshape(2, KEEP // 2, FF),
        cotangent[0],
    )
    return (out[0][None], out[1][None], out[2][None], jnp.transpose(out[3], (1, 2, 0)))


def solution(mesh):
    row = P("exp", "seq", None)
    in_specs = (row, P("exp", "seq"), P("exp", "seq")) + (row,) * 5 + (P("exp", None, "seq"), row)
    return jax.shard_map(
        body, mesh=mesh, in_specs=in_specs, out_specs=(row,) * 4, check_vma=False
    )
```

```python
import functools

import jax
import jax.numpy as jnp
from jax import lax
from jax.experimental import pallas as pl
from jax.experimental.pallas import tpu as pltpu
from jax.sharding import PartitionSpec as P

HS = 128
SLOT = 16
CAP = 12
FOLDS = 3
EPSILON = 1e-06
PIECES = 2
X = 4
QSRC = 8
F32 = jnp.float32
BF16 = jnp.bfloat16
MESH = pl.DeviceIdType.MESH
NEG = -1e30
WIDE = 768
MARK = 1024.0


def nn(a, b):
    return lax.dot_general(a, b, (((1,), (0,)), ((), ())), preferred_element_type=F32)


def nt(a, b):
    return lax.dot_general(a, b, (((1,), (1,)), ((), ())), preferred_element_type=F32)


def kernel(
    S,
    E,
    residual_h,
    kept_index_h,
    kept_count_h,
    projected_h,
    expert_ids_h,
    gate_values_h,
    gate_w,
    up_w,
    down_w,
    cotangent_h,
    output_h,
    input_grad_h,
    projected_grad_h,
    gate_grads,
    residual,
    cotangent,
    projected,
    kept_index,
    kept_count,
    expert_ids,
    gate_values,
    io_sem,
    kv_send,
    kv,
    q_send,
    q_recv,
    a_send,
    a_recv,
    g_send,
    g_recv,
    b_send,
    b_recv,
    dq_send,
    dq_recv,
    x_send,
    x_recv,
    y_send,
    y_recv,
    x_rows,
    wt,
    bias,
    k_t,
    v_t,
    prob,
    att_t,
    acc,
    other,
    send_ss,
    kv_rs,
    q_rs,
    a_rs,
    g_rs,
    b_rs,
    x_rs,
    y_rs,
    rows_rs,
    swap_rs,
    wt_rs,
    core_rs,
):
    Z = S // X
    KEEP = kept_index.shape[1]
    TOK, D = residual.shape
    FF = gate_w.shape[2]
    HEADS = D // HS
    PR = KEEP // 2
    NB = S // QSRC
    KB = QSRC * KEEP
    QB = QSRC * PR
    NS = E * SLOT
    scale = HS**-0.5
    me = lax.axis_index("seq")
    ex = lax.axis_index("exp")
    mx = me // Z
    mz = lax.rem(me, Z)
    yy = ex // 2
    core = lax.rem(ex, 2)
    sib = 1 - core
    grp = mx // 2
    half = lax.rem(mx, 2)
    head = me // 2
    par = lax.rem(me, 2)
    expert = 2 * yy + grp

    def load(i, src, dst):
        return pltpu.make_async_copy(src, dst, io_sem.at[i])

    projected_in = load(0, projected_h, projected)
    cotangent_in = load(1, cotangent_h, cotangent)
    residual_in = load(2, residual_h, residual)
    small_in = (
        load(6, kept_count_h, kept_count),
        load(7, kept_index_h, kept_index),
        load(8, expert_ids_h, expert_ids),
        load(9, gate_values_h, gate_values),
    )
    for copy in (projected_in, *small_in, cotangent_in, residual_in):
        copy.start()

    def greet(seq, exp):
        pl.semaphore_signal(
            barrier, inc=1, device_id={"seq": seq, "exp": exp}, device_id_type=MESH
        )

    barrier = pltpu.get_barrier_semaphore()

    def greet_plane(k, t):
        i = lax.rem(2 * me + core + k, 2 * S)
        greet(i // 2, 2 * yy + lax.rem(i, 2))
        return t

    def greet_others(k, t):
        e = lax.rem(2 * yy + 2 + k, E)
        for x in range(X):
            greet(x * Z + mz, e)
        return t

    lax.fori_loop(1, 2 * S, greet_plane, 0)
    lax.fori_loop(0, E - 2, greet_others, 0)

    projected_in.wait()
    for copy in small_in:
        copy.wait()
    count = kept_count[...]
    live_col = lax.broadcasted_iota(jnp.int32, (KEEP, 1), 0) < count
    for h in range(HEADS):
        c0 = h * HS
        keys = projected[:, D + c0 : D + c0 + HS].astype(F32)
        kv_send[2 * h] = jnp.where(live_col, keys, MARK).astype(BF16)
        kv_send[2 * h + 1] = projected[:, 2 * D + c0 : 2 * D + c0 + HS]
        for p in range(2):
            q_send[2 * h + p] = projected[p * PR : (p + 1) * PR, c0 : c0 + HS]

    slot_row = lax.broadcasted_iota(jnp.int32, (NS, KEEP), 0)
    slot_exp = slot_row // SLOT
    slot_pos = slot_row - slot_exp * SLOT
    entry = lax.broadcasted_iota(jnp.int32, (NS, KEEP), 1)
    live = entry < count
    assigned = jnp.zeros((NS, KEEP), F32)
    weight = jnp.zeros((NS, KEEP), F32)
    for k in range(expert_ids.shape[0]):
        match = (expert_ids[k] == slot_exp) & live
        assigned = assigned + jnp.where(match, 1.0, 0.0)
        weight = weight + jnp.where(match, gate_values[k], 0.0)
    ei = lax.broadcasted_iota(jnp.int32, (KEEP, KEEP), 0)
    ej = lax.broadcasted_iota(jnp.int32, (KEEP, KEEP), 1)
    earlier = jnp.where(ei < ej, 1.0, 0.0).astype(BF16)
    rank = nn(assigned.astype(BF16), earlier)
    table = jnp.where((assigned > 0.5) & (rank == slot_pos.astype(F32)), 1.0, 0.0)
    table_half = table.astype(BF16)
    weighted = table * weight
    slot_gate = jnp.sum(weighted, axis=1, keepdims=True)

    def turned(a):
        if a.shape[1] < 128:
            a = jnp.concatenate([a, jnp.zeros((a.shape[0], 128 - a.shape[1]), F32)], 1)
        return a.T

    table_t = turned(table)[:KEEP].astype(BF16)
    weighted_t = turned(weighted)[:KEEP]
    w_high = weighted_t.astype(BF16)
    w_low = (weighted_t - w_high.astype(F32)).astype(BF16)

    KC = Z * KEEP
    NR = 2 * NS
    fr = lax.broadcasted_iota(jnp.int32, (NR, NR), 0)
    fc = lax.broadcasted_iota(jnp.int32, (NR, NR), 1)
    spot = lax.rem(fr, SLOT)
    fold, unfold = [], []
    for g in range(FOLDS):
        gap = CAP - 4 * g
        fold.append(jnp.where((spot >= CAP) & (fc == fr - gap), 1.0, 0.0).astype(BF16))
        unfold.append(jnp.where((spot // 4 == g) & (fc == fr + gap), 1.0, 0.0).astype(BF16))

    def quarter(g):
        return slice(g * KC, (g + 1) * KC)

    def pack(ref, g, chunk, last):
        n = chunk.shape[0]
        full = chunk + nn(fold[g][:n, :n], last)
        ref[:, :, quarter(g)] = full.astype(BF16).reshape(n // SLOT, SLOT, KC)

    def pack_all(ref, rows):
        for g in range(FOLDS):
            pack(ref, g, rows[:, quarter(g)], rows[:, quarter(FOLDS)].astype(BF16))

    cotangent_in.wait()
    residual_in.wait()
    index_row = kept_index[...]
    index_col = jnp.sum(jnp.where(ei == ej, index_row, 0), axis=1, keepdims=True)
    pick = jnp.where(
        lax.broadcasted_iota(jnp.int32, (KEEP, TOK), 1) == index_col, 1.0, 0.0
    ).astype(BF16)
    grad_f = nn(pick, cotangent[...])
    kept_f = nn(pick, residual[...])
    grad_sel = nn(table_half, grad_f.astype(BF16))
    pack_all(x_send.at[0], (slot_gate * grad_sel).astype(BF16).astype(F32))
    grad_sel = grad_sel.astype(BF16)
    pl.semaphore_wait(barrier, 2 * S - 1 + X * (E - 2))

    def remote(src, dst, ss, rs, seq, exp):
        return pltpu.make_async_remote_copy(
            src_ref=src,
            dst_ref=dst,
            send_sem=ss,
            recv_sem=rs,
            device_id={"seq": seq, "exp": exp},
            device_id_type=MESH,
        )

    def landed(view, sem):
        remote(view, view, send_ss.at[0], sem, me, 2 * yy + sib).wait_recv()

    def left(n, view):
        remote(view, view, send_ss.at[n], q_rs.at[0], me, 2 * yy + sib).wait_send()

    def left_all(n, ref):
        @pl.when(par == core)
        def _():
            left(n, ref.at[pl.ds(0, S - 1)])

        @pl.when(par != core)
        def _():
            left(n, ref)

    here = 2 * head + core

    def each_head(do):
        def step(k, t):
            i = lax.rem(k + 2 * head, S)

            @pl.when((2 * (i // 2) + core != me) | (lax.rem(i, 2) != core))
            def _():
                do(i)

            return t

        lax.fori_loop(0, S, step, 0)

    def each_source(do, first=0, n=S):
        def step(k, t):
            d = first + lax.rem(me + k, n)

            @pl.when((d != me) | (par != core))
            def _():
                do(d)

            return t

        lax.fori_loop(0, n, step, 0)

    def kv_copy(i):
        p = lax.rem(i, 2)
        return remote(
            kv_send.at[i],
            kv.at[p, me],
            send_ss.at[0],
            kv_rs.at[me // QSRC],
            2 * (i // 2) + core,
            2 * yy + p,
        )

    def head_copy(n, send, recv, rs, i):
        return remote(
            send.at[i],
            recv.at[me],
            send_ss.at[n],
            rs,
            2 * (i // 2) + core,
            2 * yy + lax.rem(i, 2),
        )

    def source_copy(n, send, recv, rs, d):
        return remote(send.at[d], recv.at[here], send_ss.at[n], rs, d, 2 * yy + par)

    def own_copy(src, dst, sem):
        @pl.when(par == core)
        def _():
            pltpu.make_async_copy(src, dst, sem).start()

    def each_expert(do):
        def step(k, t):
            e = lax.rem(ex + k, E)
            for hf in range(2):
                x = 2 * lax.rem(e, 2) + hf

                @pl.when((e != expert) | (hf != half) | (core != grp))
                def _():
                    do(e, x * Z + mz, 2 * (e // 2) + grp)

            return t

        lax.fori_loop(0, E, step, 0)

    def each_list(do):
        def step(k, t):
            b = lax.rem(ex + k, E)
            for r in range(2):
                x = 2 * core + r

                @pl.when((b != ex) | (x != mx))
                def _():
                    do(r * E + b, x * Z + mz, b)

            return t

        lax.fori_loop(0, E, step, 0)

    def out_start(n):
        slot = half * E + ex

        @pl.when(core == grp)
        def _():
            pltpu.make_async_copy(x_send.at[n, expert], x_recv.at[n, slot], x_rs.at[n]).start()

        each_expert(
            lambda e, seq, exp: remote(
                x_send.at[n, e], x_recv.at[n, slot], send_ss.at[6 + n], x_rs.at[n], seq, exp
            ).start()
        )

    def x_landed(n):
        landed(x_recv.at[n], x_rs.at[n])

    def part_cols(c):
        return pl.ds(c * Z * KEEP, Z * KEEP)

    def back_start(n, cols, ss, rs):
        slot = half * E + expert

        @pl.when(core == grp)
        def _():
            pltpu.make_async_copy(
                y_send.at[n, half * E + ex, :, cols], y_recv.at[n, slot, :, cols], rs
            ).start()

        each_list(
            lambda i, seq, exp: remote(
                y_send.at[n, i, :, cols], y_recv.at[n, slot, :, cols], ss, rs, seq, exp
            ).start()
        )

    def sixteen_left(n, ref, cols):
        @pl.when(core == grp)
        def _():
            left(n, ref.at[pl.ds(0, 2 * E - 1), :, cols])

        @pl.when(core != grp)
        def _():
            left(n, ref.at[:, :, cols])

    RING, CORE, INIT = 13, 14, 15
    part_all = pl.ds(0, FOLDS * Z * KEEP)

    def at_z(o):
        return lax.rem(mz + o + Z, Z)

    def arrival(w, oz, part):
        return wt_rs.at[w, oz % Z if part != 1 else Z]

    def piece(w, oz, part, group, seq, exp, sem):
        view = wt.at[2 * core + w, at_z(oz)]
        if part is not None:
            view = wt.at[2 * core + w, at_z(oz), :, part]
        return remote(view, view, send_ss.at[group], sem, seq, exp)

    def wait(w, oz, parts):
        for part in (0, 1) if parts else (None,):
            piece(w, oz, part, RING, me, 2 * yy + sib, arrival(w, oz, part)).wait_recv()

    both = (1, -1)

    def hop(w, sgn, k):
        if k < Z // 2:
            part = None if k < Z // 2 - 1 else (0 if sgn > 0 else 1)
            sem = arrival(w, -sgn * (k + 1), part)
            piece(w, -sgn * k, part, RING, mx * Z + at_z(sgn), ex, sem).start()

    def to_core(w, oz):
        piece(w, oz, None, CORE, me, 2 * yy + sib, core_rs.at[w]).start()

    def along_z(k):
        for w in (0, 1):
            if k == Z // 2:
                wait(w, k, True)
                to_core(w, k)
            else:
                for s in both:
                    wait(w, -s * k, False)
                    hop(w, s, k)
                    to_core(w, -s * k)

    def init_start():
        for hf in range(2):
            cols = pl.ds(hf * (FF - WIDE), WIDE)
            x = 2 * core + hf
            for n, ref in enumerate((gate_w, up_w, down_w)):
                src, dst, sem = ref.at[:, :, cols], wt.at[mx, mz, n], wt_rs.at[half, 0]

                @pl.when((x == mx) & (core == grp))
                def _():
                    pltpu.make_async_copy(src, dst, sem).start()

                @pl.when((x != mx) | (core != grp))
                def _():
                    seq = x * Z + mz
                    remote(src, dst, send_ss.at[INIT], sem, seq, 2 * yy + grp).start()

    init_start()
    own_copy(kv_send.at[here], kv.at[core, me], kv_rs.at[me // QSRC])
    own_copy(q_send.at[here], q_recv.at[me], q_rs.at[0])
    each_head(lambda i: kv_copy(i).start())
    each_head(lambda i: head_copy(1, q_send, q_recv, q_rs.at[0], i).start())

    for w in (0, 1):
        landed(wt.at[2 * core + w, mz], wt_rs.at[w, 0])
        for s in both:
            hop(w, s, 0)
        to_core(w, 0)
    out_start(0)

    along_z(1)
    def swap_copy(b):
        view = kv.at[core, pl.ds(b * QSRC, QSRC)]
        return remote(view, view, send_ss.at[16], swap_rs.at[0, b], me, 2 * yy + sib)

    for b in range(NB):
        landed(kv.at[core, pl.ds(b * QSRC, QSRC)], kv_rs.at[b])
        swap_copy(b).start()
    landed(q_recv, q_rs.at[0])
    for b in range(NB):
        landed(kv.at[sib, pl.ds(b * QSRC, QSRC)], swap_rs.at[0, b])

    def key_block(c):
        return kv[0, c * QSRC : (c + 1) * QSRC].reshape(KB, HS)

    def value_block(c):
        return kv[1, c * QSRC : (c + 1) * QSRC].reshape(KB, HS)

    def query_block(b):
        return q_recv[b * QSRC : (b + 1) * QSRC].reshape(QB, HS)

    for b in range(NB):
        k_f = key_block(b).astype(F32)
        bias[b * KB : (b + 1) * KB] = jnp.where(k_f > MARK / 2, NEG, 0.0)
        k_t[:, b * KB : (b + 1) * KB] = k_f.T.astype(BF16)
        v_t[:, b * KB : (b + 1) * KB] = value_block(b).astype(F32).T.astype(BF16)

    qcol = lax.broadcasted_iota(jnp.int32, (KB, QB), 1)
    qent = (qcol // PR) * KEEP + core * PR + lax.rem(qcol, PR)
    causal = lax.broadcasted_iota(jnp.int32, (KB, QB), 0) <= qent

    def forward_block(b):
        cols = slice(b * QB, (b + 1) * QB)
        q_blk = query_block(b)
        top = None
        for c in range(b + 1):
            rows = slice(c * KB, (c + 1) * KB)
            half = bias[rows, :]
            sc = nt(key_block(c), q_blk) * scale + jnp.concatenate([half] * (QB // HS), 1)
            if c == b:
                sc = jnp.where(causal, sc, NEG)
            prob[rows, cols] = sc
            m = jnp.max(sc, axis=0, keepdims=True)
            top = m if top is None else jnp.maximum(top, m)
        total = jnp.zeros((1, QB), F32)
        for c in range(b + 1):
            rows = slice(c * KB, (c + 1) * KB)
            e = jnp.exp(prob[rows, cols] - top)
            prob[rows, cols] = e
            total = total + jnp.sum(e, axis=0, keepdims=True)
        inv = 1.0 / total
        out = jnp.zeros((HS, QB), F32)
        for c in range(b + 1):
            rows = slice(c * KB, (c + 1) * KB)
            pr = prob[rows, cols] * inv
            prob[rows, cols] = pr
            out = out + nn(v_t[:, rows], pr.astype(BF16))
        att_t[:, cols] = out
        a_send[b * QSRC : (b + 1) * QSRC] = out.T.astype(BF16).reshape(QSRC, PR, HS)
        each_source(
            lambda d: source_copy(2, a_send, a_recv, a_rs.at[0], d).start(), b * QSRC, QSRC
        )

    for b in range(NB):
        forward_block(b)
    own_copy(a_send.at[me], a_recv.at[here], a_rs.at[0])
    along_z(2)
    landed(a_recv, a_rs.at[0])

    attended = jnp.concatenate(
        [jnp.concatenate([a_recv[2 * h + p] for h in range(HEADS)], 1) for p in range(2)], 0
    )
    h1 = jnp.where(live_col, kept_f + attended.astype(F32), 0.0)
    inv_rms = lax.rsqrt(jnp.mean(h1 * h1, axis=1, keepdims=True) + EPSILON)
    normed = (h1 * inv_rms).astype(BF16)
    pack_all(x_send.at[1], nn(table_half, normed))
    out_start(1)
    pre = [jnp.zeros((NR, WIDE), F32)] * 3

    def weight_of(ax, n):
        return wt[ax, :, n].reshape(KC, WIDE)

    def expert_chunk(ax):
        cols = pl.ds(pl.multiple_of(ax * KC, KC), KC)
        r = x_rows[1, :, cols]
        g = x_rows[0, :, cols]
        pre[0] = pre[0] + nn(r, weight_of(ax, 0))
        pre[1] = pre[1] + nn(r, weight_of(ax, 1))
        pre[2] = pre[2] + nn(g, weight_of(ax, 2))

    along_z(3)
    along_z(Z // 2)
    x_landed(0)
    x_landed(1)
    used = lax.rem(lax.broadcasted_iota(jnp.int32, (NR, KC), 0), SLOT) < CAP
    for n in (0, 1):
        last = jnp.zeros((NR, KC), F32)
        for g in range(FOLDS):
            chunk = x_recv[n, :, :, quarter(g)].reshape(NR, KC)
            last = last + nn(unfold[g], chunk)
            x_rows[n, :, quarter(g)] = jnp.where(used, chunk.astype(F32), 0.0).astype(BF16)
        x_rows[n, :, quarter(FOLDS)] = last.astype(BF16)
    for w in (0, 1):
        expert_chunk(2 * core + w)
    for w in (0, 1):
        landed(wt.at[2 * sib + w], core_rs.at[w])
        expert_chunk(2 * sib + w)
    gate_pre, up_pre, mid_grad = pre
    sig = 1.0 / (1.0 + jnp.exp(-gate_pre))
    act = gate_pre * sig
    lane = lax.broadcasted_iota(jnp.int32, (NR, WIDE), 1)
    own = (lane >= 2 * WIDE - FF) | (half == 0)
    mid_grad = jnp.where(own, mid_grad, 0.0)
    gate_grad = (mid_grad * up_pre * sig * (1.0 + gate_pre * (1.0 - sig))).astype(BF16)
    up_grad = (mid_grad * act).astype(BF16)
    mid = jnp.where(own, act * up_pre, 0.0).astype(BF16)
    def back_of(c):
        return nt(gate_grad, weight_of(c, 0)) + nt(up_grad, weight_of(c, 1))

    last = back_of(FOLDS).astype(BF16)
    for g in range(FOLDS):
        pack(y_send.at[0], g, back_of(g), last)
        back_start(0, part_cols(g), send_ss.at[9 + g], rows_rs.at[g])
    last = nt(mid, weight_of(FOLDS, 2)).astype(BF16)
    for g in range(FOLDS):
        pack(y_send.at[1], g, nt(mid, weight_of(g, 2)), last)
    table_t = jnp.concatenate([table_t, table_t], 1)
    parts, last = [], jnp.zeros((KEEP, KC), F32)
    for g in range(FOLDS):
        landed(y_recv.at[0, :, :, part_cols(g)], rows_rs.at[g])
        chunk = y_recv[0, :, :, quarter(g)].reshape(NR, KC)
        parts.append(nn(table_t, chunk))
        last = last + nn(nt(table_t, fold[g]).astype(BF16), chunk)
    parts.append(last)
    normed_grad = jnp.concatenate(parts, 1)
    cubed = inv_rms * inv_rms * inv_rms
    h1_grad = (
        grad_f
        + inv_rms * normed_grad
        - h1 * cubed * jnp.mean(normed_grad * h1, axis=1, keepdims=True)
    )
    h1_grad = jnp.where(live_col, h1_grad, 0.0).astype(BF16)
    for h in range(HEADS):
        for p in range(2):
            g_send[2 * h + p] = h1_grad[p * PR : (p + 1) * PR, h * HS : (h + 1) * HS]
    own_copy(g_send.at[here], g_recv.at[me], g_rs.at[me // QSRC])
    each_head(lambda i: head_copy(3, g_send, g_recv, g_rs.at[me // QSRC], i).start())

    token = lax.broadcasted_iota(jnp.int32, (TOK, KEEP), 0)
    put = jnp.where(
        (token == index_row) & (lax.broadcasted_iota(jnp.int32, (TOK, KEEP), 1) < count),
        1.0,
        0.0,
    )
    replaced = jnp.sum(put, axis=1, keepdims=True) > 0.5
    put = put.astype(BF16)
    cotangent[...] = jnp.where(replaced, nn(put, h1_grad), cotangent[...].astype(F32)).astype(
        BF16
    )
    input_grad_out = load(0, cotangent, input_grad_h)
    input_grad_out.start()
    back_start(1, part_all, send_ss.at[8], y_rs.at[0])

    def give_copy(c):
        rows = pl.ds(c * KB, KB)
        return remote(
            acc.at[sib, rows],
            other.at[rows],
            send_ss.at[17],
            swap_rs.at[1, c],
            me,
            2 * yy + sib,
        )

    def finish_block(c):
        rows = slice(c * KB, (c + 1) * KB)
        landed(other.at[pl.ds(c * KB, KB)], swap_rs.at[1, c])
        whole = acc[core, rows] + other[rows]
        b_send[c * QSRC : (c + 1) * QSRC] = whole.astype(BF16).reshape(QSRC, KEEP, HS)
        each_source(
            lambda d: source_copy(4, b_send, b_recv, b_rs.at[0], d).start(), c * QSRC, QSRC
        )

    dout = [None] * NB
    delta = [None] * NB
    dq_t = [jnp.zeros((HS, QB), F32)] * NB
    for c in reversed(range(NB)):
        rows = slice(c * KB, (c + 1) * KB)
        block = pl.ds(c * QSRC, QSRC)
        landed(g_recv.at[block], g_rs.at[c])
        dout[c] = g_recv[c * QSRC : (c + 1) * QSRC].reshape(QB, HS)
        turn = dout[c].astype(F32).T * att_t[:, c * QB : (c + 1) * QB]
        delta[c] = jnp.sum(turn, axis=0, keepdims=True)
        dk = jnp.zeros((KB, HS), F32)
        dv = jnp.zeros((KB, HS), F32)
        for b in range(c, NB):
            pr = prob[rows, b * QB : (b + 1) * QB]
            ds = (pr * (nt(value_block(c), dout[b]) - delta[b]) * scale).astype(BF16)
            dq_t[b] = dq_t[b] + nn(k_t[:, rows], ds)
            dk = dk + nn(ds, query_block(b))
            dv = dv + nn(pr.astype(BF16), dout[b])
        acc[0, rows] = dk
        acc[1, rows] = dv
        give_copy(c).start()
        if c < NB - 1:
            finish_block(c + 1)
    for b in range(NB):
        dq_send[b * QSRC : (b + 1) * QSRC] = dq_t[b].T.astype(BF16).reshape(QSRC, PR, HS)
    each_source(lambda d: source_copy(5, dq_send, dq_recv, b_rs.at[1], d).start())
    finish_block(0)
    own_copy(dq_send.at[me], dq_recv.at[here], b_rs.at[1])
    own_copy(b_send.at[me], b_recv.at[here], b_rs.at[0])

    landed(y_recv.at[1], y_rs.at[0])
    parts, last = [], jnp.zeros((KEEP, KC), F32)
    made_last = jnp.zeros((NR, KC), F32)
    per_slot = jnp.zeros((NS, 1), F32)

    def against(rows, g):
        both_halves = (rows[:NS] + rows[NS:]) * grad_sel[:, quarter(g)].astype(F32)
        return jnp.sum(both_halves, axis=1, keepdims=True)

    for g in range(FOLDS):
        chunk = y_recv[1, :, :, quarter(g)].reshape(NR, KC)
        there = jnp.zeros((KEEP, KC), F32)
        for w in (w_high, w_low):
            w = jnp.concatenate([w, w], 1)
            there = there + nn(w, chunk)
            last = last + nn(nt(w, fold[g]).astype(BF16), chunk)
        parts.append(there)
        made_last = made_last + nn(unfold[g], chunk)
        per_slot = per_slot + against(chunk.astype(F32), g)
    per_slot = per_slot + against(made_last, FOLDS)
    mixture = jnp.concatenate(parts + [last], 1)
    new_rows = (h1 + mixture).astype(BF16)
    residual[...] = jnp.where(replaced, nn(put, new_rows), residual[...].astype(F32)).astype(BF16)
    spread = table * per_slot
    for k in range(expert_ids.shape[0]):
        hit = expert_ids[k] == slot_exp
        gate_grads[k] = jnp.sum(jnp.where(hit, spread, 0.0), axis=0, keepdims=True)
    output_out = load(1, residual, output_h)
    output_out.start()
    left_all(0, kv_send)
    left_all(1, q_send)
    left_all(2, a_send)
    left_all(3, g_send)
    for n in (0, 1):
        sixteen_left(6 + n, x_recv.at[n], part_all)
    sixteen_left(8, y_send.at[1], part_all)
    for c in range(FOLDS):
        sixteen_left(9 + c, y_send.at[0], part_cols(c))
    left(RING, wt.at[pl.ds(0, 2), pl.ds(0, Z - 1)])
    left(CORE, wt.at[pl.ds(0, 2)])
    left(16, kv.at[core])
    left(17, acc.at[sib])

    @pl.when(core == grp)
    def _():
        left(INIT, wt.at[0, 0])

    @pl.when(core != grp)
    def _():
        left(INIT, wt.at[0, pl.ds(0, 2)])

    landed(b_recv, b_rs.at[0])
    landed(dq_recv, b_rs.at[1])
    for h in range(HEADS):
        c0 = h * HS
        for p in range(2):
            projected[p * PR : (p + 1) * PR, c0 : c0 + HS] = dq_recv[2 * h + p]
            o = (1 + p) * D + c0
            projected[:, o : o + HS] = b_recv[2 * h + p]
    projected_grad_out = load(2, projected, projected_grad_h)
    projected_grad_out.start()
    left_all(4, b_send)
    left_all(5, dq_send)
    for copy in (input_grad_out, output_out, projected_grad_out):
        copy.wait()


def finish(a, b, c, d, out_a, out_b, out_c, out_d, sa, sb, sc, sd, sem):
    ins, outs = [], []
    for src, stage, dst in ((a, sa, out_a), (b, sb, out_b), (c, sc, out_c)):
        n = src.shape[0] // PIECES
        for k in range(PIECES):
            rows = pl.ds(k * n, n)
            ins.append((src.at[rows], stage.at[rows]))
            outs.append((stage.at[rows], dst.at[0, rows]))
    ins.append((d, sd))
    outs.append((sd, out_d))
    ins = [pltpu.make_async_copy(*c, sem.at[0, i]) for i, c in enumerate(ins)]
    outs = [pltpu.make_async_copy(*c, sem.at[1, i]) for i, c in enumerate(outs)]
    for copy in ins:
        copy.start()
    for copy, after in zip(ins, outs):
        copy.wait()
        after.start()
    for copy in outs:
        copy.wait()


def body(
    residual,
    kept_index,
    kept_count,
    projected,
    expert_ids,
    gate_values,
    gate_weight,
    up_weight,
    down_weight,
    cotangent,
):
    S = lax.axis_size("seq")
    E = lax.axis_size("exp")
    _, TOK, D = residual.shape
    KEEP = kept_index.shape[1]
    FF = gate_weight.shape[2]
    TOPK = expert_ids.shape[2]
    Z = S // X
    HEADS = D // HS
    PR = KEEP // 2
    NB = S // QSRC
    vm = pl.BlockSpec(memory_space=pltpu.VMEM)
    hbm = pl.BlockSpec(memory_space=pl.ANY)
    dma = pltpu.SemaphoreType.DMA
    out = pl.pallas_call(
        functools.partial(kernel, S, E),
        out_shape=[
            jax.ShapeDtypeStruct((TOK, D), BF16),
            jax.ShapeDtypeStruct((TOK, D), BF16),
            jax.ShapeDtypeStruct((KEEP, 3 * D), BF16),
            jax.ShapeDtypeStruct((TOPK, 1, KEEP), F32),
        ],
        in_specs=[hbm] * 10,
        out_specs=[hbm, hbm, hbm, vm],
        scratch_shapes=[
            pltpu.VMEM((TOK, D), BF16),
            pltpu.VMEM((TOK, D), BF16),
            pltpu.VMEM((KEEP, 3 * D), BF16),
            pltpu.VMEM((1, KEEP), jnp.int32),
            pltpu.VMEM((1, 1), jnp.int32),
            pltpu.VMEM((TOPK, 1, KEEP), jnp.int32),
            pltpu.VMEM((TOPK, 1, KEEP), F32),
            dma((10,)),
            pltpu.VMEM((S, KEEP, HS), BF16),
            pltpu.VMEM((2, S, KEEP, HS), BF16),
            pltpu.VMEM((S, PR, HS), BF16),
            pltpu.VMEM((S, PR, HS), BF16),
            pltpu.VMEM((S, PR, HS), BF16),
            pltpu.VMEM((S, PR, HS), BF16),
            pltpu.VMEM((S, PR, HS), BF16),
            pltpu.VMEM((S, PR, HS), BF16),
            pltpu.VMEM((S, KEEP, HS), BF16),
            pltpu.VMEM((S, KEEP, HS), BF16),
            pltpu.VMEM((S, PR, HS), BF16),
            pltpu.VMEM((S, PR, HS), BF16),
            pltpu.VMEM((2, E, SLOT, D * CAP // SLOT), BF16),
            pltpu.VMEM((2, 2 * E, SLOT, D * CAP // SLOT), BF16),
            pltpu.VMEM((2, 2 * E, SLOT, D * CAP // SLOT), BF16),
            pltpu.VMEM((2, 2 * E, SLOT, D * CAP // SLOT), BF16),
            pltpu.VMEM((2, 2 * E * SLOT, D), BF16),
            pltpu.VMEM((X, Z, 3, 2, KEEP // 2, WIDE), BF16),
            pltpu.VMEM((S * KEEP, HS), F32),
            pltpu.VMEM((HS, S * KEEP), BF16),
            pltpu.VMEM((HS, S * KEEP), BF16),
            pltpu.VMEM((S * KEEP, S * PR), F32),
            pltpu.VMEM((HS, S * PR), F32),
            pltpu.VMEM((2, S * KEEP, HS), F32),
            pltpu.VMEM((S * KEEP, HS), F32),
        ]
        + [
            dma((18,)),
            dma((NB,)),
            dma((1,)),
            dma((1,)),
            dma((NB,)),
            dma((2,)),
            dma((2,)),
            dma((1,)),
            dma((X,)),
            dma((2, NB)),
            dma((2, Z + 1)),
            dma((2,)),
        ],
        compiler_params=pltpu.CompilerParams(
            collective_id=0, has_side_effects=True, vmem_limit_bytes=60 * 1024 * 1024
        ),
    )(
        residual[0],
        kept_index,
        kept_count,
        projected[0],
        jnp.transpose(expert_ids, (2, 0, 1)),
        jnp.transpose(gate_values, (2, 0, 1)),
        gate_weight[0].reshape(2, KEEP // 2, FF),
        up_weight[0].reshape(2, KEEP // 2, FF),
        down_weight[0].T.reshape(2, KEEP // 2, FF),
        cotangent[0],
    )
    out = pl.pallas_call(
        finish,
        out_shape=[
            jax.ShapeDtypeStruct((1, TOK, D), BF16),
            jax.ShapeDtypeStruct((1, TOK, D), BF16),
            jax.ShapeDtypeStruct((1, KEEP, 3 * D), BF16),
            jax.ShapeDtypeStruct((TOPK, 1, KEEP), F32),
        ],
        in_specs=[hbm] * 4,
        out_specs=[hbm] * 4,
        scratch_shapes=[
            pltpu.VMEM((TOK, D), BF16),
            pltpu.VMEM((TOK, D), BF16),
            pltpu.VMEM((KEEP, 3 * D), BF16),
            pltpu.VMEM((TOPK, 1, KEEP), F32),
            dma((2, 3 * PIECES + 1)),
        ],
        compiler_params=pltpu.CompilerParams(vmem_limit_bytes=60 * 1024 * 1024),
    )(*out)
    return (out[0], out[1], out[2], jnp.transpose(out[3], (1, 2, 0)))


def solution(mesh):
    row = P("exp", "seq", None)
    in_specs = (row, P("exp", "seq"), P("exp", "seq")) + (row,) * 5 + (P("exp", None, "seq"), row)
    return jax.shard_map(
        body, mesh=mesh, in_specs=in_specs, out_specs=(row,) * 4, check_vma=False
    )
```

```python
import functools

import jax
import jax.numpy as jnp
from jax import lax
from jax.experimental import pallas as pl
from jax.experimental.pallas import tpu as pltpu
from jax.sharding import PartitionSpec as P

HS = 128
SLOT = 16
CAP = 12
FOLDS = 3
EPSILON = 1e-06
PIECES = 2
X = 4
QSRC = 8
F32 = jnp.float32
BF16 = jnp.bfloat16
MESH = pl.DeviceIdType.MESH
NEG = -1e30
LANES = 128
MARK = 1024.0


def nn(a, b):
    return lax.dot_general(a, b, (((1,), (0,)), ((), ())), preferred_element_type=F32)


def nt(a, b):
    return lax.dot_general(a, b, (((1,), (1,)), ((), ())), preferred_element_type=F32)


def kernel(
    S,
    E,
    residual_h,
    kept_index_h,
    kept_count_h,
    projected_h,
    expert_ids_h,
    gate_values_h,
    gate_w,
    up_w,
    down_w,
    cotangent_h,
    output_h,
    input_grad_h,
    projected_grad_h,
    gate_grads,
    residual,
    cotangent,
    projected,
    kept_index,
    kept_count,
    expert_ids,
    gate_values,
    io_sem,
    kv_send,
    kv,
    q_send,
    q_recv,
    a_send,
    a_recv,
    g_send,
    g_recv,
    b_send,
    b_recv,
    dq_send,
    dq_recv,
    x_send,
    x_recv,
    y_send,
    y_recv,
    x_rows,
    tile,
    mix,
    wt,
    bias,
    k_t,
    v_t,
    prob,
    att_t,
    acc,
    other,
    send_ss,
    kv_rs,
    q_rs,
    a_rs,
    g_rs,
    b_rs,
    x_rs,
    y_rs,
    rows_rs,
    swap_rs,
    wt_rs,
    core_rs,
):
    Z = S // X
    KEEP = kept_index.shape[1]
    TOK, D = residual.shape
    FF = gate_w.shape[2]
    HEADS = D // HS
    PR = KEEP // 2
    NB = S // QSRC
    KB = QSRC * KEEP
    QB = QSRC * PR
    NS = E * SLOT
    MAIN = FF // (2 * LANES) * LANES
    WIDE = MAIN + LANES
    GU = 2 * MAIN + LANES
    scale = HS**-0.5
    me = lax.axis_index("seq")
    ex = lax.axis_index("exp")
    mx = me // Z
    mz = lax.rem(me, Z)
    yy = ex // 2
    core = lax.rem(ex, 2)
    sib = 1 - core
    grp = mx // 2
    half = lax.rem(mx, 2)
    head = me // 2
    par = lax.rem(me, 2)
    expert = 2 * yy + grp

    def load(i, src, dst):
        return pltpu.make_async_copy(src, dst, io_sem.at[i])

    projected_in = load(0, projected_h, projected)
    cotangent_in = load(1, cotangent_h, cotangent)
    residual_in = load(2, residual_h, residual)
    small_in = (
        load(6, kept_count_h, kept_count),
        load(7, kept_index_h, kept_index),
        load(8, expert_ids_h, expert_ids),
        load(9, gate_values_h, gate_values),
    )
    shared = pl.ds(MAIN, LANES)
    tile_in = (
        load(3, gate_w.at[:, :, shared], tile.at[0]),
        load(4, up_w.at[:, :, shared], tile.at[1]),
    )
    for copy in (projected_in, *tile_in, *small_in, cotangent_in, residual_in):
        copy.start()

    def greet(seq, exp):
        pl.semaphore_signal(
            barrier, inc=1, device_id={"seq": seq, "exp": exp}, device_id_type=MESH
        )

    barrier = pltpu.get_barrier_semaphore()

    def greet_plane(k, t):
        i = lax.rem(2 * me + core + k, 2 * S)
        greet(i // 2, 2 * yy + lax.rem(i, 2))
        return t

    def greet_others(k, t):
        e = lax.rem(2 * yy + 2 + k, E)
        for x in range(X):
            greet(x * Z + mz, e)
        return t

    lax.fori_loop(1, 2 * S, greet_plane, 0)
    lax.fori_loop(0, E - 2, greet_others, 0)

    projected_in.wait()
    for copy in small_in:
        copy.wait()
    count = kept_count[...]
    live_col = lax.broadcasted_iota(jnp.int32, (KEEP, 1), 0) < count
    for h in range(HEADS):
        c0 = h * HS
        keys = projected[:, D + c0 : D + c0 + HS].astype(F32)
        kv_send[2 * h] = jnp.where(live_col, keys, MARK).astype(BF16)
        kv_send[2 * h + 1] = projected[:, 2 * D + c0 : 2 * D + c0 + HS]
        for p in range(2):
            q_send[2 * h + p] = projected[p * PR : (p + 1) * PR, c0 : c0 + HS]

    for copy in tile_in:
        copy.wait()
    tile_lane = lax.broadcasted_iota(jnp.int32, (KEEP, LANES), 1) // (LANES // 2)
    tile_g = tile[0].reshape(KEEP, LANES).astype(F32)
    tile_u = pltpu.roll(tile[1].reshape(KEEP, LANES).astype(F32), LANES // 2, 1)
    for hf in range(2):
        blend = jnp.where(tile_lane == hf, tile_g, tile_u).astype(BF16)
        mix[hf] = blend.reshape(2, KEEP // 2, LANES)
    slot_row = lax.broadcasted_iota(jnp.int32, (NS, KEEP), 0)
    slot_exp = slot_row // SLOT
    slot_pos = slot_row - slot_exp * SLOT
    entry = lax.broadcasted_iota(jnp.int32, (NS, KEEP), 1)
    live = entry < count
    assigned = jnp.zeros((NS, KEEP), F32)
    weight = jnp.zeros((NS, KEEP), F32)
    for k in range(expert_ids.shape[0]):
        match = (expert_ids[k] == slot_exp) & live
        assigned = assigned + jnp.where(match, 1.0, 0.0)
        weight = weight + jnp.where(match, gate_values[k], 0.0)
    ei = lax.broadcasted_iota(jnp.int32, (KEEP, KEEP), 0)
    ej = lax.broadcasted_iota(jnp.int32, (KEEP, KEEP), 1)
    earlier = jnp.where(ei < ej, 1.0, 0.0).astype(BF16)
    rank = nn(assigned.astype(BF16), earlier)
    table = jnp.where((assigned > 0.5) & (rank == slot_pos.astype(F32)), 1.0, 0.0)
    table_half = table.astype(BF16)
    weighted = table * weight
    slot_gate = jnp.sum(weighted, axis=1, keepdims=True)

    def turned(a):
        if a.shape[1] < 128:
            a = jnp.concatenate([a, jnp.zeros((a.shape[0], 128 - a.shape[1]), F32)], 1)
        return a.T

    table_t = turned(table)[:KEEP].astype(BF16)
    weighted_t = turned(weighted)[:KEEP]
    w_high = weighted_t.astype(BF16)
    w_low = (weighted_t - w_high.astype(F32)).astype(BF16)

    KC = Z * KEEP
    NR = 2 * NS
    fr = lax.broadcasted_iota(jnp.int32, (NR, NR), 0)
    fc = lax.broadcasted_iota(jnp.int32, (NR, NR), 1)
    spot = lax.rem(fr, SLOT)
    fold, unfold = [], []
    for g in range(FOLDS):
        gap = CAP - 4 * g
        fold.append(jnp.where((spot >= CAP) & (fc == fr - gap), 1.0, 0.0).astype(BF16))
        unfold.append(jnp.where((spot // 4 == g) & (fc == fr + gap), 1.0, 0.0).astype(BF16))

    def quarter(g):
        return slice(g * KC, (g + 1) * KC)

    def pack(ref, g, chunk, last):
        n = chunk.shape[0]
        full = chunk + nn(fold[g][:n, :n], last)
        ref[:, :, quarter(g)] = full.astype(BF16).reshape(n // SLOT, SLOT, KC)

    def pack_all(ref, rows):
        for g in range(FOLDS):
            pack(ref, g, rows[:, quarter(g)], rows[:, quarter(FOLDS)].astype(BF16))

    cotangent_in.wait()
    residual_in.wait()
    index_row = kept_index[...]
    index_col = jnp.sum(jnp.where(ei == ej, index_row, 0), axis=1, keepdims=True)
    pick = jnp.where(
        lax.broadcasted_iota(jnp.int32, (KEEP, TOK), 1) == index_col, 1.0, 0.0
    ).astype(BF16)
    grad_f = nn(pick, cotangent[...])
    kept_f = nn(pick, residual[...])
    grad_sel = nn(table_half, grad_f.astype(BF16))
    pack_all(x_send.at[0], (slot_gate * grad_sel).astype(BF16).astype(F32))
    grad_sel = grad_sel.astype(BF16)
    pl.semaphore_wait(barrier, 2 * S - 1 + X * (E - 2))

    def remote(src, dst, ss, rs, seq, exp):
        return pltpu.make_async_remote_copy(
            src_ref=src,
            dst_ref=dst,
            send_sem=ss,
            recv_sem=rs,
            device_id={"seq": seq, "exp": exp},
            device_id_type=MESH,
        )

    def landed(view, sem):
        remote(view, view, send_ss.at[0], sem, me, 2 * yy + sib).wait_recv()

    def left(n, view):
        remote(view, view, send_ss.at[n], q_rs.at[0], me, 2 * yy + sib).wait_send()

    def left_all(n, ref):
        @pl.when(par == core)
        def _():
            left(n, ref.at[pl.ds(0, S - 1)])

        @pl.when(par != core)
        def _():
            left(n, ref)

    here = 2 * head + core

    col_x = [lax.rem(mx + o, X) for o in range(X)]
    row_z = [lax.rem(mz + o, Z) for o in range(Z)]

    def unless_own(maybe, do, *args):
        if maybe is None:
            do(*args)
        else:
            pl.when(maybe)(lambda: do(*args))

    def each_head(do):
        for q in range(2):
            for j in range(Z // 4):
                for o, x in enumerate(col_x):
                    z = lax.rem(mz // 4 * 2 + 2 * j, Z // 2) + lax.rem(q + x, 2)
                    h = x * (Z // 2) + z
                    for p in range(2):
                        away = None if o else (h != head) | (par != core) | (core != p)
                        unless_own(away, do, 2 * h + p, h, p)

    def each_source(do, x0=None):
        for o, x in enumerate(col_x) if x0 is None else ((0, x0),):
            for k, z in enumerate(row_z):
                away = None if o or k else (x != mx) | (par != core)
                unless_own(away, do, x * Z + z)

    def kv_copy(i, h, p):
        return remote(
            kv_send.at[i], kv.at[p, me], send_ss.at[0], kv_rs.at[me // QSRC], 2 * h + core, 2 * yy + p
        )

    def head_copy(n, send, recv, rs, i, h, p):
        return remote(send.at[i], recv.at[me], send_ss.at[n], rs, 2 * h + core, 2 * yy + p)

    def source_copy(n, send, recv, rs, d):
        return remote(send.at[d], recv.at[here], send_ss.at[n], rs, d, 2 * yy + par)

    def own_copy(src, dst, sem):
        @pl.when(par == core)
        def _():
            pltpu.make_async_copy(src, dst, sem).start()

    def each_expert(do):
        def step(k, t):
            e = lax.rem(ex + k, E)
            for hf in range(2):
                x = 2 * lax.rem(e, 2) + hf

                @pl.when((e != expert) | (hf != half) | (core != grp))
                def _():
                    do(e, x * Z + mz, 2 * (e // 2) + grp)

            return t

        lax.fori_loop(0, E, step, 0)

    def each_list(do):
        def step(k, t):
            b = lax.rem(ex + k, E)
            for r in range(2):
                x = 2 * core + r

                @pl.when((b != ex) | (x != mx))
                def _():
                    do(r * E + b, x * Z + mz, b)

            return t

        lax.fori_loop(0, E, step, 0)

    def out_start(n):
        slot = half * E + ex

        @pl.when(core == grp)
        def _():
            pltpu.make_async_copy(x_send.at[n, expert], x_recv.at[n, slot], x_rs.at[n]).start()

        each_expert(
            lambda e, seq, exp: remote(
                x_send.at[n, e], x_recv.at[n, slot], send_ss.at[6 + n], x_rs.at[n], seq, exp
            ).start()
        )

    def x_landed(n):
        landed(x_recv.at[n], x_rs.at[n])

    def part_cols(c):
        return pl.ds(c * Z * KEEP, Z * KEEP)

    def back_start(n, cols, ss, rs):
        slot = half * E + expert

        @pl.when(core == grp)
        def _():
            pltpu.make_async_copy(
                y_send.at[n, half * E + ex, :, cols], y_recv.at[n, slot, :, cols], rs
            ).start()

        each_list(
            lambda i, seq, exp: remote(
                y_send.at[n, i, :, cols], y_recv.at[n, slot, :, cols], ss, rs, seq, exp
            ).start()
        )

    def sixteen_left(n, ref, cols):
        @pl.when(core == grp)
        def _():
            left(n, ref.at[pl.ds(0, 2 * E - 1), :, cols])

        @pl.when(core != grp)
        def _():
            left(n, ref.at[:, :, cols])

    RING, CORE, INIT = 13, 14, 15
    part_all = pl.ds(0, FOLDS * Z * KEEP)

    def at_z(o):
        return lax.rem(mz + o + Z, Z)

    def arrival(w, oz, part):
        return wt_rs.at[w, oz % Z if part != 1 else Z]

    def piece(w, oz, part, group, seq, exp, sem):
        view = wt.at[2 * core + w, at_z(oz)]
        if part is not None:
            view = wt.at[2 * core + w, at_z(oz), part]
        return remote(view, view, send_ss.at[group], sem, seq, exp)

    def wait(w, oz, parts):
        for part in (0, 1) if parts else (None,):
            piece(w, oz, part, RING, me, 2 * yy + sib, arrival(w, oz, part)).wait_recv()

    both = (1, -1)

    def hop(w, sgn, k):
        if k < Z // 2:
            part = None if k < Z // 2 - 1 else (0 if sgn > 0 else 1)
            sem = arrival(w, -sgn * (k + 1), part)
            piece(w, -sgn * k, part, RING, mx * Z + at_z(sgn), ex, sem).start()

    def to_core(w, oz):
        piece(w, oz, None, CORE, me, 2 * yy + sib, core_rs.at[w]).start()

    def along_z(k):
        for w in (0, 1):
            if k == Z // 2:
                wait(w, k, True)
                to_core(w, k)
            else:
                for s in both:
                    wait(w, -s * k, False)
                    hop(w, s, k)
                    to_core(w, -s * k)

    def init_start():
        for hf in range(2):
            x = 2 * core + hf
            main = pl.ds(hf * WIDE, MAIN)
            parts = (
                (gate_w.at[:, :, main], 0, MAIN),
                (up_w.at[:, :, main], MAIN, MAIN),
                (mix.at[hf], 2 * MAIN, LANES),
                (down_w.at[:, :, main], GU, MAIN),
                (down_w.at[:, :, shared], GU + MAIN, LANES),
            )
            for src, at, n in parts:
                dst, sem = wt.at[mx, mz, :, :, pl.ds(at, n)], wt_rs.at[half, 0]

                @pl.when((x == mx) & (core == grp))
                def _():
                    pltpu.make_async_copy(src, dst, sem).start()

                @pl.when((x != mx) | (core != grp))
                def _():
                    seq = x * Z + mz
                    remote(src, dst, send_ss.at[INIT], sem, seq, 2 * yy + grp).start()

    init_start()
    own_copy(kv_send.at[here], kv.at[core, me], kv_rs.at[me // QSRC])
    own_copy(q_send.at[here], q_recv.at[me], q_rs.at[0])
    each_head(lambda *i: kv_copy(*i).start())
    each_head(lambda *i: head_copy(1, q_send, q_recv, q_rs.at[0], *i).start())

    for w in (0, 1):
        landed(wt.at[2 * core + w, mz], wt_rs.at[w, 0])
        for s in both:
            hop(w, s, 0)
        to_core(w, 0)
    out_start(0)

    along_z(1)
    def swap_copy(b):
        view = kv.at[core, pl.ds(b * QSRC, QSRC)]
        return remote(view, view, send_ss.at[16], swap_rs.at[0, b], me, 2 * yy + sib)

    for b in range(NB):
        landed(kv.at[core, pl.ds(b * QSRC, QSRC)], kv_rs.at[b])
        swap_copy(b).start()
    landed(q_recv, q_rs.at[0])
    for b in range(NB):
        landed(kv.at[sib, pl.ds(b * QSRC, QSRC)], swap_rs.at[0, b])

    def key_block(c):
        return kv[0, c * QSRC : (c + 1) * QSRC].reshape(KB, HS)

    def value_block(c):
        return kv[1, c * QSRC : (c + 1) * QSRC].reshape(KB, HS)

    def query_block(b):
        return q_recv[b * QSRC : (b + 1) * QSRC].reshape(QB, HS)

    for b in range(NB):
        k_f = key_block(b).astype(F32)
        bias[b * KB : (b + 1) * KB] = jnp.where(k_f > MARK / 2, NEG, 0.0)
        k_t[:, b * KB : (b + 1) * KB] = k_f.T.astype(BF16)
        v_t[:, b * KB : (b + 1) * KB] = value_block(b).astype(F32).T.astype(BF16)

    qcol = lax.broadcasted_iota(jnp.int32, (KB, QB), 1)
    qent = (qcol // PR) * KEEP + core * PR + lax.rem(qcol, PR)
    causal = lax.broadcasted_iota(jnp.int32, (KB, QB), 0) <= qent

    def forward_block(b):
        cols = slice(b * QB, (b + 1) * QB)
        q_blk = query_block(b)
        top = None
        for c in range(b + 1):
            rows = slice(c * KB, (c + 1) * KB)
            half = bias[rows, :]
            sc = nt(key_block(c), q_blk) * scale + jnp.concatenate([half] * (QB // HS), 1)
            if c == b:
                sc = jnp.where(causal, sc, NEG)
            prob[rows, cols] = sc
            m = jnp.max(sc, axis=0, keepdims=True)
            top = m if top is None else jnp.maximum(top, m)
        total = jnp.zeros((1, QB), F32)
        for c in range(b + 1):
            rows = slice(c * KB, (c + 1) * KB)
            e = jnp.exp(prob[rows, cols] - top)
            prob[rows, cols] = e
            total = total + jnp.sum(e, axis=0, keepdims=True)
        inv = 1.0 / total
        out = jnp.zeros((HS, QB), F32)
        for c in range(b + 1):
            rows = slice(c * KB, (c + 1) * KB)
            pr = prob[rows, cols] * inv
            prob[rows, cols] = pr
            out = out + nn(v_t[:, rows], pr.astype(BF16))
        att_t[:, cols] = out
        a_send[b * QSRC : (b + 1) * QSRC] = out.T.astype(BF16).reshape(QSRC, PR, HS)
        each_source(
            lambda d: source_copy(2, a_send, a_recv, a_rs.at[0], d).start(), b
        )

    for b in range(NB):
        forward_block(b)
    own_copy(a_send.at[me], a_recv.at[here], a_rs.at[0])
    along_z(2)
    landed(a_recv, a_rs.at[0])

    attended = jnp.concatenate(
        [jnp.concatenate([a_recv[2 * h + p] for h in range(HEADS)], 1) for p in range(2)], 0
    )
    h1 = jnp.where(live_col, kept_f + attended.astype(F32), 0.0)
    inv_rms = lax.rsqrt(jnp.mean(h1 * h1, axis=1, keepdims=True) + EPSILON)
    normed = (h1 * inv_rms).astype(BF16)
    pack_all(x_send.at[1], nn(table_half, normed))
    out_start(1)
    pre = [jnp.zeros((NR, GU), F32), jnp.zeros((NR, WIDE), F32)]

    def gate_up_of(ax):
        return wt[ax, :, :, :, 0:GU].reshape(KC, GU)

    def down_of(ax):
        return wt[ax, :, :, :, GU:].reshape(KC, WIDE)

    def expert_chunk(ax):
        cols = pl.ds(pl.multiple_of(ax * KC, KC), KC)
        pre[0] = pre[0] + nn(x_rows[1, :, cols], gate_up_of(ax))
        pre[1] = pre[1] + nn(x_rows[0, :, cols], down_of(ax))

    along_z(3)
    x_landed(0)
    x_landed(1)
    used = lax.rem(lax.broadcasted_iota(jnp.int32, (NR, KC), 0), SLOT) < CAP
    for n in (0, 1):
        last = jnp.zeros((NR, KC), F32)
        for g in range(FOLDS):
            chunk = x_recv[n, :, :, quarter(g)].reshape(NR, KC)
            last = last + nn(unfold[g], chunk)
            x_rows[n, :, quarter(g)] = jnp.where(used, chunk.astype(F32), 0.0).astype(BF16)
        x_rows[n, :, quarter(FOLDS)] = last.astype(BF16)
    along_z(Z // 2)
    for w in (0, 1):
        expert_chunk(2 * core + w)
    for w in (0, 1):
        landed(wt.at[2 * sib + w], core_rs.at[w])
        expert_chunk(2 * sib + w)
    ahead, mid_grad = pre
    turned_tile = pltpu.roll(ahead[:, 2 * MAIN :], LANES // 2, 1)
    gate_pre = jnp.concatenate([ahead[:, :MAIN], ahead[:, 2 * MAIN :]], 1)
    up_pre = jnp.concatenate([ahead[:, MAIN : 2 * MAIN], turned_tile], 1)
    sig = 1.0 / (1.0 + jnp.exp(-gate_pre))
    act = gate_pre * sig
    lane = lax.broadcasted_iota(jnp.int32, (NR, WIDE), 1)
    own = (lane < MAIN) | ((lane - MAIN) // (LANES // 2) == half)
    mid_grad = jnp.where(own, mid_grad, 0.0)
    gate_grad = mid_grad * up_pre * sig * (1.0 + gate_pre * (1.0 - sig))
    up_grad = mid_grad * act
    turned_tile = pltpu.roll(up_grad[:, MAIN:], LANES // 2, 1)
    behind = jnp.concatenate(
        [gate_grad[:, :MAIN], up_grad[:, :MAIN], gate_grad[:, MAIN:] + turned_tile], 1
    ).astype(BF16)
    mid = jnp.where(own, act * up_pre, 0.0).astype(BF16)
    def back_of(c):
        return nt(behind, gate_up_of(c))

    last = back_of(FOLDS).astype(BF16)
    for g in range(FOLDS):
        pack(y_send.at[0], g, back_of(g), last)
        back_start(0, part_cols(g), send_ss.at[9 + g], rows_rs.at[g])
    last = nt(mid, down_of(FOLDS)).astype(BF16)
    for g in range(FOLDS):
        pack(y_send.at[1], g, nt(mid, down_of(g)), last)
    table_t = jnp.concatenate([table_t, table_t], 1)
    parts, last = [], jnp.zeros((KEEP, KC), F32)
    for g in range(FOLDS):
        landed(y_recv.at[0, :, :, part_cols(g)], rows_rs.at[g])
        chunk = y_recv[0, :, :, quarter(g)].reshape(NR, KC)
        parts.append(nn(table_t, chunk))
        last = last + nn(nt(table_t, fold[g]).astype(BF16), chunk)
    parts.append(last)
    normed_grad = jnp.concatenate(parts, 1)
    cubed = inv_rms * inv_rms * inv_rms
    h1_grad = (
        grad_f
        + inv_rms * normed_grad
        - h1 * cubed * jnp.mean(normed_grad * h1, axis=1, keepdims=True)
    )
    h1_grad = jnp.where(live_col, h1_grad, 0.0).astype(BF16)
    for h in range(HEADS):
        for p in range(2):
            g_send[2 * h + p] = h1_grad[p * PR : (p + 1) * PR, h * HS : (h + 1) * HS]
    own_copy(g_send.at[here], g_recv.at[me], g_rs.at[me // QSRC])
    each_head(lambda *i: head_copy(3, g_send, g_recv, g_rs.at[me // QSRC], *i).start())

    token = lax.broadcasted_iota(jnp.int32, (TOK, KEEP), 0)
    put = jnp.where(
        (token == index_row) & (lax.broadcasted_iota(jnp.int32, (TOK, KEEP), 1) < count),
        1.0,
        0.0,
    )
    replaced = jnp.sum(put, axis=1, keepdims=True) > 0.5
    put = put.astype(BF16)
    cotangent[...] = jnp.where(replaced, nn(put, h1_grad), cotangent[...].astype(F32)).astype(
        BF16
    )
    input_grad_out = load(0, cotangent, input_grad_h)
    input_grad_out.start()
    back_start(1, part_all, send_ss.at[8], y_rs.at[0])

    def give_copy(c):
        rows = pl.ds(c * KB, KB)
        return remote(
            acc.at[sib, rows],
            other.at[rows],
            send_ss.at[17],
            swap_rs.at[1, c],
            me,
            2 * yy + sib,
        )

    def finish_block(c):
        rows = slice(c * KB, (c + 1) * KB)
        landed(other.at[pl.ds(c * KB, KB)], swap_rs.at[1, c])
        whole = acc[core, rows] + other[rows]
        b_send[c * QSRC : (c + 1) * QSRC] = whole.astype(BF16).reshape(QSRC, KEEP, HS)
        each_source(
            lambda d: source_copy(4, b_send, b_recv, b_rs.at[0], d).start(), c
        )

    dout = [None] * NB
    delta = [None] * NB
    dq_t = [jnp.zeros((HS, QB), F32)] * NB
    for c in reversed(range(NB)):
        rows = slice(c * KB, (c + 1) * KB)
        block = pl.ds(c * QSRC, QSRC)
        landed(g_recv.at[block], g_rs.at[c])
        dout[c] = g_recv[c * QSRC : (c + 1) * QSRC].reshape(QB, HS)
        turn = dout[c].astype(F32).T * att_t[:, c * QB : (c + 1) * QB]
        delta[c] = jnp.sum(turn, axis=0, keepdims=True)
        dk = jnp.zeros((KB, HS), F32)
        dv = jnp.zeros((KB, HS), F32)
        for b in range(c, NB):
            pr = prob[rows, b * QB : (b + 1) * QB]
            ds = (pr * (nt(value_block(c), dout[b]) - delta[b]) * scale).astype(BF16)
            dq_t[b] = dq_t[b] + nn(k_t[:, rows], ds)
            dk = dk + nn(ds, query_block(b))
            dv = dv + nn(pr.astype(BF16), dout[b])
        acc[0, rows] = dk
        acc[1, rows] = dv
        give_copy(c).start()
        if c < NB - 1:
            finish_block(c + 1)
    for b in range(NB):
        dq_send[b * QSRC : (b + 1) * QSRC] = dq_t[b].T.astype(BF16).reshape(QSRC, PR, HS)
    each_source(lambda d: source_copy(5, dq_send, dq_recv, b_rs.at[1], d).start())
    finish_block(0)
    own_copy(dq_send.at[me], dq_recv.at[here], b_rs.at[1])
    own_copy(b_send.at[me], b_recv.at[here], b_rs.at[0])

    landed(y_recv.at[1], y_rs.at[0])
    parts, last = [], jnp.zeros((KEEP, KC), F32)
    made_last = jnp.zeros((NR, KC), F32)
    per_slot = jnp.zeros((NS, 1), F32)

    def against(rows, g):
        both_halves = (rows[:NS] + rows[NS:]) * grad_sel[:, quarter(g)].astype(F32)
        return jnp.sum(both_halves, axis=1, keepdims=True)

    for g in range(FOLDS):
        chunk = y_recv[1, :, :, quarter(g)].reshape(NR, KC)
        there = jnp.zeros((KEEP, KC), F32)
        for w in (w_high, w_low):
            w = jnp.concatenate([w, w], 1)
            there = there + nn(w, chunk)
            last = last + nn(nt(w, fold[g]).astype(BF16), chunk)
        parts.append(there)
        made_last = made_last + nn(unfold[g], chunk)
        per_slot = per_slot + against(chunk.astype(F32), g)
    per_slot = per_slot + against(made_last, FOLDS)
    mixture = jnp.concatenate(parts + [last], 1)
    new_rows = (h1 + mixture).astype(BF16)
    residual[...] = jnp.where(replaced, nn(put, new_rows), residual[...].astype(F32)).astype(BF16)
    spread = table * per_slot
    for k in range(expert_ids.shape[0]):
        hit = expert_ids[k] == slot_exp
        gate_grads[k] = jnp.sum(jnp.where(hit, spread, 0.0), axis=0, keepdims=True)
    output_out = load(1, residual, output_h)
    output_out.start()
    left_all(0, kv_send)
    left_all(1, q_send)
    left_all(2, a_send)
    left_all(3, g_send)
    for n in (0, 1):
        sixteen_left(6 + n, x_recv.at[n], part_all)
    sixteen_left(8, y_send.at[1], part_all)
    for c in range(FOLDS):
        sixteen_left(9 + c, y_send.at[0], part_cols(c))
    left(RING, wt.at[pl.ds(0, 2), pl.ds(0, Z - 1)])
    left(CORE, wt.at[pl.ds(0, 2)])
    left(16, kv.at[core])
    left(17, acc.at[sib])

    @pl.when(core == grp)
    def _():
        left(INIT, wt.at[0, 0])

    @pl.when(core != grp)
    def _():
        left(INIT, wt.at[0, pl.ds(0, 2)])

    landed(b_recv, b_rs.at[0])
    landed(dq_recv, b_rs.at[1])
    for h in range(HEADS):
        c0 = h * HS
        for p in range(2):
            projected[p * PR : (p + 1) * PR, c0 : c0 + HS] = dq_recv[2 * h + p]
            o = (1 + p) * D + c0
            projected[:, o : o + HS] = b_recv[2 * h + p]
    projected_grad_out = load(2, projected, projected_grad_h)
    projected_grad_out.start()
    left_all(4, b_send)
    left_all(5, dq_send)
    for copy in (input_grad_out, output_out, projected_grad_out):
        copy.wait()


def finish(a, b, c, d, out_a, out_b, out_c, out_d, sa, sb, sc, sd, sem):
    ins, outs = [], []
    for src, stage, dst in ((a, sa, out_a), (b, sb, out_b), (c, sc, out_c)):
        n = src.shape[0] // PIECES
        for k in range(PIECES):
            rows = pl.ds(k * n, n)
            ins.append((src.at[rows], stage.at[rows]))
            outs.append((stage.at[rows], dst.at[0, rows]))
    ins.append((d, sd))
    outs.append((sd, out_d))
    ins = [pltpu.make_async_copy(*c, sem.at[0, i]) for i, c in enumerate(ins)]
    outs = [pltpu.make_async_copy(*c, sem.at[1, i]) for i, c in enumerate(outs)]
    for copy in ins:
        copy.start()
    for copy, after in zip(ins, outs):
        copy.wait()
        after.start()
    for copy in outs:
        copy.wait()


def body(
    residual,
    kept_index,
    kept_count,
    projected,
    expert_ids,
    gate_values,
    gate_weight,
    up_weight,
    down_weight,
    cotangent,
):
    S = lax.axis_size("seq")
    E = lax.axis_size("exp")
    _, TOK, D = residual.shape
    KEEP = kept_index.shape[1]
    FF = gate_weight.shape[2]
    TOPK = expert_ids.shape[2]
    Z = S // X
    HEADS = D // HS
    PR = KEEP // 2
    NB = S // QSRC
    vm = pl.BlockSpec(memory_space=pltpu.VMEM)
    hbm = pl.BlockSpec(memory_space=pl.ANY)
    dma = pltpu.SemaphoreType.DMA
    out = pl.pallas_call(
        functools.partial(kernel, S, E),
        out_shape=[
            jax.ShapeDtypeStruct((TOK, D), BF16),
            jax.ShapeDtypeStruct((TOK, D), BF16),
            jax.ShapeDtypeStruct((KEEP, 3 * D), BF16),
            jax.ShapeDtypeStruct((TOPK, 1, KEEP), F32),
        ],
        in_specs=[hbm] * 10,
        out_specs=[hbm, hbm, hbm, vm],
        scratch_shapes=[
            pltpu.VMEM((TOK, D), BF16),
            pltpu.VMEM((TOK, D), BF16),
            pltpu.VMEM((KEEP, 3 * D), BF16),
            pltpu.VMEM((1, KEEP), jnp.int32),
            pltpu.VMEM((1, 1), jnp.int32),
            pltpu.VMEM((TOPK, 1, KEEP), jnp.int32),
            pltpu.VMEM((TOPK, 1, KEEP), F32),
            dma((10,)),
            pltpu.VMEM((S, KEEP, HS), BF16),
            pltpu.VMEM((2, S, KEEP, HS), BF16),
            pltpu.VMEM((S, PR, HS), BF16),
            pltpu.VMEM((S, PR, HS), BF16),
            pltpu.VMEM((S, PR, HS), BF16),
            pltpu.VMEM((S, PR, HS), BF16),
            pltpu.VMEM((S, PR, HS), BF16),
            pltpu.VMEM((S, PR, HS), BF16),
            pltpu.VMEM((S, KEEP, HS), BF16),
            pltpu.VMEM((S, KEEP, HS), BF16),
            pltpu.VMEM((S, PR, HS), BF16),
            pltpu.VMEM((S, PR, HS), BF16),
            pltpu.VMEM((2, E, SLOT, D * CAP // SLOT), BF16),
            pltpu.VMEM((2, 2 * E, SLOT, D * CAP // SLOT), BF16),
            pltpu.VMEM((2, 2 * E, SLOT, D * CAP // SLOT), BF16),
            pltpu.VMEM((2, 2 * E, SLOT, D * CAP // SLOT), BF16),
            pltpu.VMEM((2, 2 * E * SLOT, D), BF16),
            pltpu.VMEM((2, 2, KEEP // 2, LANES), BF16),
            pltpu.VMEM((2, 2, KEEP // 2, LANES), BF16),
            pltpu.VMEM((X, Z, 2, KEEP // 2, FF // LANES // 2 * LANES * 3 + 2 * LANES), BF16),
            pltpu.VMEM((S * KEEP, HS), F32),
            pltpu.VMEM((HS, S * KEEP), BF16),
            pltpu.VMEM((HS, S * KEEP), BF16),
            pltpu.VMEM((S * KEEP, S * PR), F32),
            pltpu.VMEM((HS, S * PR), F32),
            pltpu.VMEM((2, S * KEEP, HS), F32),
            pltpu.VMEM((S * KEEP, HS), F32),
        ]
        + [
            dma((18,)),
            dma((NB,)),
            dma((1,)),
            dma((1,)),
            dma((NB,)),
            dma((2,)),
            dma((2,)),
            dma((1,)),
            dma((X,)),
            dma((2, NB)),
            dma((2, Z + 1)),
            dma((2,)),
        ],
        compiler_params=pltpu.CompilerParams(
            collective_id=0, has_side_effects=True, vmem_limit_bytes=60 * 1024 * 1024
        ),
    )(
        residual[0],
        kept_index,
        kept_count,
        projected[0],
        jnp.transpose(expert_ids, (2, 0, 1)),
        jnp.transpose(gate_values, (2, 0, 1)),
        gate_weight[0].reshape(2, KEEP // 2, FF),
        up_weight[0].reshape(2, KEEP // 2, FF),
        down_weight[0].T.reshape(2, KEEP // 2, FF),
        cotangent[0],
    )
    out = pl.pallas_call(
        finish,
        out_shape=[
            jax.ShapeDtypeStruct((1, TOK, D), BF16),
            jax.ShapeDtypeStruct((1, TOK, D), BF16),
            jax.ShapeDtypeStruct((1, KEEP, 3 * D), BF16),
            jax.ShapeDtypeStruct((TOPK, 1, KEEP), F32),
        ],
        in_specs=[hbm] * 4,
        out_specs=[hbm] * 4,
        scratch_shapes=[
            pltpu.VMEM((TOK, D), BF16),
            pltpu.VMEM((TOK, D), BF16),
            pltpu.VMEM((KEEP, 3 * D), BF16),
            pltpu.VMEM((TOPK, 1, KEEP), F32),
            dma((2, 3 * PIECES + 1)),
        ],
        compiler_params=pltpu.CompilerParams(vmem_limit_bytes=60 * 1024 * 1024),
    )(*out)
    return (out[0], out[1], out[2], jnp.transpose(out[3], (1, 2, 0)))


def solution(mesh):
    row = P("exp", "seq", None)
    in_specs = (row, P("exp", "seq"), P("exp", "seq")) + (row,) * 5 + (P("exp", None, "seq"), row)
    return jax.shard_map(
        body, mesh=mesh, in_specs=in_specs, out_specs=(row,) * 4, check_vma=False
    )
```

```python
import functools

import jax
import jax.numpy as jnp
from jax import lax
from jax.experimental import pallas as pl
from jax.experimental.pallas import tpu as pltpu
from jax.sharding import PartitionSpec as P

HS = 128
SLOT = 16
CAP = 12
FOLDS = 3
EPSILON = 1e-06
X = 4
QSRC = 8
F32 = jnp.float32
BF16 = jnp.bfloat16
MESH = pl.DeviceIdType.MESH
NEG = -1e30
LANES = 128
MARK = 1024.0


def nn(a, b):
    return lax.dot_general(a, b, (((1,), (0,)), ((), ())), preferred_element_type=F32)


def nt(a, b):
    return lax.dot_general(a, b, (((1,), (1,)), ((), ())), preferred_element_type=F32)


def kernel(
    S,
    E,
    residual_h,
    kept_index_h,
    kept_count_h,
    projected_h,
    expert_ids_h,
    gate_values_h,
    gate_w,
    up_w,
    down_w,
    cotangent_h,
    output_h,
    input_grad_h,
    b_recv,
    dq_recv,
    gate_grads,
    residual,
    cotangent,
    projected,
    kept_index,
    kept_count,
    expert_ids,
    gate_values,
    io_sem,
    kv_send,
    kv,
    q_send,
    q_recv,
    a_send,
    a_recv,
    g_send,
    g_recv,
    b_send,
    dq_send,
    x_send,
    x_recv,
    y_send,
    y_recv,
    x_rows,
    tile,
    mix,
    wt,
    bias,
    k_t,
    v_t,
    prob,
    att_t,
    acc,
    other,
    send_ss,
    kv_rs,
    q_rs,
    a_rs,
    g_rs,
    b_rs,
    x_rs,
    y_rs,
    rows_rs,
    swap_rs,
    wt_rs,
    core_rs,
):
    Z = S // X
    KEEP = kept_index.shape[1]
    TOK, D = residual.shape
    FF = gate_w.shape[2]
    HEADS = D // HS
    PR = KEEP // 2
    NB = S // QSRC
    KB = QSRC * KEEP
    QB = QSRC * PR
    NS = E * SLOT
    MAIN = FF // (2 * LANES) * LANES
    WIDE = MAIN + LANES
    GU = 2 * MAIN + LANES
    scale = HS**-0.5
    me = lax.axis_index("seq")
    ex = lax.axis_index("exp")
    mx = me // Z
    mz = lax.rem(me, Z)
    yy = ex // 2
    core = lax.rem(ex, 2)
    sib = 1 - core
    grp = mx // 2
    half = lax.rem(mx, 2)
    head = me // 2
    par = lax.rem(me, 2)
    expert = 2 * yy + grp

    def load(i, src, dst):
        return pltpu.make_async_copy(src, dst, io_sem.at[i])

    projected_in = load(0, projected_h, projected)
    cotangent_in = load(1, cotangent_h, cotangent)
    residual_in = load(2, residual_h, residual)
    small_in = (
        load(6, kept_count_h, kept_count),
        load(7, kept_index_h, kept_index),
        load(8, expert_ids_h, expert_ids),
        load(9, gate_values_h, gate_values),
    )
    shared = pl.ds(MAIN, LANES)
    tile_in = (
        load(3, gate_w.at[:, :, shared], tile.at[0]),
        load(4, up_w.at[:, :, shared], tile.at[1]),
    )
    for copy in (projected_in, *tile_in, *small_in, cotangent_in, residual_in):
        copy.start()

    def greet(seq, exp):
        pl.semaphore_signal(
            barrier, inc=1, device_id={"seq": seq, "exp": exp}, device_id_type=MESH
        )

    barrier = pltpu.get_barrier_semaphore()

    def greet_plane(k, t):
        i = lax.rem(2 * me + core + k, 2 * S)
        greet(i // 2, 2 * yy + lax.rem(i, 2))
        return t

    def greet_others(k, t):
        e = lax.rem(2 * yy + 2 + k, E)
        for x in range(X):
            greet(x * Z + mz, e)
        return t

    lax.fori_loop(1, 2 * S, greet_plane, 0)
    lax.fori_loop(0, E - 2, greet_others, 0)

    projected_in.wait()
    for copy in small_in:
        copy.wait()
    count = kept_count[...]
    live_col = lax.broadcasted_iota(jnp.int32, (KEEP, 1), 0) < count
    for h in range(HEADS):
        c0 = h * HS
        keys = projected[:, D + c0 : D + c0 + HS].astype(F32)
        kv_send[2 * h] = jnp.where(live_col, keys, MARK).astype(BF16)
        kv_send[2 * h + 1] = projected[:, 2 * D + c0 : 2 * D + c0 + HS]
        for p in range(2):
            q_send[2 * h + p] = projected[p * PR : (p + 1) * PR, c0 : c0 + HS]

    for copy in tile_in:
        copy.wait()
    tile_lane = lax.broadcasted_iota(jnp.int32, (KEEP, LANES), 1) // (LANES // 2)
    tile_g = tile[0].reshape(KEEP, LANES).astype(F32)
    tile_u = pltpu.roll(tile[1].reshape(KEEP, LANES).astype(F32), LANES // 2, 1)
    for hf in range(2):
        blend = jnp.where(tile_lane == hf, tile_g, tile_u).astype(BF16)
        mix[hf] = blend.reshape(2, KEEP // 2, LANES)
    slot_row = lax.broadcasted_iota(jnp.int32, (NS, KEEP), 0)
    slot_exp = slot_row // SLOT
    slot_pos = slot_row - slot_exp * SLOT
    entry = lax.broadcasted_iota(jnp.int32, (NS, KEEP), 1)
    live = entry < count
    assigned = jnp.zeros((NS, KEEP), F32)
    weight = jnp.zeros((NS, KEEP), F32)
    for k in range(expert_ids.shape[0]):
        match = (expert_ids[k] == slot_exp) & live
        assigned = assigned + jnp.where(match, 1.0, 0.0)
        weight = weight + jnp.where(match, gate_values[k], 0.0)
    ei = lax.broadcasted_iota(jnp.int32, (KEEP, KEEP), 0)
    ej = lax.broadcasted_iota(jnp.int32, (KEEP, KEEP), 1)
    earlier = jnp.where(ei < ej, 1.0, 0.0).astype(BF16)
    rank = nn(assigned.astype(BF16), earlier)
    table = jnp.where((assigned > 0.5) & (rank == slot_pos.astype(F32)), 1.0, 0.0)
    table_half = table.astype(BF16)
    weighted = table * weight
    slot_gate = jnp.sum(weighted, axis=1, keepdims=True)

    def turned(a):
        if a.shape[1] < 128:
            a = jnp.concatenate([a, jnp.zeros((a.shape[0], 128 - a.shape[1]), F32)], 1)
        return a.T

    table_t = turned(table)[:KEEP].astype(BF16)
    weighted_t = turned(weighted)[:KEEP]
    w_high = weighted_t.astype(BF16)
    w_low = (weighted_t - w_high.astype(F32)).astype(BF16)

    KC = Z * KEEP
    NR = 2 * NS
    fr = lax.broadcasted_iota(jnp.int32, (NR, NR), 0)
    fc = lax.broadcasted_iota(jnp.int32, (NR, NR), 1)
    spot = lax.rem(fr, SLOT)
    fold, unfold = [], []
    for g in range(FOLDS):
        gap = CAP - 4 * g
        fold.append(jnp.where((spot >= CAP) & (fc == fr - gap), 1.0, 0.0).astype(BF16))
        unfold.append(jnp.where((spot // 4 == g) & (fc == fr + gap), 1.0, 0.0).astype(BF16))

    def quarter(g):
        return slice(g * KC, (g + 1) * KC)

    def pack(ref, g, chunk, last):
        n = chunk.shape[0]
        full = chunk + nn(fold[g][:n, :n], last)
        ref[:, :, quarter(g)] = full.astype(BF16).reshape(n // SLOT, SLOT, KC)

    def pack_all(ref, rows):
        for g in range(FOLDS):
            pack(ref, g, rows[:, quarter(g)], rows[:, quarter(FOLDS)].astype(BF16))

    cotangent_in.wait()
    residual_in.wait()
    index_row = kept_index[...]
    index_col = jnp.sum(jnp.where(ei == ej, index_row, 0), axis=1, keepdims=True)
    pick = jnp.where(
        lax.broadcasted_iota(jnp.int32, (KEEP, TOK), 1) == index_col, 1.0, 0.0
    ).astype(BF16)
    grad_f = nn(pick, cotangent[...])
    kept_f = nn(pick, residual[...])
    grad_sel = nn(table_half, grad_f.astype(BF16))
    pack_all(x_send.at[0], (slot_gate * grad_sel).astype(BF16).astype(F32))
    grad_sel = grad_sel.astype(BF16)
    pl.semaphore_wait(barrier, 2 * S - 1 + X * (E - 2))

    def remote(src, dst, ss, rs, seq, exp):
        return pltpu.make_async_remote_copy(
            src_ref=src,
            dst_ref=dst,
            send_sem=ss,
            recv_sem=rs,
            device_id={"seq": seq, "exp": exp},
            device_id_type=MESH,
        )

    def landed(view, sem):
        remote(view, view, send_ss.at[0], sem, me, 2 * yy + sib).wait_recv()

    def left(n, view):
        remote(view, view, send_ss.at[n], q_rs.at[0], me, 2 * yy + sib).wait_send()

    def left_all(n, ref):
        @pl.when(par == core)
        def _():
            left(n, ref.at[pl.ds(0, S - 1)])

        @pl.when(par != core)
        def _():
            left(n, ref)

    here = 2 * head + core

    col_x = [lax.rem(mx + o, X) for o in range(X)]
    row_z = [lax.rem(mz + o, Z) for o in range(Z)]

    def unless_own(maybe, do, *args):
        if maybe is None:
            do(*args)
        else:
            pl.when(maybe)(lambda: do(*args))

    def each_head(do):
        for q in range(Z // 2):
            for o, x in enumerate(col_x):
                h = x * (Z // 2) + lax.rem(x + q, Z // 2)
                for p in range(2):
                    away = None if o else (h != head) | (par != core) | (core != p)
                    unless_own(away, do, 2 * h + p, h, p)

    def each_source(do, x0=None):
        for o, x in enumerate(col_x) if x0 is None else ((0, x0),):
            for k, z in enumerate(row_z):
                away = None if o or k else (x != mx) | (par != core)
                unless_own(away, do, x * Z + z)

    def kv_copy(i, h, p):
        return remote(
            kv_send.at[i], kv.at[p, me], send_ss.at[0], kv_rs.at[me // QSRC], 2 * h + core, 2 * yy + p
        )

    def head_copy(n, send, recv, rs, i, h, p):
        return remote(send.at[i], recv.at[me], send_ss.at[n], rs, 2 * h + core, 2 * yy + p)

    def source_copy(n, send, recv, rs, d):
        return remote(send.at[d], recv.at[here], send_ss.at[n], rs, d, 2 * yy + par)

    def own_copy(src, dst, sem):
        @pl.when(par == core)
        def _():
            pltpu.make_async_copy(src, dst, sem).start()

    def each_expert(do):
        def step(k, t):
            e = lax.rem(ex + k, E)
            for hf in range(2):
                x = 2 * lax.rem(e, 2) + hf

                @pl.when((e != expert) | (hf != half) | (core != grp))
                def _():
                    do(e, x * Z + mz, 2 * (e // 2) + grp)

            return t

        lax.fori_loop(0, E, step, 0)

    def each_list(do):
        def step(k, t):
            b = lax.rem(ex + k, E)
            for r in range(2):
                x = 2 * core + r

                @pl.when((b != ex) | (x != mx))
                def _():
                    do(r * E + b, x * Z + mz, b)

            return t

        lax.fori_loop(0, E, step, 0)

    def out_start(n):
        slot = half * E + ex

        @pl.when(core == grp)
        def _():
            pltpu.make_async_copy(x_send.at[n, expert], x_recv.at[n, slot], x_rs.at[n]).start()

        each_expert(
            lambda e, seq, exp: remote(
                x_send.at[n, e], x_recv.at[n, slot], send_ss.at[6 + n], x_rs.at[n], seq, exp
            ).start()
        )

    def x_landed(n):
        landed(x_recv.at[n], x_rs.at[n])

    def part_cols(c):
        return pl.ds(c * Z * KEEP, Z * KEEP)

    def back_start(n, cols, ss, rs):
        slot = half * E + expert

        @pl.when(core == grp)
        def _():
            pltpu.make_async_copy(
                y_send.at[n, half * E + ex, :, cols], y_recv.at[n, slot, :, cols], rs
            ).start()

        each_list(
            lambda i, seq, exp: remote(
                y_send.at[n, i, :, cols], y_recv.at[n, slot, :, cols], ss, rs, seq, exp
            ).start()
        )

    def sixteen_left(n, ref, cols):
        @pl.when(core == grp)
        def _():
            left(n, ref.at[pl.ds(0, 2 * E - 1), :, cols])

        @pl.when(core != grp)
        def _():
            left(n, ref.at[:, :, cols])

    RING, CORE, INIT = 13, 14, 15
    part_all = pl.ds(0, FOLDS * Z * KEEP)

    def at_z(o):
        return lax.rem(mz + o + Z, Z)

    def arrival(w, oz, part):
        return wt_rs.at[w, oz % Z if part != 1 else Z]

    def piece(w, oz, part, group, seq, exp, sem):
        view = wt.at[2 * core + w, at_z(oz)]
        if part is not None:
            view = wt.at[2 * core + w, at_z(oz), part]
        return remote(view, view, send_ss.at[group], sem, seq, exp)

    def wait(w, oz, parts):
        for part in (0, 1) if parts else (None,):
            piece(w, oz, part, RING, me, 2 * yy + sib, arrival(w, oz, part)).wait_recv()

    both = (1, -1)

    def hop(w, sgn, k):
        if k < Z // 2:
            part = None if k < Z // 2 - 1 else (0 if sgn > 0 else 1)
            sem = arrival(w, -sgn * (k + 1), part)
            piece(w, -sgn * k, part, RING, mx * Z + at_z(sgn), ex, sem).start()

    def to_core(w, oz):
        piece(w, oz, None, CORE, me, 2 * yy + sib, core_rs.at[w]).start()

    def along_z(k):
        for w in (0, 1):
            if k == Z // 2:
                wait(w, k, True)
                to_core(w, k)
            else:
                for s in both:
                    wait(w, -s * k, False)
                    hop(w, s, k)
                    to_core(w, -s * k)

    def init_start():
        for hf in range(2):
            x = 2 * core + hf
            main = pl.ds(hf * WIDE, MAIN)
            parts = (
                (gate_w.at[:, :, main], 0, MAIN),
                (up_w.at[:, :, main], MAIN, MAIN),
                (mix.at[hf], 2 * MAIN, LANES),
                (down_w.at[:, :, main], GU, MAIN),
                (down_w.at[:, :, shared], GU + MAIN, LANES),
            )
            for src, at, n in parts:
                dst, sem = wt.at[mx, mz, :, :, pl.ds(at, n)], wt_rs.at[half, 0]

                @pl.when((x == mx) & (core == grp))
                def _():
                    pltpu.make_async_copy(src, dst, sem).start()

                @pl.when((x != mx) | (core != grp))
                def _():
                    seq = x * Z + mz
                    remote(src, dst, send_ss.at[INIT], sem, seq, 2 * yy + grp).start()

    init_start()
    own_copy(kv_send.at[here], kv.at[core, me], kv_rs.at[me // QSRC])
    own_copy(q_send.at[here], q_recv.at[me], q_rs.at[0])
    each_head(lambda *i: kv_copy(*i).start())
    each_head(lambda *i: head_copy(1, q_send, q_recv, q_rs.at[0], *i).start())

    for w in (0, 1):
        landed(wt.at[2 * core + w, mz], wt_rs.at[w, 0])
        for s in both:
            hop(w, s, 0)
        to_core(w, 0)
    out_start(0)

    along_z(1)
    def swap_copy(b):
        view = kv.at[core, pl.ds(b * QSRC, QSRC)]
        return remote(view, view, send_ss.at[16], swap_rs.at[0, b], me, 2 * yy + sib)

    for b in range(NB):
        landed(kv.at[core, pl.ds(b * QSRC, QSRC)], kv_rs.at[b])
        swap_copy(b).start()
    landed(q_recv, q_rs.at[0])
    for b in range(NB):
        landed(kv.at[sib, pl.ds(b * QSRC, QSRC)], swap_rs.at[0, b])

    def key_block(c):
        return kv[0, c * QSRC : (c + 1) * QSRC].reshape(KB, HS)

    def value_block(c):
        return kv[1, c * QSRC : (c + 1) * QSRC].reshape(KB, HS)

    def query_block(b):
        return q_recv[b * QSRC : (b + 1) * QSRC].reshape(QB, HS)

    for b in range(NB):
        k_f = key_block(b).astype(F32)
        bias[b * KB : (b + 1) * KB] = jnp.where(k_f > MARK / 2, NEG, 0.0)
        k_t[:, b * KB : (b + 1) * KB] = k_f.T.astype(BF16)
        v_t[:, b * KB : (b + 1) * KB] = value_block(b).astype(F32).T.astype(BF16)

    qcol = lax.broadcasted_iota(jnp.int32, (KB, QB), 1)
    qent = (qcol // PR) * KEEP + core * PR + lax.rem(qcol, PR)
    causal = lax.broadcasted_iota(jnp.int32, (KB, QB), 0) <= qent

    def forward_block(b):
        cols = slice(b * QB, (b + 1) * QB)
        q_blk = query_block(b)
        top = None
        for c in range(b + 1):
            rows = slice(c * KB, (c + 1) * KB)
            half = bias[rows, :]
            sc = nt(key_block(c), q_blk) * scale + jnp.concatenate([half] * (QB // HS), 1)
            if c == b:
                sc = jnp.where(causal, sc, NEG)
            prob[rows, cols] = sc
            m = jnp.max(sc, axis=0, keepdims=True)
            top = m if top is None else jnp.maximum(top, m)
        total = jnp.zeros((1, QB), F32)
        for c in range(b + 1):
            rows = slice(c * KB, (c + 1) * KB)
            e = jnp.exp(prob[rows, cols] - top)
            prob[rows, cols] = e
            total = total + jnp.sum(e, axis=0, keepdims=True)
        inv = 1.0 / total
        out = jnp.zeros((HS, QB), F32)
        for c in range(b + 1):
            rows = slice(c * KB, (c + 1) * KB)
            pr = prob[rows, cols] * inv
            prob[rows, cols] = pr
            out = out + nn(v_t[:, rows], pr.astype(BF16))
        att_t[:, cols] = out
        a_send[b * QSRC : (b + 1) * QSRC] = out.T.astype(BF16).reshape(QSRC, PR, HS)
        each_source(
            lambda d: source_copy(2, a_send, a_recv, a_rs.at[0], d).start(), b
        )

    for b in range(NB):
        forward_block(b)
    own_copy(a_send.at[me], a_recv.at[here], a_rs.at[0])
    along_z(2)
    landed(a_recv, a_rs.at[0])

    attended = jnp.concatenate(
        [jnp.concatenate([a_recv[2 * h + p] for h in range(HEADS)], 1) for p in range(2)], 0
    )
    h1 = jnp.where(live_col, kept_f + attended.astype(F32), 0.0)
    inv_rms = lax.rsqrt(jnp.mean(h1 * h1, axis=1, keepdims=True) + EPSILON)
    normed = (h1 * inv_rms).astype(BF16)
    pack_all(x_send.at[1], nn(table_half, normed))
    out_start(1)
    pre = [jnp.zeros((NR, GU), F32), jnp.zeros((NR, WIDE), F32)]

    def gate_up_of(ax):
        return wt[ax, :, :, :, 0:GU].reshape(KC, GU)

    def down_of(ax):
        return wt[ax, :, :, :, GU:].reshape(KC, WIDE)

    def expert_chunk(ax):
        cols = pl.ds(pl.multiple_of(ax * KC, KC), KC)
        pre[0] = pre[0] + nn(x_rows[1, :, cols], gate_up_of(ax))
        pre[1] = pre[1] + nn(x_rows[0, :, cols], down_of(ax))

    along_z(3)
    x_landed(0)
    x_landed(1)
    used = lax.rem(lax.broadcasted_iota(jnp.int32, (NR, KC), 0), SLOT) < CAP
    for n in (0, 1):
        last = jnp.zeros((NR, KC), F32)
        for g in range(FOLDS):
            chunk = x_recv[n, :, :, quarter(g)].reshape(NR, KC)
            last = last + nn(unfold[g], chunk)
            x_rows[n, :, quarter(g)] = jnp.where(used, chunk.astype(F32), 0.0).astype(BF16)
        x_rows[n, :, quarter(FOLDS)] = last.astype(BF16)
    along_z(Z // 2)
    for w in (0, 1):
        expert_chunk(2 * core + w)
    for w in (0, 1):
        landed(wt.at[2 * sib + w], core_rs.at[w])
        expert_chunk(2 * sib + w)
    ahead, mid_grad = pre
    turned_tile = pltpu.roll(ahead[:, 2 * MAIN :], LANES // 2, 1)
    gate_pre = jnp.concatenate([ahead[:, :MAIN], ahead[:, 2 * MAIN :]], 1)
    up_pre = jnp.concatenate([ahead[:, MAIN : 2 * MAIN], turned_tile], 1)
    sig = 1.0 / (1.0 + jnp.exp(-gate_pre))
    act = gate_pre * sig
    lane = lax.broadcasted_iota(jnp.int32, (NR, WIDE), 1)
    own = (lane < MAIN) | ((lane - MAIN) // (LANES // 2) == half)
    mid_grad = jnp.where(own, mid_grad, 0.0)
    gate_grad = mid_grad * up_pre * sig * (1.0 + gate_pre * (1.0 - sig))
    up_grad = mid_grad * act
    turned_tile = pltpu.roll(up_grad[:, MAIN:], LANES // 2, 1)
    behind = jnp.concatenate(
        [gate_grad[:, :MAIN], up_grad[:, :MAIN], gate_grad[:, MAIN:] + turned_tile], 1
    ).astype(BF16)
    mid = jnp.where(own, act * up_pre, 0.0).astype(BF16)
    def back_of(c):
        return nt(gate_up_of(c), behind).T

    last = back_of(FOLDS).astype(BF16)
    for g in range(FOLDS):
        pack(y_send.at[0], g, back_of(g), last)
        back_start(0, part_cols(g), send_ss.at[9 + g], rows_rs.at[g])
    last = nt(down_of(FOLDS), mid).T.astype(BF16)
    for g in range(FOLDS):
        pack(y_send.at[1], g, nt(down_of(g), mid).T, last)
    table_t = jnp.concatenate([table_t, table_t], 1)
    parts, last = [], jnp.zeros((KEEP, KC), F32)
    for g in range(FOLDS):
        landed(y_recv.at[0, :, :, part_cols(g)], rows_rs.at[g])
        chunk = y_recv[0, :, :, quarter(g)].reshape(NR, KC)
        parts.append(nn(table_t, chunk))
        last = last + nn(nt(table_t, fold[g]).astype(BF16), chunk)
    parts.append(last)
    normed_grad = jnp.concatenate(parts, 1)
    cubed = inv_rms * inv_rms * inv_rms
    h1_grad = (
        grad_f
        + inv_rms * normed_grad
        - h1 * cubed * jnp.mean(normed_grad * h1, axis=1, keepdims=True)
    )
    h1_grad = jnp.where(live_col, h1_grad, 0.0).astype(BF16)
    for h in range(HEADS):
        for p in range(2):
            g_send[2 * h + p] = h1_grad[p * PR : (p + 1) * PR, h * HS : (h + 1) * HS]
    own_copy(g_send.at[here], g_recv.at[me], g_rs.at[me // QSRC])
    each_head(lambda *i: head_copy(3, g_send, g_recv, g_rs.at[me // QSRC], *i).start())

    token = lax.broadcasted_iota(jnp.int32, (TOK, KEEP), 0)
    put = jnp.where(
        (token == index_row) & (lax.broadcasted_iota(jnp.int32, (TOK, KEEP), 1) < count),
        1.0,
        0.0,
    )
    replaced = jnp.sum(put, axis=1, keepdims=True) > 0.5
    put = put.astype(BF16)
    cotangent[...] = jnp.where(replaced, nn(put, h1_grad), cotangent[...].astype(F32)).astype(
        BF16
    )
    input_grad_out = load(0, cotangent, input_grad_h)
    input_grad_out.start()
    back_start(1, part_all, send_ss.at[8], y_rs.at[0])

    def give_copy(c):
        rows = pl.ds(c * KB, KB)
        return remote(
            acc.at[sib, rows],
            other.at[rows],
            send_ss.at[17],
            swap_rs.at[1, c],
            me,
            2 * yy + sib,
        )

    def finish_block(c):
        rows = slice(c * KB, (c + 1) * KB)
        landed(other.at[pl.ds(c * KB, KB)], swap_rs.at[1, c])
        whole = acc[core, rows] + other[rows]
        b_send[c * QSRC : (c + 1) * QSRC] = whole.astype(BF16).reshape(QSRC, KEEP, HS)
        each_source(
            lambda d: source_copy(4, b_send, b_recv, b_rs.at[0], d).start(), c
        )

    dout = [None] * NB
    delta = [None] * NB
    dq_t = [jnp.zeros((HS, QB), F32)] * NB
    for c in reversed(range(NB)):
        rows = slice(c * KB, (c + 1) * KB)
        block = pl.ds(c * QSRC, QSRC)
        landed(g_recv.at[block], g_rs.at[c])
        dout[c] = g_recv[c * QSRC : (c + 1) * QSRC].reshape(QB, HS)
        turn = dout[c].astype(F32).T * att_t[:, c * QB : (c + 1) * QB]
        delta[c] = jnp.sum(turn, axis=0, keepdims=True)
        dk = jnp.zeros((KB, HS), F32)
        dv = jnp.zeros((KB, HS), F32)
        for b in range(c, NB):
            pr = prob[rows, b * QB : (b + 1) * QB]
            ds = (pr * (nt(value_block(c), dout[b]) - delta[b]) * scale).astype(BF16)
            dq_t[b] = dq_t[b] + nn(k_t[:, rows], ds)
            dk = dk + nn(ds, query_block(b))
            dv = dv + nn(pr.astype(BF16), dout[b])
        acc[0, rows] = dk
        acc[1, rows] = dv
        give_copy(c).start()
        if c < NB - 1:
            finish_block(c + 1)
    for b in range(NB):
        dq_send[b * QSRC : (b + 1) * QSRC] = dq_t[b].T.astype(BF16).reshape(QSRC, PR, HS)
    each_source(lambda d: source_copy(5, dq_send, dq_recv, b_rs.at[1], d).start())
    finish_block(0)
    own_copy(dq_send.at[me], dq_recv.at[here], b_rs.at[1])
    own_copy(b_send.at[me], b_recv.at[here], b_rs.at[0])

    landed(y_recv.at[1], y_rs.at[0])
    parts, last = [], jnp.zeros((KEEP, KC), F32)
    made_last = jnp.zeros((NR, KC), F32)
    per_slot = jnp.zeros((NS, 1), F32)

    def against(rows, g):
        both_halves = (rows[:NS] + rows[NS:]) * grad_sel[:, quarter(g)].astype(F32)
        return jnp.sum(both_halves, axis=1, keepdims=True)

    for g in range(FOLDS):
        chunk = y_recv[1, :, :, quarter(g)].reshape(NR, KC)
        there = jnp.zeros((KEEP, KC), F32)
        for w in (w_high, w_low):
            w = jnp.concatenate([w, w], 1)
            there = there + nn(w, chunk)
            last = last + nn(nt(w, fold[g]).astype(BF16), chunk)
        parts.append(there)
        made_last = made_last + nn(unfold[g], chunk)
        per_slot = per_slot + against(chunk.astype(F32), g)
    per_slot = per_slot + against(made_last, FOLDS)
    mixture = jnp.concatenate(parts + [last], 1)
    new_rows = (h1 + mixture).astype(BF16)
    residual[...] = jnp.where(replaced, nn(put, new_rows), residual[...].astype(F32)).astype(BF16)
    spread = table * per_slot
    for k in range(expert_ids.shape[0]):
        hit = expert_ids[k] == slot_exp
        gate_grads[k] = jnp.sum(jnp.where(hit, spread, 0.0), axis=0, keepdims=True)
    output_out = load(1, residual, output_h)
    output_out.start()
    left_all(0, kv_send)
    left_all(1, q_send)
    left_all(2, a_send)
    left_all(3, g_send)
    for n in (0, 1):
        sixteen_left(6 + n, x_recv.at[n], part_all)
    sixteen_left(8, y_send.at[1], part_all)
    for c in range(FOLDS):
        sixteen_left(9 + c, y_send.at[0], part_cols(c))
    left(RING, wt.at[pl.ds(0, 2), pl.ds(0, Z - 1)])
    left(CORE, wt.at[pl.ds(0, 2)])
    left(16, kv.at[core])
    left(17, acc.at[sib])

    @pl.when(core == grp)
    def _():
        left(INIT, wt.at[0, 0])

    @pl.when(core != grp)
    def _():
        left(INIT, wt.at[0, pl.ds(0, 2)])

    landed(b_recv, b_rs.at[0])
    landed(dq_recv, b_rs.at[1])
    left_all(4, b_send)
    left_all(5, dq_send)
    for copy in (input_grad_out, output_out):
        copy.wait()


def finish(a, b, c, e, d, out_a, out_b, out_c, out_d, sa, sb, sc, se, sd, sp, sem):
    heads, _, width = c.shape
    rows = e.shape[1]
    ins, outs = [], []
    pairs = ((c, sc, None), (e, se, None), (a, sa, out_a.at[0]), (b, sb, out_b.at[0]), (d, sd, out_d))
    for i, (src, stage, dst) in enumerate(pairs):
        ins.append(pltpu.make_async_copy(src, stage, sem.at[0, i]))
        if dst is not None:
            outs.append(pltpu.make_async_copy(stage, dst, sem.at[1, i]))
    for copy in ins:
        copy.start()
    for copy in ins[:2]:
        copy.wait()
    for i in range(heads):
        c0, p = i // 2 * width, i % 2
        o = (1 + p) * (heads // 2) * width + c0
        sp[p * rows : (p + 1) * rows, c0 : c0 + width] = se[i]
        sp[:, o : o + width] = sc[i]
    outs.append(pltpu.make_async_copy(sp, out_c.at[0], sem.at[1, 0]))
    outs[-1].start()
    for copy, after in zip(ins[2:], outs):
        copy.wait()
        after.start()
    for copy in outs:
        copy.wait()


def body(
    residual,
    kept_index,
    kept_count,
    projected,
    expert_ids,
    gate_values,
    gate_weight,
    up_weight,
    down_weight,
    cotangent,
):
    S = lax.axis_size("seq")
    E = lax.axis_size("exp")
    _, TOK, D = residual.shape
    KEEP = kept_index.shape[1]
    FF = gate_weight.shape[2]
    TOPK = expert_ids.shape[2]
    Z = S // X
    HEADS = D // HS
    PR = KEEP // 2
    NB = S // QSRC
    vm = pl.BlockSpec(memory_space=pltpu.VMEM)
    hbm = pl.BlockSpec(memory_space=pl.ANY)
    dma = pltpu.SemaphoreType.DMA
    out = pl.pallas_call(
        functools.partial(kernel, S, E),
        out_shape=[
            jax.ShapeDtypeStruct((TOK, D), BF16),
            jax.ShapeDtypeStruct((TOK, D), BF16),
            jax.ShapeDtypeStruct((S, KEEP, HS), BF16),
            jax.ShapeDtypeStruct((S, PR, HS), BF16),
            jax.ShapeDtypeStruct((TOPK, 1, KEEP), F32),
        ],
        in_specs=[hbm] * 10,
        out_specs=[hbm, hbm, hbm, hbm, vm],
        scratch_shapes=[
            pltpu.VMEM((TOK, D), BF16),
            pltpu.VMEM((TOK, D), BF16),
            pltpu.VMEM((KEEP, 3 * D), BF16),
            pltpu.VMEM((1, KEEP), jnp.int32),
            pltpu.VMEM((1, 1), jnp.int32),
            pltpu.VMEM((TOPK, 1, KEEP), jnp.int32),
            pltpu.VMEM((TOPK, 1, KEEP), F32),
            dma((10,)),
            pltpu.VMEM((S, KEEP, HS), BF16),
            pltpu.VMEM((2, S, KEEP, HS), BF16),
            pltpu.VMEM((S, PR, HS), BF16),
            pltpu.VMEM((S, PR, HS), BF16),
            pltpu.VMEM((S, PR, HS), BF16),
            pltpu.VMEM((S, PR, HS), BF16),
            pltpu.VMEM((S, PR, HS), BF16),
            pltpu.VMEM((S, PR, HS), BF16),
            pltpu.VMEM((S, KEEP, HS), BF16),
            pltpu.VMEM((S, PR, HS), BF16),
            pltpu.VMEM((2, E, SLOT, D * CAP // SLOT), BF16),
            pltpu.VMEM((2, 2 * E, SLOT, D * CAP // SLOT), BF16),
            pltpu.VMEM((2, 2 * E, SLOT, D * CAP // SLOT), BF16),
            pltpu.VMEM((2, 2 * E, SLOT, D * CAP // SLOT), BF16),
            pltpu.VMEM((2, 2 * E * SLOT, D), BF16),
            pltpu.VMEM((2, 2, KEEP // 2, LANES), BF16),
            pltpu.VMEM((2, 2, KEEP // 2, LANES), BF16),
            pltpu.VMEM((X, Z, 2, KEEP // 2, FF // LANES // 2 * LANES * 3 + 2 * LANES), BF16),
            pltpu.VMEM((S * KEEP, HS), F32),
            pltpu.VMEM((HS, S * KEEP), BF16),
            pltpu.VMEM((HS, S * KEEP), BF16),
            pltpu.VMEM((S * KEEP, S * PR), F32),
            pltpu.VMEM((HS, S * PR), F32),
            pltpu.VMEM((2, S * KEEP, HS), F32),
            pltpu.VMEM((S * KEEP, HS), F32),
        ]
        + [
            dma((18,)),
            dma((NB,)),
            dma((1,)),
            dma((1,)),
            dma((NB,)),
            dma((2,)),
            dma((2,)),
            dma((1,)),
            dma((X,)),
            dma((2, NB)),
            dma((2, Z + 1)),
            dma((2,)),
        ],
        compiler_params=pltpu.CompilerParams(
            collective_id=0, has_side_effects=True, vmem_limit_bytes=60 * 1024 * 1024
        ),
    )(
        residual[0],
        kept_index,
        kept_count,
        projected[0],
        jnp.transpose(expert_ids, (2, 0, 1)),
        jnp.transpose(gate_values, (2, 0, 1)),
        gate_weight[0].reshape(2, KEEP // 2, FF),
        up_weight[0].reshape(2, KEEP // 2, FF),
        down_weight[0].T.reshape(2, KEEP // 2, FF),
        cotangent[0],
    )
    out = pl.pallas_call(
        finish,
        out_shape=[
            jax.ShapeDtypeStruct((1, TOK, D), BF16),
            jax.ShapeDtypeStruct((1, TOK, D), BF16),
            jax.ShapeDtypeStruct((1, KEEP, 3 * D), BF16),
            jax.ShapeDtypeStruct((TOPK, 1, KEEP), F32),
        ],
        in_specs=[hbm] * 5,
        out_specs=[hbm] * 4,
        scratch_shapes=[
            pltpu.VMEM((TOK, D), BF16),
            pltpu.VMEM((TOK, D), BF16),
            pltpu.VMEM((S, KEEP, HS), BF16),
            pltpu.VMEM((S, PR, HS), BF16),
            pltpu.VMEM((TOPK, 1, KEEP), F32),
            pltpu.VMEM((KEEP, 3 * D), BF16),
            dma((2, 5)),
        ],
        compiler_params=pltpu.CompilerParams(vmem_limit_bytes=60 * 1024 * 1024),
    )(*out)
    return (out[0], out[1], out[2], jnp.transpose(out[3], (1, 2, 0)))


def solution(mesh):
    row = P("exp", "seq", None)
    in_specs = (row, P("exp", "seq"), P("exp", "seq")) + (row,) * 5 + (P("exp", None, "seq"), row)
    return jax.shard_map(
        body, mesh=mesh, in_specs=in_specs, out_specs=(row,) * 4, check_vma=False
    )
```

```python
import functools

import jax
import jax.numpy as jnp
from jax import lax
from jax.experimental import pallas as pl
from jax.experimental.pallas import tpu as pltpu
from jax.sharding import PartitionSpec as P

HS = 128
SLOT = 16
CAP = 12
FOLDS = 3
EPSILON = 1e-06
X = 4
QSRC = 8
F32 = jnp.float32
BF16 = jnp.bfloat16
MESH = pl.DeviceIdType.MESH
NEG = -1e30
LANES = 128
MARK = 1024.0


def nn(a, b):
    return lax.dot_general(a, b, (((1,), (0,)), ((), ())), preferred_element_type=F32)


def nt(a, b):
    return lax.dot_general(a, b, (((1,), (1,)), ((), ())), preferred_element_type=F32)


def kernel(
    S,
    E,
    residual_h,
    kept_index_h,
    kept_count_h,
    projected_h,
    expert_ids_h,
    gate_values_h,
    gate_w,
    up_w,
    down_w,
    cotangent_h,
    output_h,
    input_grad_h,
    b_recv,
    dq_recv,
    gate_grads,
    residual,
    cotangent,
    projected,
    kept_index,
    kept_count,
    expert_ids,
    gate_values,
    io_sem,
    kv_send,
    kv,
    q_send,
    q_recv,
    a_send,
    a_recv,
    g_send,
    g_recv,
    b_send,
    dq_send,
    x_send,
    x_recv,
    y_send,
    y_recv,
    x_rows,
    tile,
    mix,
    wt,
    bias,
    k_t,
    v_t,
    prob,
    att_t,
    acc,
    other,
    send_ss,
    kv_rs,
    q_rs,
    a_rs,
    g_rs,
    b_rs,
    x_rs,
    y_rs,
    rows_rs,
    swap_rs,
    wt_rs,
    core_rs,
):
    Z = S // X
    KEEP = kept_index.shape[1]
    TOK, D = residual.shape
    FF = gate_w.shape[2]
    HEADS = D // HS
    PR = KEEP // 2
    NB = S // QSRC
    KB = QSRC * KEEP
    QB = QSRC * PR
    NS = E * SLOT
    MAIN = FF // (2 * LANES) * LANES
    WIDE = MAIN + LANES
    GU = 2 * MAIN + LANES
    scale = HS**-0.5
    me = lax.axis_index("seq")
    ex = lax.axis_index("exp")
    mx = me // Z
    mz = lax.rem(me, Z)
    yy = ex // 2
    core = lax.rem(ex, 2)
    sib = 1 - core
    grp = mx // 2
    half = lax.rem(mx, 2)
    head = me // 2
    par = lax.rem(me, 2)
    expert = 2 * yy + grp

    def load(i, src, dst):
        return pltpu.make_async_copy(src, dst, io_sem.at[i])

    projected_in = load(0, projected_h, projected)
    cotangent_in = load(1, cotangent_h, cotangent)
    residual_in = load(2, residual_h, residual)
    small_in = (
        load(6, kept_count_h, kept_count),
        load(7, kept_index_h, kept_index),
        load(8, expert_ids_h, expert_ids),
        load(9, gate_values_h, gate_values),
    )
    shared = pl.ds(MAIN, LANES)
    tile_in = (
        load(3, gate_w.at[:, :, shared], tile.at[0]),
        load(4, up_w.at[:, :, shared], tile.at[1]),
    )
    for copy in (projected_in, *tile_in, *small_in, cotangent_in, residual_in):
        copy.start()

    def greet(seq, exp):
        pl.semaphore_signal(
            barrier, inc=1, device_id={"seq": seq, "exp": exp}, device_id_type=MESH
        )

    barrier = pltpu.get_barrier_semaphore()

    def greet_plane(k, t):
        i = lax.rem(2 * me + core + k, 2 * S)
        greet(i // 2, 2 * yy + lax.rem(i, 2))
        return t

    def greet_others(k, t):
        e = lax.rem(2 * yy + 2 + k, E)
        for x in range(X):
            greet(x * Z + mz, e)
        return t

    lax.fori_loop(1, 2 * S, greet_plane, 0)
    lax.fori_loop(0, E - 2, greet_others, 0)

    projected_in.wait()
    for copy in small_in:
        copy.wait()
    count = kept_count[...]
    live_col = lax.broadcasted_iota(jnp.int32, (KEEP, 1), 0) < count
    for h in range(HEADS):
        c0 = h * HS
        keys = projected[:, D + c0 : D + c0 + HS].astype(F32)
        kv_send[2 * h] = jnp.where(live_col, keys, MARK).astype(BF16)
        kv_send[2 * h + 1] = projected[:, 2 * D + c0 : 2 * D + c0 + HS]
        for p in range(2):
            q_send[2 * h + p] = projected[p * PR : (p + 1) * PR, c0 : c0 + HS]

    for copy in tile_in:
        copy.wait()
    tile_lane = lax.broadcasted_iota(jnp.int32, (KEEP, LANES), 1) // (LANES // 2)
    tile_g = tile[0].reshape(KEEP, LANES).astype(F32)
    tile_u = pltpu.roll(tile[1].reshape(KEEP, LANES).astype(F32), LANES // 2, 1)
    for hf in range(2):
        blend = jnp.where(tile_lane == hf, tile_g, tile_u).astype(BF16)
        mix[hf] = blend.reshape(2, KEEP // 2, LANES)
    slot_row = lax.broadcasted_iota(jnp.int32, (NS, KEEP), 0)
    slot_exp = slot_row // SLOT
    slot_pos = slot_row - slot_exp * SLOT
    entry = lax.broadcasted_iota(jnp.int32, (NS, KEEP), 1)
    live = entry < count
    assigned = jnp.zeros((NS, KEEP), F32)
    weight = jnp.zeros((NS, KEEP), F32)
    for k in range(expert_ids.shape[0]):
        match = (expert_ids[k] == slot_exp) & live
        assigned = assigned + jnp.where(match, 1.0, 0.0)
        weight = weight + jnp.where(match, gate_values[k], 0.0)
    ei = lax.broadcasted_iota(jnp.int32, (KEEP, KEEP), 0)
    ej = lax.broadcasted_iota(jnp.int32, (KEEP, KEEP), 1)
    earlier = jnp.where(ei < ej, 1.0, 0.0).astype(BF16)
    rank = nn(assigned.astype(BF16), earlier)
    table = jnp.where((assigned > 0.5) & (rank == slot_pos.astype(F32)), 1.0, 0.0)
    table_half = table.astype(BF16)
    weighted = table * weight
    slot_gate = jnp.sum(weighted, axis=1, keepdims=True)

    def turned(a):
        if a.shape[1] < 128:
            a = jnp.concatenate([a, jnp.zeros((a.shape[0], 128 - a.shape[1]), F32)], 1)
        return a.T

    table_t = turned(table)[:KEEP].astype(BF16)
    weighted_t = turned(weighted)[:KEEP]
    w_high = weighted_t.astype(BF16)
    w_low = (weighted_t - w_high.astype(F32)).astype(BF16)

    KC = Z * KEEP
    NR = 2 * NS
    fr = lax.broadcasted_iota(jnp.int32, (NR, NR), 0)
    fc = lax.broadcasted_iota(jnp.int32, (NR, NR), 1)
    spot = lax.rem(fr, SLOT)
    fold, unfold = [], []
    for g in range(FOLDS):
        gap = CAP - 4 * g
        fold.append(jnp.where((spot >= CAP) & (fc == fr - gap), 1.0, 0.0).astype(BF16))
        unfold.append(jnp.where((spot // 4 == g) & (fc == fr + gap), 1.0, 0.0).astype(BF16))

    def quarter(g):
        return slice(g * KC, (g + 1) * KC)

    def pack(ref, g, chunk, last):
        n = chunk.shape[0]
        full = chunk + nn(fold[g][:n, :n], last)
        ref[:, :, quarter(g)] = full.astype(BF16).reshape(n // SLOT, SLOT, KC)

    def pack_all(ref, rows):
        for g in range(FOLDS):
            pack(ref, g, rows[:, quarter(g)], rows[:, quarter(FOLDS)].astype(BF16))

    cotangent_in.wait()
    residual_in.wait()
    index_row = kept_index[...]
    index_col = jnp.sum(jnp.where(ei == ej, index_row, 0), axis=1, keepdims=True)
    pick = jnp.where(
        lax.broadcasted_iota(jnp.int32, (KEEP, TOK), 1) == index_col, 1.0, 0.0
    ).astype(BF16)
    grad_f = nn(pick, cotangent[...])
    kept_f = nn(pick, residual[...])
    grad_sel = nn(table_half, grad_f.astype(BF16))
    pack_all(x_send.at[0], (slot_gate * grad_sel).astype(BF16).astype(F32))
    grad_sel = grad_sel.astype(BF16)
    pl.semaphore_wait(barrier, 2 * S - 1 + X * (E - 2))

    def remote(src, dst, ss, rs, seq, exp):
        return pltpu.make_async_remote_copy(
            src_ref=src,
            dst_ref=dst,
            send_sem=ss,
            recv_sem=rs,
            device_id={"seq": seq, "exp": exp},
            device_id_type=MESH,
        )

    def landed(view, sem):
        remote(view, view, send_ss.at[0], sem, me, 2 * yy + sib).wait_recv()

    def left(n, view):
        remote(view, view, send_ss.at[n], q_rs.at[0], me, 2 * yy + sib).wait_send()

    def left_all(n, ref):
        @pl.when(par == core)
        def _():
            left(n, ref.at[pl.ds(0, S - 1)])

        @pl.when(par != core)
        def _():
            left(n, ref)

    here = 2 * head + core

    col_x = [lax.rem(mx + o, X) for o in range(X)]
    row_z = [lax.rem(mz + o, Z) for o in range(Z)]

    def unless_own(maybe, do, *args):
        if maybe is None:
            do(*args)
        else:
            pl.when(maybe)(lambda: do(*args))

    def each_head(do):
        for q in range(Z // 2):
            for o, x in enumerate(col_x):
                h = x * (Z // 2) + lax.rem(x + q, Z // 2)
                for p in range(2):
                    away = None if o else (h != head) | (par != core) | (core != p)
                    unless_own(away, do, 2 * h + p, h, p)

    def each_source(do, x0=None):
        for o, x in enumerate(col_x) if x0 is None else ((0, x0),):
            for k, z in enumerate(row_z):
                away = None if o or k else (x != mx) | (par != core)
                unless_own(away, do, x * Z + z)

    def kv_copy(i, h, p):
        return remote(
            kv_send.at[i], kv.at[p, me], send_ss.at[0], kv_rs.at[me // QSRC], 2 * h + core, 2 * yy + p
        )

    def head_copy(n, send, recv, rs, i, h, p):
        return remote(send.at[i], recv.at[me], send_ss.at[n], rs, 2 * h + core, 2 * yy + p)

    def source_copy(n, send, recv, rs, d):
        return remote(send.at[d], recv.at[here], send_ss.at[n], rs, d, 2 * yy + par)

    def own_copy(src, dst, sem):
        @pl.when(par == core)
        def _():
            pltpu.make_async_copy(src, dst, sem).start()

    def each_expert(do):
        def step(k, t):
            e = lax.rem(ex + k, E)
            for hf in range(2):
                x = 2 * lax.rem(e, 2) + hf

                @pl.when((e != expert) | (hf != half) | (core != grp))
                def _():
                    do(e, x * Z + mz, 2 * (e // 2) + grp)

            return t

        lax.fori_loop(0, E, step, 0)

    def each_list(do):
        def step(k, t):
            b = lax.rem(ex + k, E)
            for r in range(2):
                x = 2 * core + r

                @pl.when((b != ex) | (x != mx))
                def _():
                    do(r * E + b, x * Z + mz, b)

            return t

        lax.fori_loop(0, E, step, 0)

    def out_start(n):
        slot = half * E + ex

        @pl.when(core == grp)
        def _():
            pltpu.make_async_copy(x_send.at[n, expert], x_recv.at[n, slot], x_rs.at[n]).start()

        each_expert(
            lambda e, seq, exp: remote(
                x_send.at[n, e], x_recv.at[n, slot], send_ss.at[6 + n], x_rs.at[n], seq, exp
            ).start()
        )

    def x_landed(n):
        landed(x_recv.at[n], x_rs.at[n])

    def part_cols(c):
        return pl.ds(c * Z * KEEP, Z * KEEP)

    def back_start(n, cols, ss, rs):
        slot = half * E + expert

        @pl.when(core == grp)
        def _():
            pltpu.make_async_copy(
                y_send.at[n, half * E + ex, :, cols], y_recv.at[n, slot, :, cols], rs
            ).start()

        each_list(
            lambda i, seq, exp: remote(
                y_send.at[n, i, :, cols], y_recv.at[n, slot, :, cols], ss, rs, seq, exp
            ).start()
        )

    def sixteen_left(n, ref, cols):
        @pl.when(core == grp)
        def _():
            left(n, ref.at[pl.ds(0, 2 * E - 1), :, cols])

        @pl.when(core != grp)
        def _():
            left(n, ref.at[:, :, cols])

    RING, CORE, INIT = 13, 14, 15
    part_all = pl.ds(0, FOLDS * Z * KEEP)

    def at_z(o):
        return lax.rem(mz + o + Z, Z)

    def arrival(w, oz, part):
        return wt_rs.at[w, oz % Z if part != 1 else Z]

    def piece(w, oz, part, group, seq, exp, sem):
        view = wt.at[2 * core + w, at_z(oz)]
        if part is not None:
            view = wt.at[2 * core + w, at_z(oz), part]
        return remote(view, view, send_ss.at[group], sem, seq, exp)

    def wait(w, oz, parts):
        for part in (0, 1) if parts else (None,):
            piece(w, oz, part, RING, me, 2 * yy + sib, arrival(w, oz, part)).wait_recv()

    both = (1, -1)

    def hop(w, sgn, k):
        if k < Z // 2:
            part = None if k < Z // 2 - 1 else (0 if sgn > 0 else 1)
            sem = arrival(w, -sgn * (k + 1), part)
            piece(w, -sgn * k, part, RING, mx * Z + at_z(sgn), ex, sem).start()

    def to_core(w, oz):
        piece(w, oz, None, CORE, me, 2 * yy + sib, core_rs.at[w]).start()

    def along_z(k):
        for w in (0, 1):
            if k == Z // 2:
                wait(w, k, True)
                to_core(w, k)
            else:
                for s in both:
                    wait(w, -s * k, False)
                    hop(w, s, k)
                    to_core(w, -s * k)

    def init_start():
        for hf in range(2):
            x = 2 * core + hf
            main = pl.ds(hf * WIDE, MAIN)
            parts = (
                (gate_w.at[:, :, main], 0, MAIN),
                (up_w.at[:, :, main], MAIN, MAIN),
                (mix.at[hf], 2 * MAIN, LANES),
                (down_w.at[:, :, main], GU, MAIN),
                (down_w.at[:, :, shared], GU + MAIN, LANES),
            )
            for src, at, n in parts:
                dst, sem = wt.at[mx, mz, :, :, pl.ds(at, n)], wt_rs.at[half, 0]

                @pl.when((x == mx) & (core == grp))
                def _():
                    pltpu.make_async_copy(src, dst, sem).start()

                @pl.when((x != mx) | (core != grp))
                def _():
                    seq = x * Z + mz
                    remote(src, dst, send_ss.at[INIT], sem, seq, 2 * yy + grp).start()

    init_start()
    own_copy(kv_send.at[here], kv.at[core, me], kv_rs.at[me // QSRC])
    own_copy(q_send.at[here], q_recv.at[me], q_rs.at[0])
    each_head(lambda *i: kv_copy(*i).start())
    each_head(lambda *i: head_copy(1, q_send, q_recv, q_rs.at[0], *i).start())

    for w in (0, 1):
        landed(wt.at[2 * core + w, mz], wt_rs.at[w, 0])
        for s in both:
            hop(w, s, 0)
        to_core(w, 0)
    out_start(0)

    along_z(1)
    def swap_copy(b):
        view = kv.at[core, pl.ds(b * QSRC, QSRC)]
        return remote(view, view, send_ss.at[16], swap_rs.at[0, b], me, 2 * yy + sib)

    for b in range(NB):
        landed(kv.at[core, pl.ds(b * QSRC, QSRC)], kv_rs.at[b])
        swap_copy(b).start()
    landed(q_recv, q_rs.at[0])
    for b in range(NB):
        landed(kv.at[sib, pl.ds(b * QSRC, QSRC)], swap_rs.at[0, b])

    def key_block(c):
        return kv[0, c * QSRC : (c + 1) * QSRC].reshape(KB, HS)

    def value_block(c):
        return kv[1, c * QSRC : (c + 1) * QSRC].reshape(KB, HS)

    def query_block(b):
        return q_recv[b * QSRC : (b + 1) * QSRC].reshape(QB, HS)

    for b in range(NB):
        k_f = key_block(b).astype(F32)
        bias[b * KB : (b + 1) * KB] = jnp.where(k_f > MARK / 2, NEG, 0.0)
        k_t[:, b * KB : (b + 1) * KB] = k_f.T.astype(BF16)
        v_t[:, b * KB : (b + 1) * KB] = value_block(b).astype(F32).T.astype(BF16)

    qcol = lax.broadcasted_iota(jnp.int32, (KB, QB), 1)
    qent = (qcol // PR) * KEEP + core * PR + lax.rem(qcol, PR)
    causal = lax.broadcasted_iota(jnp.int32, (KB, QB), 0) <= qent

    def forward_block(b):
        cols = slice(b * QB, (b + 1) * QB)
        q_blk = query_block(b)
        top = None
        for c in range(b + 1):
            rows = slice(c * KB, (c + 1) * KB)
            half = bias[rows, :]
            sc = nt(key_block(c), q_blk) * scale + jnp.concatenate([half] * (QB // HS), 1)
            if c == b:
                sc = jnp.where(causal, sc, NEG)
            prob[rows, cols] = sc
            m = jnp.max(sc, axis=0, keepdims=True)
            top = m if top is None else jnp.maximum(top, m)
        total = jnp.zeros((1, QB), F32)
        for c in range(b + 1):
            rows = slice(c * KB, (c + 1) * KB)
            e = jnp.exp(prob[rows, cols] - top)
            prob[rows, cols] = e
            total = total + jnp.sum(e, axis=0, keepdims=True)
        inv = 1.0 / total
        out = jnp.zeros((HS, QB), F32)
        for c in range(b + 1):
            rows = slice(c * KB, (c + 1) * KB)
            pr = prob[rows, cols] * inv
            prob[rows, cols] = pr
            out = out + nn(v_t[:, rows], pr.astype(BF16))
        att_t[:, cols] = out
        a_send[b * QSRC : (b + 1) * QSRC] = out.T.astype(BF16).reshape(QSRC, PR, HS)
        each_source(
            lambda d: source_copy(2, a_send, a_recv, a_rs.at[0], d).start(), b
        )

    for b in range(NB):
        forward_block(b)
    own_copy(a_send.at[me], a_recv.at[here], a_rs.at[0])
    along_z(2)
    landed(a_recv, a_rs.at[0])

    attended = jnp.concatenate(
        [jnp.concatenate([a_recv[2 * h + p] for h in range(HEADS)], 1) for p in range(2)], 0
    )
    h1 = jnp.where(live_col, kept_f + attended.astype(F32), 0.0)
    inv_rms = lax.rsqrt(jnp.mean(h1 * h1, axis=1, keepdims=True) + EPSILON)
    normed = (h1 * inv_rms).astype(BF16)
    pack_all(x_send.at[1], nn(table_half, normed))
    out_start(1)
    pre = [jnp.zeros((NR, GU), F32), jnp.zeros((NR, WIDE), F32)]

    def gate_up_of(ax):
        return wt[ax, :, :, :, 0:GU].reshape(KC, GU)

    def down_of(ax):
        return wt[ax, :, :, :, GU:].reshape(KC, WIDE)

    def expert_chunk(ax):
        cols = pl.ds(pl.multiple_of(ax * KC, KC), KC)
        pre[0] = pre[0] + nn(x_rows[1, :, cols], gate_up_of(ax))
        pre[1] = pre[1] + nn(x_rows[0, :, cols], down_of(ax))

    along_z(3)
    x_landed(0)
    x_landed(1)
    used = lax.rem(lax.broadcasted_iota(jnp.int32, (NR, KC), 0), SLOT) < CAP
    for n in (0, 1):
        last = jnp.zeros((NR, KC), F32)
        for g in range(FOLDS):
            chunk = x_recv[n, :, :, quarter(g)].reshape(NR, KC)
            last = last + nn(unfold[g], chunk)
            x_rows[n, :, quarter(g)] = jnp.where(used, chunk.astype(F32), 0.0).astype(BF16)
        x_rows[n, :, quarter(FOLDS)] = last.astype(BF16)
    along_z(Z // 2)
    for w in (0, 1):
        expert_chunk(2 * core + w)
    for w in (0, 1):
        landed(wt.at[2 * sib + w], core_rs.at[w])
        expert_chunk(2 * sib + w)
    ahead, mid_grad = pre
    turned_tile = pltpu.roll(ahead[:, 2 * MAIN :], LANES // 2, 1)
    gate_pre = jnp.concatenate([ahead[:, :MAIN], ahead[:, 2 * MAIN :]], 1)
    up_pre = jnp.concatenate([ahead[:, MAIN : 2 * MAIN], turned_tile], 1)
    sig = 1.0 / (1.0 + jnp.exp(-gate_pre))
    act = gate_pre * sig
    lane = lax.broadcasted_iota(jnp.int32, (NR, WIDE), 1)
    own = (lane < MAIN) | ((lane - MAIN) // (LANES // 2) == half)
    mid_grad = jnp.where(own, mid_grad, 0.0)
    gate_grad = mid_grad * up_pre * sig * (1.0 + gate_pre * (1.0 - sig))
    up_grad = mid_grad * act
    turned_tile = pltpu.roll(up_grad[:, MAIN:], LANES // 2, 1)
    behind = jnp.concatenate(
        [gate_grad[:, :MAIN], up_grad[:, :MAIN], gate_grad[:, MAIN:] + turned_tile], 1
    ).astype(BF16)
    mid = jnp.where(own, act * up_pre, 0.0).astype(BF16)
    def back_of(c):
        return nt(gate_up_of(c), behind).T

    last = back_of(FOLDS).astype(BF16)
    for g in range(FOLDS):
        pack(y_send.at[0], g, back_of(g), last)
        back_start(0, part_cols(g), send_ss.at[9 + g], rows_rs.at[g])
    last = nt(down_of(FOLDS), mid).T.astype(BF16)
    for g in range(FOLDS):
        pack(y_send.at[1], g, nt(down_of(g), mid).T, last)
    table_t = jnp.concatenate([table_t, table_t], 1)
    parts, last = [], jnp.zeros((KEEP, KC), F32)
    for g in range(FOLDS):
        landed(y_recv.at[0, :, :, part_cols(g)], rows_rs.at[g])
        chunk = y_recv[0, :, :, quarter(g)].reshape(NR, KC)
        parts.append(nn(table_t, chunk))
        last = last + nn(nt(table_t, fold[g]).astype(BF16), chunk)
    parts.append(last)
    normed_grad = jnp.concatenate(parts, 1)
    cubed = inv_rms * inv_rms * inv_rms
    h1_grad = (
        grad_f
        + inv_rms * normed_grad
        - h1 * cubed * jnp.mean(normed_grad * h1, axis=1, keepdims=True)
    )
    h1_grad = jnp.where(live_col, h1_grad, 0.0).astype(BF16)
    for h in range(HEADS):
        for p in range(2):
            g_send[2 * h + p] = h1_grad[p * PR : (p + 1) * PR, h * HS : (h + 1) * HS]
    own_copy(g_send.at[here], g_recv.at[me], g_rs.at[me // QSRC])
    each_head(lambda *i: head_copy(3, g_send, g_recv, g_rs.at[me // QSRC], *i).start())

    token = lax.broadcasted_iota(jnp.int32, (TOK, KEEP), 0)
    put = jnp.where(
        (token == index_row) & (lax.broadcasted_iota(jnp.int32, (TOK, KEEP), 1) < count),
        1.0,
        0.0,
    )
    replaced = jnp.sum(put, axis=1, keepdims=True) > 0.5
    put = put.astype(BF16)
    cotangent[...] = jnp.where(replaced, nn(put, h1_grad), cotangent[...].astype(F32)).astype(
        BF16
    )
    input_grad_out = load(0, cotangent, input_grad_h)
    input_grad_out.start()

    def give_copy(c):
        rows = pl.ds(c * KB, KB)
        return remote(
            acc.at[sib, rows],
            other.at[rows],
            send_ss.at[17],
            swap_rs.at[1, c],
            me,
            2 * yy + sib,
        )

    def finish_block(c):
        rows = slice(c * KB, (c + 1) * KB)
        landed(other.at[pl.ds(c * KB, KB)], swap_rs.at[1, c])
        whole = acc[core, rows] + other[rows]
        b_send[c * QSRC : (c + 1) * QSRC] = whole.astype(BF16).reshape(QSRC, KEEP, HS)
        each_source(
            lambda d: source_copy(4, b_send, b_recv, b_rs.at[0], d).start(), c
        )

    dout = [None] * NB
    delta = [None] * NB
    dq_t = [jnp.zeros((HS, QB), F32)] * NB
    for c in reversed(range(NB)):
        rows = slice(c * KB, (c + 1) * KB)
        block = pl.ds(c * QSRC, QSRC)
        landed(g_recv.at[block], g_rs.at[c])
        if c == 0:
            back_start(1, part_all, send_ss.at[8], y_rs.at[0])
        dout[c] = g_recv[c * QSRC : (c + 1) * QSRC].reshape(QB, HS)
        turn = dout[c].astype(F32).T * att_t[:, c * QB : (c + 1) * QB]
        delta[c] = jnp.sum(turn, axis=0, keepdims=True)
        dk = jnp.zeros((KB, HS), F32)
        dv = jnp.zeros((KB, HS), F32)
        for b in range(c, NB):
            pr = prob[rows, b * QB : (b + 1) * QB]
            ds = (pr * (nt(value_block(c), dout[b]) - delta[b]) * scale).astype(BF16)
            dq_t[b] = dq_t[b] + nn(k_t[:, rows], ds)
            dk = dk + nn(ds, query_block(b))
            dv = dv + nn(pr.astype(BF16), dout[b])
        acc[0, rows] = dk
        acc[1, rows] = dv
        give_copy(c).start()
        if c < NB - 1:
            finish_block(c + 1)
    for b in range(NB):
        dq_send[b * QSRC : (b + 1) * QSRC] = dq_t[b].T.astype(BF16).reshape(QSRC, PR, HS)
    each_source(lambda d: source_copy(5, dq_send, dq_recv, b_rs.at[1], d).start())
    finish_block(0)
    own_copy(dq_send.at[me], dq_recv.at[here], b_rs.at[1])
    own_copy(b_send.at[me], b_recv.at[here], b_rs.at[0])

    landed(y_recv.at[1], y_rs.at[0])
    parts, last = [], jnp.zeros((KEEP, KC), F32)
    made_last = jnp.zeros((NR, KC), F32)
    per_slot = jnp.zeros((NS, 1), F32)

    def against(rows, g):
        both_halves = (rows[:NS] + rows[NS:]) * grad_sel[:, quarter(g)].astype(F32)
        return jnp.sum(both_halves, axis=1, keepdims=True)

    for g in range(FOLDS):
        chunk = y_recv[1, :, :, quarter(g)].reshape(NR, KC)
        there = jnp.zeros((KEEP, KC), F32)
        for w in (w_high, w_low):
            w = jnp.concatenate([w, w], 1)
            there = there + nn(w, chunk)
            last = last + nn(nt(w, fold[g]).astype(BF16), chunk)
        parts.append(there)
        made_last = made_last + nn(unfold[g], chunk)
        per_slot = per_slot + against(chunk.astype(F32), g)
    per_slot = per_slot + against(made_last, FOLDS)
    mixture = jnp.concatenate(parts + [last], 1)
    new_rows = (h1 + mixture).astype(BF16)
    residual[...] = jnp.where(replaced, nn(put, new_rows), residual[...].astype(F32)).astype(BF16)
    spread = table * per_slot
    for k in range(expert_ids.shape[0]):
        hit = expert_ids[k] == slot_exp
        gate_grads[k] = jnp.sum(jnp.where(hit, spread, 0.0), axis=0, keepdims=True)
    output_out = load(1, residual, output_h)
    output_out.start()
    left_all(0, kv_send)
    left_all(1, q_send)
    left_all(2, a_send)
    left_all(3, g_send)
    for n in (0, 1):
        sixteen_left(6 + n, x_recv.at[n], part_all)
    sixteen_left(8, y_send.at[1], part_all)
    for c in range(FOLDS):
        sixteen_left(9 + c, y_send.at[0], part_cols(c))
    left(RING, wt.at[pl.ds(0, 2), pl.ds(0, Z - 1)])
    left(CORE, wt.at[pl.ds(0, 2)])
    left(16, kv.at[core])
    left(17, acc.at[sib])

    @pl.when(core == grp)
    def _():
        left(INIT, wt.at[0, 0])

    @pl.when(core != grp)
    def _():
        left(INIT, wt.at[0, pl.ds(0, 2)])

    landed(b_recv, b_rs.at[0])
    landed(dq_recv, b_rs.at[1])
    left_all(4, b_send)
    left_all(5, dq_send)
    for copy in (input_grad_out, output_out):
        copy.wait()


def finish(a, b, c, e, d, out_a, out_b, out_c, out_d, sa, sb, sc, se, sd, sp, sem):
    heads, _, width = c.shape
    rows = e.shape[1]
    ins, outs = [], []
    pairs = ((c, sc, None), (e, se, None), (a, sa, out_a.at[0]), (b, sb, out_b.at[0]), (d, sd, out_d))
    for i, (src, stage, dst) in enumerate(pairs):
        ins.append(pltpu.make_async_copy(src, stage, sem.at[0, i]))
        if dst is not None:
            outs.append(pltpu.make_async_copy(stage, dst, sem.at[1, i]))
    for copy in ins:
        copy.start()
    for copy in ins[:2]:
        copy.wait()
    for i in range(heads):
        c0, p = i // 2 * width, i % 2
        o = (1 + p) * (heads // 2) * width + c0
        sp[p * rows : (p + 1) * rows, c0 : c0 + width] = se[i]
        sp[:, o : o + width] = sc[i]
    outs.append(pltpu.make_async_copy(sp, out_c.at[0], sem.at[1, 0]))
    outs[-1].start()
    for copy, after in zip(ins[2:], outs):
        copy.wait()
        after.start()
    for copy in outs:
        copy.wait()


def body(
    residual,
    kept_index,
    kept_count,
    projected,
    expert_ids,
    gate_values,
    gate_weight,
    up_weight,
    down_weight,
    cotangent,
):
    S = lax.axis_size("seq")
    E = lax.axis_size("exp")
    _, TOK, D = residual.shape
    KEEP = kept_index.shape[1]
    FF = gate_weight.shape[2]
    TOPK = expert_ids.shape[2]
    Z = S // X
    HEADS = D // HS
    PR = KEEP // 2
    NB = S // QSRC
    vm = pl.BlockSpec(memory_space=pltpu.VMEM)
    hbm = pl.BlockSpec(memory_space=pl.ANY)
    dma = pltpu.SemaphoreType.DMA
    out = pl.pallas_call(
        functools.partial(kernel, S, E),
        out_shape=[
            jax.ShapeDtypeStruct((TOK, D), BF16),
            jax.ShapeDtypeStruct((TOK, D), BF16),
            jax.ShapeDtypeStruct((S, KEEP, HS), BF16),
            jax.ShapeDtypeStruct((S, PR, HS), BF16),
            jax.ShapeDtypeStruct((TOPK, 1, KEEP), F32),
        ],
        in_specs=[hbm] * 10,
        out_specs=[hbm, hbm, hbm, hbm, vm],
        scratch_shapes=[
            pltpu.VMEM((TOK, D), BF16),
            pltpu.VMEM((TOK, D), BF16),
            pltpu.VMEM((KEEP, 3 * D), BF16),
            pltpu.VMEM((1, KEEP), jnp.int32),
            pltpu.VMEM((1, 1), jnp.int32),
            pltpu.VMEM((TOPK, 1, KEEP), jnp.int32),
            pltpu.VMEM((TOPK, 1, KEEP), F32),
            dma((10,)),
            pltpu.VMEM((S, KEEP, HS), BF16),
            pltpu.VMEM((2, S, KEEP, HS), BF16),
            pltpu.VMEM((S, PR, HS), BF16),
            pltpu.VMEM((S, PR, HS), BF16),
            pltpu.VMEM((S, PR, HS), BF16),
            pltpu.VMEM((S, PR, HS), BF16),
            pltpu.VMEM((S, PR, HS), BF16),
            pltpu.VMEM((S, PR, HS), BF16),
            pltpu.VMEM((S, KEEP, HS), BF16),
            pltpu.VMEM((S, PR, HS), BF16),
            pltpu.VMEM((2, E, SLOT, D * CAP // SLOT), BF16),
            pltpu.VMEM((2, 2 * E, SLOT, D * CAP // SLOT), BF16),
            pltpu.VMEM((2, 2 * E, SLOT, D * CAP // SLOT), BF16),
            pltpu.VMEM((2, 2 * E, SLOT, D * CAP // SLOT), BF16),
            pltpu.VMEM((2, 2 * E * SLOT, D), BF16),
            pltpu.VMEM((2, 2, KEEP // 2, LANES), BF16),
            pltpu.VMEM((2, 2, KEEP // 2, LANES), BF16),
            pltpu.VMEM((X, Z, 2, KEEP // 2, FF // LANES // 2 * LANES * 3 + 2 * LANES), BF16),
            pltpu.VMEM((S * KEEP, HS), F32),
            pltpu.VMEM((HS, S * KEEP), BF16),
            pltpu.VMEM((HS, S * KEEP), BF16),
            pltpu.VMEM((S * KEEP, S * PR), F32),
            pltpu.VMEM((HS, S * PR), F32),
            pltpu.VMEM((2, S * KEEP, HS), F32),
            pltpu.VMEM((S * KEEP, HS), F32),
        ]
        + [
            dma((18,)),
            dma((NB,)),
            dma((1,)),
            dma((1,)),
            dma((NB,)),
            dma((2,)),
            dma((2,)),
            dma((1,)),
            dma((X,)),
            dma((2, NB)),
            dma((2, Z + 1)),
            dma((2,)),
        ],
        compiler_params=pltpu.CompilerParams(
            collective_id=0, has_side_effects=True, vmem_limit_bytes=60 * 1024 * 1024
        ),
    )(
        residual[0],
        kept_index,
        kept_count,
        projected[0],
        jnp.transpose(expert_ids, (2, 0, 1)),
        jnp.transpose(gate_values, (2, 0, 1)),
        gate_weight[0].reshape(2, KEEP // 2, FF),
        up_weight[0].reshape(2, KEEP // 2, FF),
        down_weight[0].T.reshape(2, KEEP // 2, FF),
        cotangent[0],
    )
    out = pl.pallas_call(
        finish,
        out_shape=[
            jax.ShapeDtypeStruct((1, TOK, D), BF16),
            jax.ShapeDtypeStruct((1, TOK, D), BF16),
            jax.ShapeDtypeStruct((1, KEEP, 3 * D), BF16),
            jax.ShapeDtypeStruct((TOPK, 1, KEEP), F32),
        ],
        in_specs=[hbm] * 5,
        out_specs=[hbm] * 4,
        scratch_shapes=[
            pltpu.VMEM((TOK, D), BF16),
            pltpu.VMEM((TOK, D), BF16),
            pltpu.VMEM((S, KEEP, HS), BF16),
            pltpu.VMEM((S, PR, HS), BF16),
            pltpu.VMEM((TOPK, 1, KEEP), F32),
            pltpu.VMEM((KEEP, 3 * D), BF16),
            dma((2, 5)),
        ],
        compiler_params=pltpu.CompilerParams(vmem_limit_bytes=60 * 1024 * 1024),
    )(*out)
    return (out[0], out[1], out[2], jnp.transpose(out[3], (1, 2, 0)))


def solution(mesh):
    row = P("exp", "seq", None)
    in_specs = (row, P("exp", "seq"), P("exp", "seq")) + (row,) * 5 + (P("exp", None, "seq"), row)
    return jax.shard_map(
        body, mesh=mesh, in_specs=in_specs, out_specs=(row,) * 4, check_vma=False
    )
```
